128 devices in a mesh: store: 8 (over z, core), scorer: 16 (over y, x).
Axes of the slice: x: 4, y: 4, z: 4, core: 2. Of those that a mesh axis runs over, the one named last changes fastest.
Arguments:
- store_rows: bfloat16 [262144, 256], P(('store', 'scorer')), may hold values from -11 to 11
- cluster_logsize: bfloat16 [262144], P(('store', 'scorer')), may hold values from 0 to 318
- cluster_home: int32 [262144], replicated, may hold values from 0 to 262143, as said below
- cluster_ids: int32 [1024, 512], P(('store', 'scorer')), may hold values from 0 to 262143, as said below
- valid_count: int32 [1024], P(('store', 'scorer')), may hold values from 64 to 512
- candidates: bfloat16 [1024, 512, 256], P(('store', 'scorer')), may hold values from -11 to 11
- cand_count: int32 [1024], P(('store', 'scorer')), may hold values from 0 to 512, as said below
- candidate_row: int32 [1024, 512], P(('store', 'scorer')), may hold values from 0 to 32767, as said below
- query_proj: bfloat16 [256, 256], replicated, may hold values from -0.375 to 0.375
- key_proj: bfloat16 [256, 256], replicated, may hold values from -0.375 to 0.375
- value_proj: bfloat16 [256, 256], replicated, may hold values from -0.375 to 0.375
- out_proj: bfloat16 [256, 256], replicated, may hold values from -0.375 to 0.375
- mlp_first: bfloat16 [512, 512], replicated, may hold values from -0.25 to 0.25
- bias_first: float32 [512], replicated, may hold values from -3 to 3
- mlp_second: bfloat16 [512, 256], replicated, may hold values from -0.25 to 0.25
- bias_second: float32 [256], replicated, may hold values from -3 to 3
- score_proj: bfloat16 [256], replicated, may hold values from -0.375 to 0.375
Outputs:
- span_scores: float32 [262144], P(('store', 'scorer'))
The draws below stay inside these ranges and needn't reach their ends.
Inputs may be any that keep to these rules, and one draw needn't show every extreme that they name: A permutation: cluster c is row cluster_home[c] of store_rows. `cluster_ids`: of the 4096 entries of one device's requests, exactly 32 name clusters whose rows lie on each device's rows of store_rows, valid slots or not. `cand_count`: the counts of the 16 devices of one store group sum to 32768; in every group one device has all its requests full. `candidate_row`: the valid candidates of a store group fill each of its 32768 rows once; rows c * 2048 to (c + 1) * 2048 - 1 form span c, held by the group's device of scorer index c. One device has at most 256 valid candidates in one span, and in every group one device has exactly 256 in each span. Padded slots hold 0.
All inputs are finite; a program needn't handle non-finite values.
Results may differ from the reference program's by a relative error of at most 0.0065.
Values may be sent and summed in bfloat16 or wider, within the bound.
A program may use at most 128 MiB of HBM per device.

```python
import math
import jax
import jax.numpy as jnp
from jax import lax

W = 256
HEADS = 4
K = 512
M1 = 512
M2 = 256
REQ_DEV = 8
CAND_CAP = 512
ROWS_DEV = 2048
REQS = 1024
CLUSTERS = 262144
SPAN_LIVE = 2048
SCORE_ROWS = 262144
N_SCORER = 16


def placing(key):
    return jax.random.permutation(jax.random.fold_in(key, 101), CLUSTERS).astype(jnp.int32)


def shared_direction(key):
    return jnp.clip(jax.random.normal(jax.random.fold_in(key, 404), (W,), jnp.float32), -3.0, 3.0)


def listed_clusters(key):
    shared = placing(key)
    key = jax.random.fold_in(key, 303)
    device_count = REQS // REQ_DEV
    slot_total = REQ_DEV * K
    subkeys = jax.random.split(key, device_count + 1)
    shuffles = jax.vmap(lambda subkey: jax.random.permutation(subkey, slot_total))(subkeys[:device_count])
    home_dev = (shuffles % device_count).astype(jnp.int32)
    local_row = jax.random.randint(subkeys[device_count], (device_count, slot_total), 0, ROWS_DEV, dtype=jnp.int32)
    cluster_at = jnp.zeros((CLUSTERS,), jnp.int32).at[shared].set(jnp.arange(CLUSTERS, dtype=jnp.int32))
    return cluster_at[home_dev * ROWS_DEV + local_row].reshape(REQS, K)


def candidate_plan(key):
    key = jax.random.fold_in(key, 202)
    subkeys = jax.random.split(key, 5)
    groups = REQS // (REQ_DEV * N_SCORER)
    halves = N_SCORER // 2
    own_max = REQ_DEV * CAND_CAP
    span_live = own_max // 2
    amounts = jax.random.randint(subkeys[0], (groups, halves), 0, own_max + 1, dtype=jnp.int32)
    forced = jax.random.randint(subkeys[1], (groups, 1), 0, halves, dtype=jnp.int32)
    amounts = jnp.where(jnp.arange(halves, dtype=jnp.int32)[None, :] == forced, own_max, amounts)
    totals = jnp.concatenate([amounts, own_max - amounts], axis=1)
    owner_order = jax.vmap(lambda subkey: jax.random.permutation(subkey, N_SCORER))(jax.random.split(subkeys[2], groups))
    totals = jnp.take_along_axis(totals, owner_order.astype(jnp.int32), axis=1)
    filled = jnp.clip(totals[:, :, None] - CAND_CAP * jnp.arange(REQ_DEV, dtype=jnp.int32)[None, None, :], 0, CAND_CAP)
    request_order = jax.vmap(lambda subkey: jax.random.permutation(subkey, REQ_DEV))(jax.random.split(subkeys[3], groups * N_SCORER))
    request_order = request_order.reshape(groups, N_SCORER, REQ_DEV).astype(jnp.int32)
    counts = jnp.take_along_axis(filled, request_order, axis=2).astype(jnp.int32)
    flat = counts.reshape(groups, N_SCORER * REQ_DEV)
    offsets = jnp.cumsum(flat, axis=1) - flat
    slot_index = jnp.arange(CAND_CAP, dtype=jnp.int32)
    serial = offsets[:, :, None] + slot_index[None, None, :]
    valid_mask = slot_index[None, None, :] < flat[:, :, None]
    span_index = serial % N_SCORER
    within = jnp.where(valid_mask, serial // N_SCORER, 0)
    shuffles = jax.vmap(lambda subkey: jax.random.permutation(subkey, span_live))(jax.random.split(subkeys[4], groups * N_SCORER))
    shuffles = shuffles.reshape(groups, N_SCORER * span_live).astype(jnp.int32)
    lookup_at = (span_index * span_live + within).reshape(groups, -1)
    picked = jnp.take_along_axis(shuffles, lookup_at, axis=1).reshape(serial.shape)
    rows_out = jnp.where(valid_mask, span_index * span_live + picked, 0).astype(jnp.int32)
    return (counts.reshape(REQS), rows_out.reshape(REQS, CAND_CAP))


def draw_store_rows(key, part):
    direction = shared_direction(key)
    key = jax.random.fold_in(key, 7)
    sign_key, noise_key = jax.random.split(key)
    signs = jnp.where(jax.random.bernoulli(sign_key, 0.5, (CLUSTERS, 1)), 1.0, -1.0).astype(jnp.float32)
    noise = jnp.clip(jax.random.normal(noise_key, (CLUSTERS, W), jnp.float32), -6.0, 6.0)
    amplitude = 1.5
    return jnp.clip(noise + amplitude * signs * direction[None, :], -11.0, 11.0).astype(jnp.bfloat16)


def draw_candidates(key, part):
    direction = shared_direction(key)
    key = jax.random.fold_in(key, 8)
    sign_key, noise_key = jax.random.split(key)
    signs = jnp.where(jax.random.bernoulli(sign_key, 0.5, (REQS, CAND_CAP, 1)), 1.0, -1.0).astype(jnp.float32)
    noise = jnp.clip(jax.random.normal(noise_key, (REQS, CAND_CAP, W), jnp.float32), -6.0, 6.0)
    amplitude = 1.5
    return jnp.clip(noise + amplitude * signs * direction[None, None, :], -11.0, 11.0).astype(jnp.bfloat16)


def draw_cluster_logsize(key, part):
    key = jax.random.fold_in(key, 6)
    return jax.random.uniform(key, (CLUSTERS,), jnp.float32, 1.6, 2.8).astype(jnp.bfloat16)


def draw_cluster_home(key, part):
    shared = placing(key)
    return shared


def draw_cluster_ids(key, part):
    listed = listed_clusters(key)
    return listed


def draw_valid_count(key, part):
    key = jax.random.fold_in(key, 3)
    first_key, second_key = jax.random.split(key)
    counts = jax.random.randint(first_key, (REQS,), K // 8, K + 1, dtype=jnp.int32)
    chosen = jax.random.randint(second_key, (), 0, REQS, dtype=jnp.int32)
    return jnp.where(jnp.arange(REQS, dtype=jnp.int32) == chosen, K, counts).astype(jnp.int32)


def draw_cand_count(key, part):
    counts, rows_out = candidate_plan(key)
    return counts


def draw_candidate_row(key, part):
    counts, rows_out = candidate_plan(key)
    return rows_out


def gaussian(stream_key, shape, scale, most, kind=jnp.bfloat16):
    result = scale * jax.random.normal(stream_key, shape, jnp.float32)
    return jnp.clip(result, min=-most, max=most).astype(kind)


def setup_inputs(seed: int = 0) -> dict:
    arg_keys = jax.random.split(jax.random.key(seed), 18)
    store_rows = draw_store_rows(jax.random.fold_in(arg_keys[17], 71), 0)
    cluster_logsize = draw_cluster_logsize(jax.random.fold_in(arg_keys[17], 71), 0)
    cluster_home = draw_cluster_home(jax.random.fold_in(arg_keys[17], 71), 0)
    cluster_ids = draw_cluster_ids(jax.random.fold_in(arg_keys[17], 71), 0)
    valid_count = draw_valid_count(jax.random.fold_in(arg_keys[17], 71), 0)
    candidates = draw_candidates(jax.random.fold_in(arg_keys[17], 71), 0)
    cand_count = draw_cand_count(jax.random.fold_in(arg_keys[17], 71), 0)
    candidate_row = draw_candidate_row(jax.random.fold_in(arg_keys[17], 71), 0)
    query_proj = gaussian(arg_keys[8], (W, W), W ** -0.5, 0.375)
    key_proj = gaussian(arg_keys[9], (W, W), W ** -0.5, 0.375)
    value_proj = gaussian(arg_keys[10], (W, W), W ** -0.5, 0.375)
    out_proj = gaussian(arg_keys[11], (W, W), W ** -0.5, 0.375)
    mlp_first = gaussian(arg_keys[12], (2 * W, M1), (2 * W) ** -0.5, 0.25)
    bias_first = gaussian(arg_keys[13], (M1,), 0.5, 3.0, jnp.float32)
    mlp_second = gaussian(arg_keys[14], (M1, M2), M1 ** -0.5, 0.25)
    bias_second = gaussian(arg_keys[15], (M2,), 0.5, 3.0, jnp.float32)
    score_proj = gaussian(arg_keys[16], (M2,), M2 ** -0.5, 0.375)
    return dict(store_rows=store_rows, cluster_logsize=cluster_logsize, cluster_home=cluster_home, cluster_ids=cluster_ids, valid_count=valid_count, candidates=candidates, cand_count=cand_count, candidate_row=candidate_row, query_proj=query_proj, key_proj=key_proj, value_proj=value_proj, out_proj=out_proj, mlp_first=mlp_first, bias_first=bias_first, mlp_second=mlp_second, bias_second=bias_second, score_proj=score_proj)


def attend(cand_block, key_rows, key_sizes, key_count, query_proj, key_proj, value_proj, out_proj):
    batch_size, cand_slots, row_width = cand_block.shape
    cluster_slots = key_rows.shape[1]
    head_size = row_width // HEADS
    queries = jnp.dot(cand_block.reshape(-1, row_width), query_proj, preferred_element_type=jnp.float32).astype(jnp.bfloat16)
    keys_all = jnp.dot(key_rows.reshape(-1, row_width), key_proj, preferred_element_type=jnp.float32).astype(jnp.bfloat16)
    values_all = jnp.dot(key_rows.reshape(-1, row_width), value_proj, preferred_element_type=jnp.float32).astype(jnp.bfloat16)
    queries = queries.reshape(batch_size, cand_slots, HEADS, head_size).astype(jnp.float32)
    keys_all = keys_all.reshape(batch_size, cluster_slots, HEADS, head_size).astype(jnp.float32)
    values_all = values_all.reshape(batch_size, cluster_slots, HEADS, head_size).astype(jnp.float32)
    logits = jnp.einsum('bchd,bkhd->bhck', queries, keys_all)
    logits = logits * (1.0 / math.sqrt(head_size)) + key_sizes.astype(jnp.float32)[:, None, None, :]
    usable = jnp.arange(cluster_slots, dtype=jnp.int32)[None, :] < key_count[:, None]
    logits = jnp.where(usable[:, None, None, :], logits, -1e+30)
    row_max = lax.optimization_barrier(jnp.max(logits, axis=-1, keepdims=True))
    weights = jnp.exp(logits - row_max)
    probs = (weights / lax.optimization_barrier(jnp.sum(weights, axis=-1, keepdims=True))).astype(jnp.bfloat16)
    context = jnp.einsum('bhck,bkhd->bchd', probs.astype(jnp.float32), values_all).astype(jnp.bfloat16)
    context = context.reshape(batch_size * cand_slots, row_width)
    attended = jnp.dot(context, out_proj, preferred_element_type=jnp.float32).astype(jnp.bfloat16)
    return attended.reshape(batch_size, cand_slots, row_width)

def score_rows(features, mlp_first, bias_first, mlp_second, bias_second, score_proj):
    hidden_one = jnp.maximum(jnp.dot(features, mlp_first, preferred_element_type=jnp.float32) + bias_first, 0.0).astype(jnp.bfloat16)
    hidden_two = jnp.maximum(jnp.dot(hidden_one, mlp_second, preferred_element_type=jnp.float32) + bias_second, 0.0).astype(jnp.bfloat16)
    return jnp.dot(hidden_two, score_proj, preferred_element_type=jnp.float32)

def reference(store_rows, cluster_logsize, cluster_home, cluster_ids, valid_count, candidates, cand_count, candidate_row, query_proj, key_proj, value_proj, out_proj, mlp_first, bias_first, mlp_second, bias_second, score_proj):
    block_total = REQS // REQ_DEV

    def one_block(block_index):
        block_start = block_index * REQ_DEV
        block_ids = lax.dynamic_slice_in_dim(cluster_ids, block_start, REQ_DEV, 0)
        global_row = cluster_home[block_ids]
        block_rows = store_rows[global_row]
        block_sizes = cluster_logsize[global_row]
        key_count = lax.dynamic_slice_in_dim(valid_count, block_start, REQ_DEV, 0)
        cand_block = lax.dynamic_slice_in_dim(candidates, block_start, REQ_DEV, 0)
        attended = attend(cand_block, block_rows, block_sizes, key_count, query_proj, key_proj, value_proj, out_proj)
        features = jnp.concatenate([cand_block, attended], axis=-1).reshape(REQ_DEV * CAND_CAP, 2 * W)
        return score_rows(features, mlp_first, bias_first, mlp_second, bias_second, score_proj).reshape(REQ_DEV, CAND_CAP)
    cand_score = lax.map(one_block, jnp.arange(block_total, dtype=jnp.int32)).reshape(REQS, CAND_CAP)
    group_of = jnp.arange(REQS, dtype=jnp.int32) // (REQ_DEV * N_SCORER)
    valid_mask = jnp.arange(CAND_CAP, dtype=jnp.int32)[None, :] < cand_count[:, None]
    out_index = jnp.where(valid_mask, group_of[:, None] * (N_SCORER * SPAN_LIVE) + candidate_row, SCORE_ROWS).astype(jnp.int32)
    span_scores = jnp.zeros((SCORE_ROWS,), jnp.float32).at[out_index.reshape(-1)].set(cand_score.reshape(-1), mode='drop')
    return span_scores
```

```python
import functools

import jax
import jax.numpy as jnp
from jax import lax
from jax.experimental import pallas as pl
from jax.experimental.pallas import tpu as pltpu
from jax.sharding import PartitionSpec as P

HEADS = 4
AXES = ("store", "scorer")
LANES = 128
NT = (((1,), (1,)), ((), ()))
TN = (((0,), (0,)), ((), ()))
BF = jnp.bfloat16
F32 = jnp.float32
VMEM_LIMIT = 48 * 1024 * 1024


def lane_pick(rows, lane_index):
    return jnp.take_along_axis(rows, lane_index, axis=1)


def column_of(row):
    return jnp.broadcast_to(row, (LANES, LANES)).T


def route_kernel(rows_dev, per_pair, ids_smem, ids_ref, table_ref, ask_ref, pos_ref, home_ref, rows_scr):
    tiles = ids_ref.shape[0]
    shift_rows = rows_dev.bit_length() - 1

    def fetch(t, carry):
        for u in range(LANES):
            c = ids_smem[t, u]
            rows_scr[pl.ds(t * LANES + u, 1), :] = table_ref[
                pl.ds(lax.shift_right_logical(c, 7), 1), :
            ]
        return carry

    lax.fori_loop(0, tiles, fetch, 0)
    lane = lax.broadcasted_iota(jnp.int32, (LANES, LANES), 1)
    sub = lax.broadcasted_iota(jnp.int32, (LANES, LANES), 0)
    lower = jnp.where(sub >= lane, 1.0, 0.0).astype(BF)
    ones = jnp.ones((LANES, LANES), BF)
    base = jnp.zeros((1, LANES), F32)
    acc = jnp.zeros((LANES, 2 * LANES), F32)
    for t in range(tiles):
        ids_col = column_of(ids_ref[t : t + 1, :])
        home = lane_pick(rows_scr[t * LANES : (t + 1) * LANES, :], ids_col & (LANES - 1))
        dest = lax.shift_right_logical(home, shift_rows)
        hot = dest == lane
        hot_b = jnp.where(hot, 1.0, 0.0).astype(BF)
        incl = jnp.dot(lower, hot_b, preferred_element_type=F32)
        picked = jnp.where(hot, incl + (base - 1.0), 0.0).astype(BF)
        rank = jnp.dot(picked, ones, preferred_element_type=F32).astype(jnp.int32)
        base = base + incl[LANES - 1 : LANES, :]
        low = (home & 255).astype(F32)
        high = (lax.shift_right_logical(home, 8) & ((rows_dev >> 8) - 1)).astype(F32)
        at = rank == lane
        parts = jnp.concatenate(
            [jnp.where(at, low, 0.0), jnp.where(at, high, 0.0)], axis=1
        ).astype(BF)
        acc = acc + lax.dot_general(hot_b, parts, TN, preferred_element_type=F32)
        diag = sub == lane
        pos = (dest * per_pair + rank).astype(F32)
        pos_ref[t : t + 1, :] = jnp.sum(
            jnp.where(diag, pos, 0.0), axis=0, keepdims=True
        ).astype(jnp.int32)
        home_ref[t : t + 1, :] = jnp.sum(
            jnp.where(diag, home.astype(F32), 0.0), axis=0, keepdims=True
        ).astype(jnp.int32)
    ask_ref[...] = (acc[:, :LANES] + 256.0 * acc[:, LANES:]).astype(jnp.int32)


def route(ids, table, rows_dev, per_pair):
    tiles = ids.shape[0]
    vm = pl.BlockSpec(memory_space=pltpu.VMEM)
    return pl.pallas_call(
        functools.partial(route_kernel, rows_dev, per_pair),
        out_shape=(
            jax.ShapeDtypeStruct((LANES, LANES), jnp.int32),
            jax.ShapeDtypeStruct((tiles, LANES), jnp.int32),
            jax.ShapeDtypeStruct((tiles, LANES), jnp.int32),
        ),
        in_specs=[pl.BlockSpec(memory_space=pltpu.SMEM), vm, vm],
        out_specs=(vm, vm, vm),
        scratch_shapes=[pltpu.VMEM((tiles * LANES, LANES), jnp.int32)],
        compiler_params=pltpu.CompilerParams(vmem_limit_bytes=VMEM_LIMIT),
        name="route",
    )(ids, ids, table)


def serve_kernel(per_pair, ask_smem, store_ref, out_ref, store_scr, stage):
    store_scr[...] = store_ref[...].astype(F32)
    pairs = ask_smem.shape[0]
    group = 4

    def some(g, carry):
        for q in range(group):
            for j in range(per_pair):
                row = ask_smem[g * group + q, j]
                stage[pl.ds(q * per_pair + j, 1), :] = store_scr[pl.ds(row, 1), :]
        out_ref[pl.ds(g * (group * per_pair), group * per_pair), :] = stage[...].astype(BF)
        return carry

    lax.fori_loop(0, pairs // group, some, 0)


def serve(asked, store_rows, per_pair):
    pairs = asked.shape[0]
    width = store_rows.shape[1]
    vm = pl.BlockSpec(memory_space=pltpu.VMEM)
    return pl.pallas_call(
        functools.partial(serve_kernel, per_pair),
        out_shape=jax.ShapeDtypeStruct((pairs * per_pair, width), BF),
        in_specs=[pl.BlockSpec(memory_space=pltpu.SMEM), vm],
        out_specs=vm,
        scratch_shapes=[
            pltpu.VMEM(store_rows.shape, F32),
            pltpu.VMEM((4 * per_pair, width), F32),
        ],
        compiler_params=pltpu.CompilerParams(vmem_limit_bytes=VMEM_LIMIT),
        name="serve",
    )(asked, store_rows)


def score_kernel(
    pos_smem,
    home_smem,
    valid_smem,
    count_smem,
    home_ref,
    sizes_ref,
    arrived_ref,
    cand_ref,
    row_ref,
    wq_ref,
    wk_ref,
    wv_ref,
    wo_ref,
    m1_ref,
    b1_ref,
    m2_ref,
    b2_ref,
    sp_ref,
    out_ref,
    arr_scr,
    x_scr,
    sz_scr,
    k_scr,
    v_scr,
):
    r = pl.program_id(0)
    slots, width = x_scr.shape
    cands = cand_ref.shape[1]
    per_req = slots // LANES
    head_size = width // HEADS
    step = 256

    @pl.when(r == 0)
    def _():
        arr_scr[...] = arrived_ref[...].astype(F32)
        x_scr[...] = jnp.zeros_like(x_scr)
        sz_scr[...] = jnp.zeros_like(sz_scr)
        out_ref[...] = jnp.zeros_like(out_ref)

    valid = valid_smem[r]
    count = count_smem[r]

    unroll = 32

    def fetch(b, carry):
        line = r * per_req + b // (LANES // unroll)
        col = lax.rem(b, LANES // unroll) * unroll
        for u in range(unroll):
            at = pos_smem[line, col + u]
            home = home_smem[line, col + u]
            x_scr[pl.ds(b * unroll + u, 1), :] = arr_scr[pl.ds(at, 1), :]
            sz_scr[pl.ds(b * unroll + u, 1), :] = sizes_ref[
                pl.ds(lax.shift_right_logical(home, 7), 1), :
            ]
        return carry

    lax.fori_loop(0, pl.cdiv(valid, unroll), fetch, 0)

    x = x_scr[...].astype(BF)
    keys = jnp.dot(x, wk_ref[...], preferred_element_type=F32).astype(BF).astype(F32) * 0.125
    values = jnp.dot(x, wv_ref[...], preferred_element_type=F32).astype(BF).astype(F32)
    sizes = []
    for t in range(per_req):
        home_col = column_of(home_ref[0, t : t + 1, :])
        size = lane_pick(sz_scr[t * LANES : (t + 1) * LANES, :], home_col & (LANES - 1))
        slot = lax.broadcasted_iota(jnp.int32, (LANES, LANES), 0) + t * LANES
        sizes.append(jnp.where(slot < valid, size, -1e30))
    sizes = jnp.concatenate(sizes, axis=0)
    lane = lax.broadcasted_iota(jnp.int32, (slots, LANES), 1)
    bias = jnp.where(lane == 0, sizes, 0.0).astype(BF)
    for h in range(HEADS):
        half = slice((h // 2) * LANES, (h // 2 + 1) * LANES)
        other = slice((1 - h // 2) * LANES, (2 - h // 2) * LANES)
        mine = (lane // head_size) == (h % 2)
        k_scr[h, :, half] = jnp.where(mine, keys[:, half], 0.0).astype(BF)
        k_scr[h, :, other] = bias
        v_scr[h, :, :LANES] = jnp.where(mine, values[:, half], 0.0).astype(BF)
        v_scr[h, :, LANES:] = jnp.where(mine, 1.0, 0.0).astype(BF)

    for c in range(0, cands, step):
        cand = cand_ref[0, c : c + step, :]
        query = jnp.dot(cand, wq_ref[...], preferred_element_type=F32)
        clane = lax.broadcasted_iota(jnp.int32, (step, LANES), 1)
        halves = []
        for p in range(2):
            own = query[:, p * LANES : (p + 1) * LANES].astype(BF)
            other = query[:, (1 - p) * LANES : (2 - p) * LANES]
            other = jnp.where(clane == 0, 1.0, other).astype(BF)
            parts = [own, other] if p == 0 else [other, own]
            q_p = jnp.concatenate(parts, axis=1)
            total = None
            for h in (2 * p, 2 * p + 1):
                logits = lax.dot_general(q_p, k_scr[h], NT, preferred_element_type=F32)
                top = jnp.max(logits, axis=1, keepdims=True)
                probs = jnp.exp(logits - top).astype(BF)
                part = jnp.dot(probs, v_scr[h], preferred_element_type=F32)
                total = part if total is None else total + part
            halves.append((total[:, :LANES] / total[:, LANES:]).astype(BF))
        context = jnp.concatenate(halves, axis=1)
        attended = jnp.dot(context, wo_ref[...], preferred_element_type=F32).astype(BF)
        hidden = jnp.dot(cand, m1_ref[:width, :], preferred_element_type=F32)
        hidden += jnp.dot(attended, m1_ref[width:, :], preferred_element_type=F32)
        hidden = jnp.maximum(hidden + b1_ref[...], 0.0).astype(BF)
        hidden = jnp.dot(hidden, m2_ref[...], preferred_element_type=F32)
        hidden = jnp.maximum(hidden + b2_ref[...], 0.0).astype(BF)
        score = lax.dot_general(sp_ref[...], hidden, NT, preferred_element_type=F32)[0:1, :]
        slot = lax.broadcasted_iota(jnp.int32, (1, step), 1) + c
        score = jnp.where(slot < count, score, 0.0)
        first = score.astype(BF).astype(F32)
        second = score - first
        row = row_ref[0, :, c : c + step]
        lines = out_ref.shape[0]
        at_line = lax.broadcasted_iota(jnp.int32, (lines, step), 0) == lax.shift_right_logical(row, 7)
        at_lane = lax.broadcasted_iota(jnp.int32, (LANES, step), 0) == (row & (LANES - 1))
        at_lane = jnp.where(at_lane, 1.0, 0.0).astype(BF)
        out_ref[...] += lax.dot_general(
            jnp.where(at_line, first, 0.0).astype(BF), at_lane, NT, preferred_element_type=F32
        ) + lax.dot_general(
            jnp.where(at_line, second, 0.0).astype(BF), at_lane, NT, preferred_element_type=F32
        )


def score(pos, home, valid, count, sizes, arrived, candidates, rows, weights, lines):
    reqs, cands, width = candidates.shape
    slots = pos.size // reqs
    sm = pl.BlockSpec(memory_space=pltpu.SMEM)

    def whole(a):
        return pl.BlockSpec(a.shape, lambda r, n=a.ndim: (0,) * n)

    home3 = home.reshape(reqs, slots // LANES, LANES)
    rows3 = rows.reshape(reqs, 1, cands)
    return pl.pallas_call(
        score_kernel,
        grid=(reqs,),
        out_shape=jax.ShapeDtypeStruct((lines, LANES), F32),
        in_specs=[
            sm,
            sm,
            sm,
            sm,
            pl.BlockSpec((1, slots // LANES, LANES), lambda r: (r, 0, 0)),
            whole(sizes),
            whole(arrived),
            pl.BlockSpec((1, cands, width), lambda r: (r, 0, 0)),
            pl.BlockSpec((1, 1, cands), lambda r: (r, 0, 0)),
        ]
        + [whole(w) for w in weights],
        out_specs=pl.BlockSpec((lines, LANES), lambda r: (0, 0)),
        scratch_shapes=[
            pltpu.VMEM(arrived.shape, F32),
            pltpu.VMEM((slots, width), F32),
            pltpu.VMEM((slots, LANES), F32),
            pltpu.VMEM((HEADS, slots, width), BF),
            pltpu.VMEM((HEADS, slots, width), BF),
        ],
        compiler_params=pltpu.CompilerParams(vmem_limit_bytes=VMEM_LIMIT),
        name="score",
    )(pos, home, valid, count, home3, sizes, arrived, candidates, rows3, *weights)


def on_device(
    store_rows,
    cluster_logsize,
    cluster_home,
    cluster_ids,
    valid_count,
    candidates,
    cand_count,
    candidate_row,
    query_proj,
    key_proj,
    value_proj,
    out_proj,
    mlp_first,
    bias_first,
    mlp_second,
    bias_second,
    score_proj,
):
    device_count = lax.axis_size(AXES)
    scorer_count = lax.axis_size("scorer")
    rows_dev, width = store_rows.shape
    slot_total = cluster_ids.size
    per_pair = slot_total // device_count
    reqs, cands = candidate_row.shape
    sizes = lax.all_gather(cluster_logsize, AXES, tiled=True)
    sizes = sizes.astype(F32).reshape(-1, LANES)
    ask, pos, home = route(
        cluster_ids.reshape(-1, LANES), cluster_home.reshape(-1, LANES), rows_dev, per_pair
    )
    asked = lax.all_to_all(
        ask[:device_count, :per_pair], AXES, split_axis=0, concat_axis=0, tiled=True
    )
    found = serve(asked, store_rows, per_pair)
    arrived = lax.all_to_all(
        found.reshape(device_count, per_pair, width), AXES, split_axis=0, concat_axis=0, tiled=True
    ).reshape(slot_total, width)
    weights = (
        query_proj,
        key_proj,
        value_proj,
        out_proj,
        mlp_first,
        bias_first.reshape(1, -1),
        mlp_second,
        bias_second.reshape(1, -1),
        jnp.broadcast_to(score_proj.reshape(1, -1), (16, score_proj.size)),
    )
    lines = scorer_count * (reqs * cands // 2) // LANES
    table = score(
        pos, home, valid_count, cand_count, sizes, arrived, candidates, candidate_row, weights, lines
    )
    blocks = table.reshape(scorer_count, lines // scorer_count, LANES)
    blocks = lax.all_to_all(blocks, "scorer", split_axis=0, concat_axis=0, tiled=True)
    return jnp.sum(blocks, axis=0).reshape(-1)


def solution(mesh):
    split = P(AXES)
    in_specs = (
        P(AXES, None),
        split,
        P(),
        P(AXES, None),
        split,
        P(AXES, None, None),
        split,
        P(AXES, None),
    ) + (P(),) * 9
    return jax.shard_map(
        on_device, mesh=mesh, in_specs=in_specs, out_specs=split, check_vma=False
    )
```

```python
import functools

import jax
import jax.numpy as jnp
from jax import lax
from jax.experimental import pallas as pl
from jax.experimental.pallas import tpu as pltpu
from jax.sharding import PartitionSpec as P

HEADS = 4
AXES = ("store", "scorer")
LANES = 128
NT = (((1,), (1,)), ((), ()))
TN = (((0,), (0,)), ((), ()))
BF = jnp.bfloat16
F32 = jnp.float32
VMEM_LIMIT = 48 * 1024 * 1024
MESH = pl.DeviceIdType.MESH


def lane_pick(rows, lane_index):
    return jnp.take_along_axis(rows, lane_index, axis=1)


def column_of(row):
    return jnp.broadcast_to(row, (LANES, LANES)).T


def route_kernel(rows_dev, per_pair, ids_smem, ids_ref, table_ref, ask_ref, pos_ref, rows_scr):
    tiles = ids_ref.shape[0]
    shift_rows = rows_dev.bit_length() - 1

    def fetch(t, carry):
        for u in range(LANES):
            c = ids_smem[t, u]
            rows_scr[pl.ds(t * LANES + u, 1), :] = table_ref[
                pl.ds(lax.shift_right_logical(c, 7), 1), :
            ]
        return carry

    lax.fori_loop(0, tiles, fetch, 0)
    lane = lax.broadcasted_iota(jnp.int32, (LANES, LANES), 1)
    sub = lax.broadcasted_iota(jnp.int32, (LANES, LANES), 0)
    lower = jnp.where(sub >= lane, 1.0, 0.0).astype(BF)
    ones = jnp.ones((LANES, LANES), BF)
    base = jnp.zeros((1, LANES), F32)
    acc = jnp.zeros((LANES, 2 * LANES), F32)
    for t in range(tiles):
        ids_col = column_of(ids_ref[t : t + 1, :])
        home = lane_pick(rows_scr[t * LANES : (t + 1) * LANES, :], ids_col & (LANES - 1))
        dest = lax.shift_right_logical(home, shift_rows)
        hot = dest == lane
        hot_b = jnp.where(hot, 1.0, 0.0).astype(BF)
        incl = jnp.dot(lower, hot_b, preferred_element_type=F32)
        picked = jnp.where(hot, incl + (base - 1.0), 0.0).astype(BF)
        rank = jnp.dot(picked, ones, preferred_element_type=F32).astype(jnp.int32)
        base = base + incl[LANES - 1 : LANES, :]
        low = (home & 255).astype(F32)
        high = (lax.shift_right_logical(home, 8) & ((rows_dev >> 8) - 1)).astype(F32)
        at = rank == lane
        parts = jnp.concatenate(
            [jnp.where(at, low, 0.0), jnp.where(at, high, 0.0)], axis=1
        ).astype(BF)
        acc = acc + lax.dot_general(hot_b, parts, TN, preferred_element_type=F32)
        diag = sub == lane
        pos = (dest * per_pair + rank).astype(F32)
        pos_ref[t : t + 1, :] = jnp.sum(
            jnp.where(diag, pos, 0.0), axis=0, keepdims=True
        ).astype(jnp.int32)
    ask_ref[...] = (acc[:, :LANES] + 256.0 * acc[:, LANES:]).astype(jnp.int32)


def route(ids, table, rows_dev, per_pair):
    tiles = ids.shape[0]
    vm = pl.BlockSpec(memory_space=pltpu.VMEM)
    return pl.pallas_call(
        functools.partial(route_kernel, rows_dev, per_pair),
        out_shape=(
            jax.ShapeDtypeStruct((LANES, LANES), jnp.int32),
            jax.ShapeDtypeStruct((tiles, LANES), jnp.int32),
        ),
        in_specs=[pl.BlockSpec(memory_space=pltpu.SMEM), vm, vm],
        out_specs=(vm, vm),
        scratch_shapes=[pltpu.VMEM((tiles * LANES, LANES), jnp.int32)],
        compiler_params=pltpu.CompilerParams(vmem_limit_bytes=VMEM_LIMIT),
        name="route",
    )(ids, ids, table)


def peer_of(step, stores, scorers):
    store = lax.rem(lax.axis_index("store") + step // scorers, stores)
    scorer = lax.rem(lax.axis_index("scorer") + lax.rem(step, scorers), scorers)
    return store, scorer


def exchange_kernel(
    stores,
    scorers,
    per_pair,
    ask_ref,
    store_ref,
    sizes_ref,
    rows_out,
    sizes_out,
    ask_in,
    ask_smem,
    store_scr,
    size_scr,
    stage,
    size_stage,
    rows_send,
    sizes_send,
    send_sems,
    recv_sems,
    local_sem,
):
    pairs = stores * scorers
    me = lax.axis_index("store") * scorers + lax.axis_index("scorer")
    barrier = pltpu.get_barrier_semaphore()

    def greet(i, carry):
        pl.semaphore_signal(barrier, inc=1, device_id=peer_of(i, stores, scorers), device_id_type=MESH)
        return carry

    lax.fori_loop(1, pairs, greet, 0)
    store_scr[...] = store_ref[...].astype(F32)
    for t in range(sizes_ref.shape[0]):
        size_scr[t * LANES : (t + 1) * LANES, :] = column_of(sizes_ref[t : t + 1, :])
    pl.semaphore_wait(barrier, pairs - 1)

    def ask(i, carry):
        store, scorer = peer_of(i, stores, scorers)
        pltpu.make_async_remote_copy(
            src_ref=ask_ref.at[store * scorers + scorer],
            dst_ref=ask_in.at[me],
            send_sem=send_sems.at[0],
            recv_sem=recv_sems.at[0],
            device_id=(store, scorer),
            device_id_type=MESH,
        ).start()
        return carry

    lax.fori_loop(1, pairs, ask, 0)
    ask_in[me] = ask_ref[me]

    def settle(ref, sem):
        part = ref.at[pl.ds(0, pairs - 1)]
        pltpu.make_async_copy(part, part, sem).wait()

    settle(ask_in, recv_sems.at[0])
    down = pltpu.make_async_copy(ask_in, ask_smem, local_sem)
    down.start()
    down.wait()

    lane = lax.broadcasted_iota(jnp.int32, (per_pair, LANES), 1)
    sub = lax.broadcasted_iota(jnp.int32, (per_pair, LANES), 0)

    def collect(who):
        for j in range(per_pair):
            row = ask_smem[who, 0, j]
            stage[pl.ds(j, 1), :] = store_scr[pl.ds(row, 1), :]
            size_stage[pl.ds(j, 1), :] = size_scr[pl.ds(row, 1), :]
        sizes = jnp.sum(jnp.where(lane == sub, size_stage[...], 0.0), axis=0, keepdims=True)
        return stage[...].astype(BF), sizes

    def answer(i, carry):
        store, scorer = peer_of(i, stores, scorers)
        who = store * scorers + scorer
        rows, sizes = collect(who)
        rows_send[who] = rows
        sizes_send[who] = sizes
        pltpu.make_async_remote_copy(
            src_ref=rows_send.at[who],
            dst_ref=rows_out.at[me],
            send_sem=send_sems.at[1],
            recv_sem=recv_sems.at[1],
            device_id=(store, scorer),
            device_id_type=MESH,
        ).start()
        pltpu.make_async_remote_copy(
            src_ref=sizes_send.at[who],
            dst_ref=sizes_out.at[me],
            send_sem=send_sems.at[2],
            recv_sem=recv_sems.at[2],
            device_id=(store, scorer),
            device_id_type=MESH,
        ).start()
        return carry

    lax.fori_loop(1, pairs, answer, 0)
    rows, sizes = collect(me)
    rows_out[me] = rows
    sizes_out[me] = sizes
    settle(ask_in, send_sems.at[0])
    settle(rows_send, send_sems.at[1])
    settle(sizes_send, send_sems.at[2])
    settle(rows_out, recv_sems.at[1])
    settle(sizes_out, recv_sems.at[2])


def exchange(ask, store_rows, logsize, stores, scorers, per_pair):
    pairs = stores * scorers
    width = store_rows.shape[1]
    vm = pl.BlockSpec(memory_space=pltpu.VMEM)
    return pl.pallas_call(
        functools.partial(exchange_kernel, stores, scorers, per_pair),
        out_shape=(
            jax.ShapeDtypeStruct((pairs, per_pair, width), BF),
            jax.ShapeDtypeStruct((pairs, 1, LANES), F32),
        ),
        in_specs=[vm, vm, vm],
        out_specs=(vm, vm),
        scratch_shapes=[
            pltpu.VMEM((pairs, 1, LANES), jnp.int32),
            pltpu.SMEM((pairs, 1, LANES), jnp.int32),
            pltpu.VMEM(store_rows.shape, F32),
            pltpu.VMEM((store_rows.shape[0], LANES), F32),
            pltpu.VMEM((per_pair, width), F32),
            pltpu.VMEM((per_pair, LANES), F32),
            pltpu.VMEM((pairs, per_pair, width), BF),
            pltpu.VMEM((pairs, 1, LANES), F32),
            pltpu.SemaphoreType.DMA((3,)),
            pltpu.SemaphoreType.DMA((3,)),
            pltpu.SemaphoreType.DMA,
        ],
        compiler_params=pltpu.CompilerParams(
            vmem_limit_bytes=VMEM_LIMIT, collective_id=0, has_side_effects=True
        ),
        name="exchange",
    )(ask, store_rows, logsize)


def gather_kernel(scorers, table_ref, out_ref, landed, send_sem, recv_sem):
    part = out_ref.shape[0]
    store = lax.axis_index("store")
    me = lax.axis_index("scorer")
    barrier = pltpu.get_barrier_semaphore()

    def greet(i, carry):
        pl.semaphore_signal(
            barrier, inc=1, device_id=(store, lax.rem(me + i, scorers)), device_id_type=MESH
        )
        return carry

    lax.fori_loop(1, scorers, greet, 0)
    pl.semaphore_wait(barrier, scorers - 1)

    def send(i, carry):
        to = lax.rem(me + i, scorers)
        pltpu.make_async_remote_copy(
            src_ref=table_ref.at[to],
            dst_ref=landed.at[i - 1],
            send_sem=send_sem,
            recv_sem=recv_sem,
            device_id=(store, to),
            device_id_type=MESH,
        ).start()
        return carry

    lax.fori_loop(1, scorers, send, 0)
    pltpu.make_async_copy(landed, landed, send_sem).wait()
    pltpu.make_async_copy(landed, landed, recv_sem).wait()
    out_ref[...] = table_ref[me] + jnp.sum(landed[...], axis=0)


def gather_spans(table, scorers):
    lines = table.shape[0] // scorers
    vm = pl.BlockSpec(memory_space=pltpu.VMEM)
    return pl.pallas_call(
        functools.partial(gather_kernel, scorers),
        out_shape=jax.ShapeDtypeStruct((lines, LANES), F32),
        in_specs=[vm],
        out_specs=vm,
        scratch_shapes=[
            pltpu.VMEM((scorers - 1, lines, LANES), F32),
            pltpu.SemaphoreType.DMA,
            pltpu.SemaphoreType.DMA,
        ],
        compiler_params=pltpu.CompilerParams(collective_id=1, has_side_effects=True),
        name="gather_spans",
    )(table.reshape(scorers, lines, LANES))


def score_kernel(
    per_pair,
    pos_smem,
    valid_smem,
    count_smem,
    pos_ref,
    sizes_ref,
    arrived_ref,
    cand_ref,
    row_ref,
    wq_ref,
    wk_ref,
    wv_ref,
    wo_ref,
    m1_ref,
    b1_ref,
    m2_ref,
    b2_ref,
    sp_ref,
    out_ref,
    arr_scr,
    x_scr,
    sz_scr,
    k_scr,
    v_scr,
):
    r = pl.program_id(0)
    slots, width = x_scr.shape
    cands = cand_ref.shape[1]
    per_req = slots // LANES
    head_size = width // HEADS
    step = 256
    pair_shift = per_pair.bit_length() - 1

    @pl.when(r == 0)
    def _():
        arr_scr[...] = arrived_ref[...].astype(F32)
        x_scr[...] = jnp.zeros_like(x_scr)
        sz_scr[...] = jnp.zeros_like(sz_scr)
        out_ref[...] = jnp.zeros_like(out_ref)

    valid = valid_smem[r]
    count = count_smem[r]

    unroll = 32

    def fetch(b, carry):
        line = r * per_req + b // (LANES // unroll)
        col = lax.rem(b, LANES // unroll) * unroll
        for u in range(unroll):
            at = pos_smem[line, col + u]
            x_scr[pl.ds(b * unroll + u, 1), :] = arr_scr[pl.ds(at, 1), :]
            sz_scr[pl.ds(b * unroll + u, 1), :] = sizes_ref[
                pl.ds(lax.shift_right_logical(at, pair_shift), 1), :
            ]
        return carry

    lax.fori_loop(0, pl.cdiv(valid, unroll), fetch, 0)

    x = x_scr[...].astype(BF)
    keys = jnp.dot(x, wk_ref[...], preferred_element_type=F32).astype(BF).astype(F32) * 0.125
    values = jnp.dot(x, wv_ref[...], preferred_element_type=F32).astype(BF).astype(F32)
    sizes = []
    for t in range(per_req):
        pos_col = column_of(pos_ref[0, t : t + 1, :])
        size = lane_pick(sz_scr[t * LANES : (t + 1) * LANES, :], pos_col & (per_pair - 1))
        slot = lax.broadcasted_iota(jnp.int32, (LANES, LANES), 0) + t * LANES
        sizes.append(jnp.where(slot < valid, size, -1e30))
    sizes = jnp.concatenate(sizes, axis=0)
    lane = lax.broadcasted_iota(jnp.int32, (slots, LANES), 1)
    bias = jnp.where(lane == 0, sizes, 0.0).astype(BF)
    for h in range(HEADS):
        half = slice((h // 2) * LANES, (h // 2 + 1) * LANES)
        other = slice((1 - h // 2) * LANES, (2 - h // 2) * LANES)
        mine = (lane // head_size) == (h % 2)
        k_scr[h, :, half] = jnp.where(mine, keys[:, half], 0.0).astype(BF)
        k_scr[h, :, other] = bias
        v_scr[h, :, :LANES] = jnp.where(mine, values[:, half], 0.0).astype(BF)
        v_scr[h, :, LANES:] = jnp.where(mine, 1.0, 0.0).astype(BF)

    for c in range(0, cands, step):
        cand = cand_ref[0, c : c + step, :]
        query = jnp.dot(cand, wq_ref[...], preferred_element_type=F32)
        clane = lax.broadcasted_iota(jnp.int32, (step, LANES), 1)
        halves = []
        for p in range(2):
            own = query[:, p * LANES : (p + 1) * LANES].astype(BF)
            other = query[:, (1 - p) * LANES : (2 - p) * LANES]
            other = jnp.where(clane == 0, 1.0, other).astype(BF)
            parts = [own, other] if p == 0 else [other, own]
            q_p = jnp.concatenate(parts, axis=1)
            total = None
            for h in (2 * p, 2 * p + 1):
                logits = lax.dot_general(q_p, k_scr[h], NT, preferred_element_type=F32)
                top = jnp.max(logits, axis=1, keepdims=True)
                probs = jnp.exp(logits - top).astype(BF)
                part = jnp.dot(probs, v_scr[h], preferred_element_type=F32)
                total = part if total is None else total + part
            halves.append((total[:, :LANES] / total[:, LANES:]).astype(BF))
        context = jnp.concatenate(halves, axis=1)
        attended = jnp.dot(context, wo_ref[...], preferred_element_type=F32).astype(BF)
        hidden = jnp.dot(cand, m1_ref[:width, :], preferred_element_type=F32)
        hidden += jnp.dot(attended, m1_ref[width:, :], preferred_element_type=F32)
        hidden = jnp.maximum(hidden + b1_ref[...], 0.0).astype(BF)
        hidden = jnp.dot(hidden, m2_ref[...], preferred_element_type=F32)
        hidden = jnp.maximum(hidden + b2_ref[...], 0.0).astype(BF)
        score = lax.dot_general(sp_ref[...], hidden, NT, preferred_element_type=F32)[0:1, :]
        slot = lax.broadcasted_iota(jnp.int32, (1, step), 1) + c
        score = jnp.where(slot < count, score, 0.0)
        first = score.astype(BF).astype(F32)
        second = score - first
        row = row_ref[0, :, c : c + step]
        lines = out_ref.shape[0]
        at_line = lax.broadcasted_iota(jnp.int32, (lines, step), 0) == lax.shift_right_logical(row, 7)
        at_lane = lax.broadcasted_iota(jnp.int32, (LANES, step), 0) == (row & (LANES - 1))
        at_lane = jnp.where(at_lane, 1.0, 0.0).astype(BF)
        out_ref[...] += lax.dot_general(
            jnp.where(at_line, first, 0.0).astype(BF), at_lane, NT, preferred_element_type=F32
        ) + lax.dot_general(
            jnp.where(at_line, second, 0.0).astype(BF), at_lane, NT, preferred_element_type=F32
        )


def score(pos, per_pair, valid, count, sizes, arrived, candidates, rows, weights, lines):
    reqs, cands, width = candidates.shape
    slots = pos.size // reqs
    sm = pl.BlockSpec(memory_space=pltpu.SMEM)

    def whole(a):
        return pl.BlockSpec(a.shape, lambda r, n=a.ndim: (0,) * n)

    pos3 = pos.reshape(reqs, slots // LANES, LANES)
    rows3 = rows.reshape(reqs, 1, cands)
    return pl.pallas_call(
        functools.partial(score_kernel, per_pair),
        grid=(reqs,),
        out_shape=jax.ShapeDtypeStruct((lines, LANES), F32),
        in_specs=[
            sm,
            sm,
            sm,
            pl.BlockSpec((1, slots // LANES, LANES), lambda r: (r, 0, 0)),
            whole(sizes),
            whole(arrived),
            pl.BlockSpec((1, cands, width), lambda r: (r, 0, 0)),
            pl.BlockSpec((1, 1, cands), lambda r: (r, 0, 0)),
        ]
        + [whole(w) for w in weights],
        out_specs=pl.BlockSpec((lines, LANES), lambda r: (0, 0)),
        scratch_shapes=[
            pltpu.VMEM(arrived.shape, F32),
            pltpu.VMEM((slots, width), F32),
            pltpu.VMEM((slots, LANES), F32),
            pltpu.VMEM((HEADS, slots, width), BF),
            pltpu.VMEM((HEADS, slots, width), BF),
        ],
        compiler_params=pltpu.CompilerParams(vmem_limit_bytes=VMEM_LIMIT),
        name="score",
    )(pos, valid, count, pos3, sizes, arrived, candidates, rows3, *weights)


def on_device(
    store_rows,
    cluster_logsize,
    cluster_home,
    cluster_ids,
    valid_count,
    candidates,
    cand_count,
    candidate_row,
    query_proj,
    key_proj,
    value_proj,
    out_proj,
    mlp_first,
    bias_first,
    mlp_second,
    bias_second,
    score_proj,
):
    device_count = lax.axis_size(AXES)
    scorer_count = lax.axis_size("scorer")
    rows_dev, width = store_rows.shape
    slot_total = cluster_ids.size
    per_pair = slot_total // device_count
    reqs, cands = candidate_row.shape
    ask, pos = route(
        cluster_ids.reshape(-1, LANES), cluster_home.reshape(-1, LANES), rows_dev, per_pair
    )
    arrived, sizes = exchange(
        ask.reshape(device_count, 1, LANES),
        store_rows,
        cluster_logsize.astype(F32).reshape(-1, LANES),
        device_count // scorer_count,
        scorer_count,
        per_pair,
    )
    arrived = arrived.reshape(slot_total, width)
    sizes = sizes.reshape(device_count, LANES)
    weights = (
        query_proj,
        key_proj,
        value_proj,
        out_proj,
        mlp_first,
        bias_first.reshape(1, -1),
        mlp_second,
        bias_second.reshape(1, -1),
        jnp.broadcast_to(score_proj.reshape(1, -1), (16, score_proj.size)),
    )
    lines = scorer_count * (reqs * cands // 2) // LANES
    table = score(
        pos, per_pair, valid_count, cand_count, sizes, arrived, candidates, candidate_row, weights, lines
    )
    return gather_spans(table, scorer_count).reshape(-1)


def solution(mesh):
    split = P(AXES)
    in_specs = (
        P(AXES, None),
        split,
        P(),
        P(AXES, None),
        split,
        P(AXES, None, None),
        split,
        P(AXES, None),
    ) + (P(),) * 9
    return jax.shard_map(
        on_device, mesh=mesh, in_specs=in_specs, out_specs=split, check_vma=False
    )
```

```python
import functools

import jax
import jax.numpy as jnp
from jax import lax
from jax.experimental import pallas as pl
from jax.experimental.pallas import tpu as pltpu
from jax.sharding import PartitionSpec as P

HEADS = 4
CHUNK = 16
AXES = ("store", "scorer")
LANES = 128
NT = (((1,), (1,)), ((), ()))
TN = (((0,), (0,)), ((), ()))
BF = jnp.bfloat16
F32 = jnp.float32
VMEM_LIMIT = 48 * 1024 * 1024
MESH = pl.DeviceIdType.MESH


def lane_pick(rows, lane_index):
    return jnp.take_along_axis(rows, lane_index, axis=1)


def column_of(row):
    return jnp.broadcast_to(row, (LANES, LANES)).T


def route_kernel(rows_dev, per_pair, ids_smem, valid_smem, ids_ref, table_ref, ask_ref, plan_ref, rows_scr):
    reqs, slots = ids_ref.shape
    per_req = slots // LANES
    shift_rows = rows_dev.bit_length() - 1

    def fetch(r, carry):
        start = pl.multiple_of(r * slots, slots)
        for u in range(slots):
            c = ids_smem[r, u]
            rows_scr[pl.ds(start + u, 1), :] = table_ref[pl.ds(lax.shift_right_logical(c, 7), 1), :]
        return carry

    lax.fori_loop(0, reqs, fetch, 0)
    lane = lax.broadcasted_iota(jnp.int32, (LANES, LANES), 1)
    sub = lax.broadcasted_iota(jnp.int32, (LANES, LANES), 0)
    lower = jnp.where(sub >= lane, 1.0, 0.0).astype(BF)
    before = jnp.where(sub < lane, 1.0, 0.0).astype(BF)
    ones = jnp.ones((LANES, LANES), BF)
    base = jnp.zeros((1, LANES), F32)
    acc = jnp.zeros((LANES, 2 * LANES), F32)
    bases = []
    for t in range(reqs * per_req):
        r, q = t // per_req, t % per_req
        if q == 0:
            bases.append(base)
        ids_col = column_of(ids_ref[r : r + 1, q * LANES : (q + 1) * LANES])
        home = lane_pick(rows_scr[t * LANES : (t + 1) * LANES, :], ids_col & (LANES - 1))
        hot = lax.shift_right_logical(home, shift_rows) == lane
        hot = jnp.where(sub + q * LANES < valid_smem[r], jnp.where(hot, 1.0, 0.0), 0.0)
        hot_b = hot.astype(BF)
        incl = jnp.dot(lower, hot_b, preferred_element_type=F32)
        picked = (hot * (incl + (base - 1.0))).astype(BF)
        rank = jnp.dot(picked, ones, preferred_element_type=F32).astype(jnp.int32)
        base = base + incl[LANES - 1 : LANES, :]
        low = (home & 255).astype(F32)
        high = (lax.shift_right_logical(home, 8) & ((rows_dev >> 8) - 1)).astype(F32)
        at = rank == lane
        parts = jnp.concatenate(
            [jnp.where(at, low, 0.0), jnp.where(at, high, 0.0)], axis=1
        ).astype(BF)
        acc = acc + lax.dot_general(hot_b, parts, TN, preferred_element_type=F32)
    bases.append(base)
    ask_ref[...] = (acc[:, :LANES] + 256.0 * acc[:, LANES:]).astype(jnp.int32)
    starts = jnp.concatenate(bases[:reqs], axis=0)
    counts = jnp.concatenate(bases[1:], axis=0) - starts
    spots = jnp.dot(counts.astype(BF), before, preferred_element_type=F32)
    source = lax.broadcasted_iota(jnp.int32, (reqs, LANES), 1) * per_pair
    plan_ref[0:reqs, :] = source + starts.astype(jnp.int32)
    plan_ref[reqs : 2 * reqs, :] = spots.astype(jnp.int32)
    plan_ref[2 * reqs : 3 * reqs, :] = counts.astype(jnp.int32)
    most = jnp.max(counts, axis=1, keepdims=True)
    plan_ref[3 * reqs :, :] = jnp.broadcast_to(most, (reqs, LANES)).astype(jnp.int32)


def route(ids, valid, table, rows_dev, per_pair):
    reqs, slots = ids.shape
    sm = pl.BlockSpec(memory_space=pltpu.SMEM)
    vm = pl.BlockSpec(memory_space=pltpu.VMEM)
    return pl.pallas_call(
        functools.partial(route_kernel, rows_dev, per_pair),
        out_shape=(
            jax.ShapeDtypeStruct((LANES, LANES), jnp.int32),
            jax.ShapeDtypeStruct((4 * reqs, LANES), jnp.int32),
        ),
        in_specs=[sm, sm, vm, vm],
        out_specs=(vm, vm),
        scratch_shapes=[pltpu.VMEM((reqs * slots, LANES), jnp.int32)],
        compiler_params=pltpu.CompilerParams(vmem_limit_bytes=VMEM_LIMIT),
        name="route",
    )(ids, valid, ids, table)


def peer_of(step, stores, scorers):
    store = lax.rem(lax.axis_index("store") + step // scorers, stores)
    scorer = lax.rem(lax.axis_index("scorer") + lax.rem(step, scorers), scorers)
    return store, scorer


def exchange_kernel(
    stores,
    scorers,
    per_pair,
    ask_ref,
    store_ref,
    sizes_ref,
    rows_out,
    sizes_out,
    ask_in,
    ask_smem,
    left_scr,
    right_scr,
    size_scr,
    left,
    right,
    size_stage,
    rows_send,
    sizes_send,
    send_sems,
    recv_sems,
    local_sem,
):
    pairs = stores * scorers
    me = lax.axis_index("store") * scorers + lax.axis_index("scorer")
    barrier = pltpu.get_barrier_semaphore()

    def greet(i, carry):
        pl.semaphore_signal(barrier, inc=1, device_id=peer_of(i, stores, scorers), device_id_type=MESH)
        return carry

    lax.fori_loop(1, pairs, greet, 0)
    left_scr[...] = store_ref[:, :LANES].astype(F32)
    right_scr[...] = store_ref[:, LANES:].astype(F32)
    offsets = sizes_ref[...].astype(F32)
    for t in range(sizes_ref.shape[0]):
        size_scr[t * LANES : (t + 1) * LANES, :] = column_of(offsets[t : t + 1, :])
    pl.semaphore_wait(barrier, pairs - 1)

    def ask(i, carry):
        store, scorer = peer_of(i, stores, scorers)
        pltpu.make_async_remote_copy(
            src_ref=ask_ref.at[store * scorers + scorer],
            dst_ref=ask_in.at[me],
            send_sem=send_sems.at[0],
            recv_sem=recv_sems.at[0],
            device_id=(store, scorer),
            device_id_type=MESH,
        ).start()
        return carry

    lax.fori_loop(1, pairs, ask, 0)
    ask_in[me] = ask_ref[me]

    def settle(ref, sem):
        part = ref.at[pl.ds(0, pairs - 1)]
        pltpu.make_async_copy(part, part, sem).wait()

    settle(ask_in, recv_sems.at[0])
    down = pltpu.make_async_copy(ask_in, ask_smem, local_sem)
    down.start()
    down.wait()

    lane = lax.broadcasted_iota(jnp.int32, (per_pair, LANES), 1)
    sub = lax.broadcasted_iota(jnp.int32, (per_pair, LANES), 0)
    sub = sub + lax.rem(me, LANES // per_pair) * per_pair

    def collect(who):
        for j in range(per_pair):
            row = ask_smem[who, 0, j]
            left[pl.ds(j, 1), :] = left_scr[pl.ds(row, 1), :]
            right[pl.ds(j, 1), :] = right_scr[pl.ds(row, 1), :]
            size_stage[pl.ds(j, 1), :] = size_scr[pl.ds(row, 1), :]
        sizes = jnp.sum(jnp.where(lane == sub, size_stage[...], 0.0), axis=0, keepdims=True)
        return left[...].astype(BF), right[...].astype(BF), sizes

    def answer(i, carry):
        store, scorer = peer_of(i, stores, scorers)
        who = store * scorers + scorer
        rows_send[who, :, :LANES], rows_send[who, :, LANES:], sizes_send[who] = collect(who)
        pltpu.make_async_remote_copy(
            src_ref=rows_send.at[who],
            dst_ref=rows_out.at[me],
            send_sem=send_sems.at[1],
            recv_sem=recv_sems.at[1],
            device_id=(store, scorer),
            device_id_type=MESH,
        ).start()
        pltpu.make_async_remote_copy(
            src_ref=sizes_send.at[who],
            dst_ref=sizes_out.at[me],
            send_sem=send_sems.at[2],
            recv_sem=recv_sems.at[2],
            device_id=(store, scorer),
            device_id_type=MESH,
        ).start()
        return carry

    lax.fori_loop(1, pairs, answer, 0)
    rows_out[me, :, :LANES], rows_out[me, :, LANES:], sizes_out[me] = collect(me)
    settle(ask_in, send_sems.at[0])
    settle(rows_send, send_sems.at[1])
    settle(sizes_send, send_sems.at[2])
    settle(rows_out, recv_sems.at[1])
    settle(sizes_out, recv_sems.at[2])


def exchange(ask, store_rows, logsize, stores, scorers, per_pair):
    pairs = stores * scorers
    width = store_rows.shape[1]
    vm = pl.BlockSpec(memory_space=pltpu.VMEM)
    return pl.pallas_call(
        functools.partial(exchange_kernel, stores, scorers, per_pair),
        out_shape=(
            jax.ShapeDtypeStruct((pairs, per_pair, width), BF),
            jax.ShapeDtypeStruct((pairs, 1, LANES), F32),
        ),
        in_specs=[vm, vm, vm],
        out_specs=(vm, vm),
        scratch_shapes=[
            pltpu.VMEM((pairs, 1, LANES), jnp.int32),
            pltpu.SMEM((pairs, 1, LANES), jnp.int32),
            pltpu.VMEM((store_rows.shape[0], LANES), F32),
            pltpu.VMEM((store_rows.shape[0], LANES), F32),
            pltpu.VMEM((store_rows.shape[0], LANES), F32),
            pltpu.VMEM((per_pair, LANES), F32),
            pltpu.VMEM((per_pair, LANES), F32),
            pltpu.VMEM((per_pair, LANES), F32),
            pltpu.VMEM((pairs, per_pair, width), BF),
            pltpu.VMEM((pairs, 1, LANES), F32),
            pltpu.SemaphoreType.DMA((3,)),
            pltpu.SemaphoreType.DMA((3,)),
            pltpu.SemaphoreType.DMA,
        ],
        compiler_params=pltpu.CompilerParams(
            vmem_limit_bytes=VMEM_LIMIT, collective_id=0, has_side_effects=True
        ),
        name="exchange",
    )(ask, store_rows, logsize)


def gather_kernel(scorers, table_ref, out_ref, landed, send_sem, recv_sem):
    part = out_ref.shape[0]
    store = lax.axis_index("store")
    me = lax.axis_index("scorer")
    barrier = pltpu.get_barrier_semaphore()

    def greet(i, carry):
        pl.semaphore_signal(
            barrier, inc=1, device_id=(store, lax.rem(me + i, scorers)), device_id_type=MESH
        )
        return carry

    lax.fori_loop(1, scorers, greet, 0)
    pl.semaphore_wait(barrier, scorers - 1)

    def send(i, carry):
        to = lax.rem(me + i, scorers)
        pltpu.make_async_remote_copy(
            src_ref=table_ref.at[to],
            dst_ref=landed.at[i - 1],
            send_sem=send_sem,
            recv_sem=recv_sem,
            device_id=(store, to),
            device_id_type=MESH,
        ).start()
        return carry

    lax.fori_loop(1, scorers, send, 0)
    pltpu.make_async_copy(landed, landed, send_sem).wait()
    pltpu.make_async_copy(landed, landed, recv_sem).wait()
    out_ref[...] = table_ref[me] + jnp.sum(landed[...], axis=0)


def gather_spans(table, scorers):
    lines = table.shape[0] // scorers
    vm = pl.BlockSpec(memory_space=pltpu.VMEM)
    return pl.pallas_call(
        functools.partial(gather_kernel, scorers),
        out_shape=jax.ShapeDtypeStruct((lines, LANES), F32),
        in_specs=[vm],
        out_specs=vm,
        scratch_shapes=[
            pltpu.VMEM((scorers - 1, lines, LANES), F32),
            pltpu.SemaphoreType.DMA,
            pltpu.SemaphoreType.DMA,
        ],
        compiler_params=pltpu.CompilerParams(collective_id=1, has_side_effects=True),
        name="gather_spans",
    )(table.reshape(scorers, lines, LANES))


def score_kernel(
    per_pair,
    plan_smem,
    valid_smem,
    count_smem,
    sizes_ref,
    arrived_ref,
    cand_ref,
    row_ref,
    wq_ref,
    wk_ref,
    wv_ref,
    wo_ref,
    m1_ref,
    b1_ref,
    m2_ref,
    b2_ref,
    sp_ref,
    out_ref,
    left_scr,
    right_scr,
    size_scr,
    x_left,
    x_right,
    x_size,
    k_scr,
    v_scr,
    ctx_scr,
):
    r = pl.program_id(0)
    reqs = pl.num_programs(0)
    total_slots, width = arrived_ref.shape
    slots = ctx_scr.shape[0]
    cands = cand_ref.shape[1]
    pairs = sizes_ref.shape[0]
    head_size = width // HEADS
    copies = ((left_scr, x_left), (right_scr, x_right), (size_scr, x_size))

    @pl.when(r == 0)
    def _():
        left_scr[:total_slots, :] = arrived_ref[:, :LANES].astype(F32)
        right_scr[:total_slots, :] = arrived_ref[:, LANES:].astype(F32)
        group = LANES // per_pair
        one = lax.broadcasted_iota(jnp.int32, (pairs // group, pairs), 1) // group
        one = one == lax.broadcasted_iota(jnp.int32, (pairs // group, pairs), 0)
        packed = jnp.dot(
            jnp.where(one, 1.0, 0.0).astype(BF),
            sizes_ref[...].astype(BF),
            preferred_element_type=F32,
        )
        for t in range(pairs // group):
            size_scr[t * LANES : (t + 1) * LANES, :] = column_of(packed[t : t + 1, :])
        for held, taken in copies:
            held[total_slots:, :] = jnp.zeros((CHUNK, LANES), F32)
            taken[...] = jnp.zeros_like(taken)
        out_ref[...] = jnp.zeros_like(out_ref)

    valid = valid_smem[r]
    count = count_smem[r]

    for s in range(pairs):
        at = plan_smem[r, s]
        to = plan_smem[r + reqs, s]
        for held, taken in copies:
            taken[pl.ds(to, CHUNK), :] = held[pl.ds(at, CHUNK), :]

    @pl.when(plan_smem[r + 3 * reqs, 0] > CHUNK)
    def _():
        def rest(s, carry):
            at = plan_smem[r, s]
            to = plan_smem[r + reqs, s]
            left = plan_smem[r + 2 * reqs, s]
            sub = lax.broadcasted_iota(jnp.int32, (CHUNK, LANES), 0)

            @pl.when(left > CHUNK)
            def _():
                for held, taken in copies:
                    old = taken[pl.ds(to + CHUNK, CHUNK), :]
                    new = held[pl.ds(at + CHUNK, CHUNK), :]
                    taken[pl.ds(to + CHUNK, CHUNK), :] = jnp.where(sub < left - CHUNK, new, old)

            return carry

        lax.fori_loop(0, pairs, rest, 0)

    cand = cand_ref[0]
    query = jnp.dot(cand, wq_ref[...], preferred_element_type=F32)
    clane = lax.broadcasted_iota(jnp.int32, (cands, LANES), 1)
    queries = []
    for p in range(2):
        own = query[:, p * LANES : (p + 1) * LANES].astype(BF)
        other = query[:, (1 - p) * LANES : (2 - p) * LANES]
        other = jnp.where(clane == 0, 1.0, other).astype(BF)
        queries.append(jnp.concatenate([own, other] if p == 0 else [other, own], axis=1))

    def attend(live):
        x = jnp.concatenate([x_left[:live, :], x_right[:live, :]], axis=1).astype(BF)
        keys = jnp.dot(x, wk_ref[...], preferred_element_type=F32).astype(BF).astype(F32) * 0.125
        values = jnp.dot(x, wv_ref[...], preferred_element_type=F32).astype(BF).astype(F32)
        lane = lax.broadcasted_iota(jnp.int32, (live, LANES), 1)
        slot = lax.broadcasted_iota(jnp.int32, (live, LANES), 0)
        bias = jnp.where(slot < valid, x_size[:live, :], -1e30)
        bias = jnp.where(lane == 0, bias, 0.0).astype(BF)
        for h in range(HEADS):
            half = slice((h // 2) * LANES, (h // 2 + 1) * LANES)
            other = slice((1 - h // 2) * LANES, (2 - h // 2) * LANES)
            mine = (lane // head_size) == (h % 2)
            k_scr[h, :live, half] = jnp.where(mine, keys[:, half], 0.0).astype(BF)
            k_scr[h, :live, other] = bias
            v_scr[h, :live, :LANES] = jnp.where(mine, values[:, half], 0.0).astype(BF)
            v_scr[h, :live, LANES:] = jnp.where(mine, 1.0, 0.0).astype(BF)
        for p in range(2):
            total = None
            for h in (2 * p, 2 * p + 1):
                logits = lax.dot_general(
                    queries[p], k_scr[h, :live, :], NT, preferred_element_type=F32
                )
                top = jnp.max(logits, axis=1, keepdims=True)
                probs = jnp.exp(logits - top).astype(BF)
                part = jnp.dot(probs, v_scr[h, :live, :], preferred_element_type=F32)
                total = part if total is None else total + part
            ctx_scr[:, p * LANES : (p + 1) * LANES] = (
                total[:, :LANES] / total[:, LANES:]
            ).astype(BF)

    blocks = slots // LANES
    for n in range(1, blocks + 1):

        @pl.when(jnp.logical_and(valid <= n * LANES, valid > (n - 1) * LANES))
        def _(n=n):
            attend(n * LANES)

    attended = jnp.dot(ctx_scr[...], wo_ref[...], preferred_element_type=F32).astype(BF)
    hidden = jnp.dot(cand, m1_ref[:width, :], preferred_element_type=F32)
    hidden += jnp.dot(attended, m1_ref[width:, :], preferred_element_type=F32)
    hidden = jnp.maximum(hidden + b1_ref[...], 0.0).astype(BF)
    hidden = jnp.dot(hidden, m2_ref[...], preferred_element_type=F32)
    hidden = jnp.maximum(hidden + b2_ref[...], 0.0).astype(BF)
    weight = jnp.broadcast_to(sp_ref[...].astype(F32), (16, width)).astype(BF)
    score = lax.dot_general(weight, hidden, NT, preferred_element_type=F32)[0:1, :]
    slot = lax.broadcasted_iota(jnp.int32, (1, cands), 1)
    score = jnp.where(slot < count, score, 0.0)
    first = score.astype(BF).astype(F32)
    second = score - first
    row = row_ref[pl.ds(r, 1), :]
    lines = out_ref.shape[0]
    at_line = lax.broadcasted_iota(jnp.int32, (lines, cands), 0) == lax.shift_right_logical(row, 7)
    at_lane = lax.broadcasted_iota(jnp.int32, (LANES, cands), 0) == (row & (LANES - 1))
    at_lane = jnp.where(at_lane, 1.0, 0.0).astype(BF)
    out_ref[...] += lax.dot_general(
        jnp.where(at_line, first, 0.0).astype(BF), at_lane, NT, preferred_element_type=F32
    ) + lax.dot_general(
        jnp.where(at_line, second, 0.0).astype(BF), at_lane, NT, preferred_element_type=F32
    )


def score(plan, per_pair, valid, count, sizes, arrived, candidates, rows, weights, lines):
    reqs, cands, width = candidates.shape
    total_slots = arrived.shape[0]
    slots = total_slots // reqs
    sm = pl.BlockSpec(memory_space=pltpu.SMEM)

    def whole(a):
        return pl.BlockSpec(a.shape, lambda r, n=a.ndim: (0,) * n)

    held = pltpu.VMEM((total_slots + CHUNK, LANES), F32)
    taken = pltpu.VMEM((slots + 2 * CHUNK, LANES), F32)
    return pl.pallas_call(
        functools.partial(score_kernel, per_pair),
        grid=(reqs,),
        out_shape=jax.ShapeDtypeStruct((lines, LANES), F32),
        in_specs=[
            sm,
            sm,
            sm,
            whole(sizes),
            whole(arrived),
            pl.BlockSpec((1, cands, width), lambda r: (r, 0, 0)),
            whole(rows),
        ]
        + [whole(w) for w in weights],
        out_specs=pl.BlockSpec((lines, LANES), lambda r: (0, 0)),
        scratch_shapes=[
            held,
            held,
            held,
            taken,
            taken,
            taken,
            pltpu.VMEM((HEADS, slots, width), BF),
            pltpu.VMEM((HEADS, slots, width), BF),
            pltpu.VMEM((cands, width), BF),
        ],
        compiler_params=pltpu.CompilerParams(vmem_limit_bytes=VMEM_LIMIT),
        name="score",
    )(plan, valid, count, sizes, arrived, candidates, rows, *weights)


def on_device(
    store_rows,
    cluster_logsize,
    cluster_home,
    cluster_ids,
    valid_count,
    candidates,
    cand_count,
    candidate_row,
    query_proj,
    key_proj,
    value_proj,
    out_proj,
    mlp_first,
    bias_first,
    mlp_second,
    bias_second,
    score_proj,
):
    device_count = lax.axis_size(AXES)
    scorer_count = lax.axis_size("scorer")
    rows_dev, width = store_rows.shape
    slot_total = cluster_ids.size
    per_pair = slot_total // device_count
    reqs, cands = candidate_row.shape
    ask, plan = route(
        cluster_ids, valid_count, cluster_home.reshape(-1, LANES), rows_dev, per_pair
    )
    arrived, sizes = exchange(
        ask.reshape(device_count, 1, LANES),
        store_rows,
        cluster_logsize.reshape(-1, LANES),
        device_count // scorer_count,
        scorer_count,
        per_pair,
    )
    arrived = arrived.reshape(slot_total, width)
    sizes = sizes.reshape(device_count, LANES)
    weights = (
        query_proj,
        key_proj,
        value_proj,
        out_proj,
        mlp_first,
        bias_first.reshape(1, -1),
        mlp_second,
        bias_second.reshape(1, -1),
        score_proj.reshape(1, -1),
    )
    lines = scorer_count * (reqs * cands // 2) // LANES
    table = score(
        plan, per_pair, valid_count, cand_count, sizes, arrived, candidates, candidate_row, weights, lines
    )
    return gather_spans(table, scorer_count).reshape(-1)


def solution(mesh):
    split = P(AXES)
    in_specs = (
        P(AXES, None),
        split,
        P(),
        P(AXES, None),
        split,
        P(AXES, None, None),
        split,
        P(AXES, None),
    ) + (P(),) * 9
    return jax.shard_map(
        on_device, mesh=mesh, in_specs=in_specs, out_specs=split, check_vma=False
    )
```

```python
import functools

import jax
import jax.numpy as jnp
from jax import lax
from jax.experimental import pallas as pl
from jax.experimental.pallas import tpu as pltpu
from jax.sharding import PartitionSpec as P

HEADS = 4
CHUNK = 16
AHEAD = 4
TURN = 59
FETCH_FLOPS = 40_000_000_000
SCORE_FLOPS = 30_000_000_000
AXES = ("store", "scorer")
LANES = 128
NT = (((1,), (1,)), ((), ()))
TN = (((0,), (0,)), ((), ()))
BF = jnp.bfloat16
F32 = jnp.float32
VMEM_LIMIT = 48 * 1024 * 1024
MESH = pl.DeviceIdType.MESH


def lane_pick(rows, lane_index):
    return jnp.take_along_axis(rows, lane_index, axis=1)


def column_of(row):
    return jnp.broadcast_to(row, (LANES, LANES)).T


def peer_of(step, pairs, scorers):
    turn = lax.rem(step * TURN, pairs)
    store = jnp.bitwise_xor(lax.axis_index("store"), turn // scorers)
    scorer = jnp.bitwise_xor(lax.axis_index("scorer"), lax.rem(turn, scorers))
    return store, scorer


def fetch_kernel(
    stores,
    scorers,
    per_pair,
    ids_hbm,
    valid_hbm,
    table_hbm,
    store_hbm,
    sizes_hbm,
    rows_out,
    sizes_out,
    plan_ref,
    ids_smem,
    valid_smem,
    ids_ref,
    table_ref,
    store_ref,
    sizes_ref,
    homes,
    ask_ref,
    ask_in,
    ask_smem,
    left_scr,
    right_scr,
    size_scr,
    left,
    right,
    size_stage,
    rows_send,
    sizes_send,
    load_sems,
    ask_sems,
    down_sems,
    send_sems,
    recv_sems,
):
    pairs = stores * scorers
    groups = ask_sems.shape[0]
    group = pairs // groups
    reqs, slots = ids_ref.shape
    per_req = slots // LANES
    rows_dev = store_ref.shape[0]
    shift_rows = rows_dev.bit_length() - 1
    me = lax.axis_index("store") * scorers + lax.axis_index("scorer")
    barrier = pltpu.get_barrier_semaphore()

    loads = [
        pltpu.make_async_copy(src, dst, load_sems.at[n])
        for n, (src, dst) in enumerate(
            (
                (ids_hbm, ids_smem),
                (table_hbm, table_ref),
                (ids_hbm, ids_ref),
                (valid_hbm, valid_smem),
                (store_hbm, store_ref),
                (sizes_hbm, sizes_ref),
            )
        )
    ]
    for load in loads:
        load.start()

    def greet(i, carry):
        pl.semaphore_signal(barrier, inc=1, device_id=peer_of(i, pairs, scorers), device_id_type=MESH)
        return carry

    lax.fori_loop(1, pairs, greet, 0)
    for load in loads:
        load.wait()

    def look(r, carry):
        start = pl.multiple_of(r * slots, slots)
        for u in range(slots):
            c = ids_smem[r, u]
            homes[pl.ds(start + u, 1), :] = table_ref[pl.ds(lax.shift_right_logical(c, 7), 1), :]
        return carry

    lax.fori_loop(0, reqs, look, 0)
    lane = lax.broadcasted_iota(jnp.int32, (LANES, LANES), 1)
    sub = lax.broadcasted_iota(jnp.int32, (LANES, LANES), 0)
    lower = jnp.where(sub >= lane, 1.0, 0.0).astype(BF)
    before = jnp.where(sub < lane, 1.0, 0.0).astype(BF)
    ones = jnp.ones((LANES, LANES), BF)
    base = jnp.zeros((1, LANES), F32)
    acc = jnp.zeros((LANES, 2 * LANES), F32)
    bases = []
    for t in range(reqs * per_req):
        r, q = t // per_req, t % per_req
        if q == 0:
            bases.append(base)
        ids_col = column_of(ids_ref[r : r + 1, q * LANES : (q + 1) * LANES])
        home = lane_pick(homes[t * LANES : (t + 1) * LANES, :], ids_col & (LANES - 1))
        hot = lax.shift_right_logical(home, shift_rows) == lane
        hot = jnp.where(sub + q * LANES < valid_smem[r], jnp.where(hot, 1.0, 0.0), 0.0)
        hot_b = hot.astype(BF)
        incl = jnp.dot(lower, hot_b, preferred_element_type=F32)
        picked = (hot * (incl + (base - 1.0))).astype(BF)
        rank = jnp.dot(picked, ones, preferred_element_type=F32).astype(jnp.int32)
        base = base + incl[LANES - 1 : LANES, :]
        low = (home & 255).astype(F32)
        high = (lax.shift_right_logical(home, 8) & ((rows_dev >> 8) - 1)).astype(F32)
        at = rank == lane
        parts = jnp.concatenate(
            [jnp.where(at, low, 0.0), jnp.where(at, high, 0.0)], axis=1
        ).astype(BF)
        acc = acc + lax.dot_general(hot_b, parts, TN, preferred_element_type=F32)
    bases.append(base)
    ask = (acc[:, :LANES] + 256.0 * acc[:, LANES:]).astype(jnp.int32)
    ask_ref[...] = ask.reshape(pairs, 1, LANES)
    starts = jnp.concatenate(bases[:reqs], axis=0)
    counts = jnp.concatenate(bases[1:], axis=0) - starts
    spots = jnp.dot(counts.astype(BF), before, preferred_element_type=F32)
    source = lax.broadcasted_iota(jnp.int32, (reqs, LANES), 1) * per_pair
    plan_ref[0:reqs, :] = source + starts.astype(jnp.int32)
    plan_ref[reqs : 2 * reqs, :] = spots.astype(jnp.int32)
    plan_ref[2 * reqs : 3 * reqs, :] = counts.astype(jnp.int32)
    most = jnp.max(counts, axis=1, keepdims=True)
    plan_ref[3 * reqs :, :] = jnp.broadcast_to(most, (reqs, LANES)).astype(jnp.int32)

    pl.semaphore_wait(barrier, pairs - 1)

    def ask_group(g, first):
        def one(j, carry):
            i = g * group + j
            store, scorer = peer_of(i, pairs, scorers)
            pltpu.make_async_remote_copy(
                src_ref=ask_ref.at[store * scorers + scorer],
                dst_ref=ask_in.at[i],
                send_sem=send_sems.at[0],
                recv_sem=ask_sems.at[g],
                device_id=(store, scorer),
                device_id_type=MESH,
            ).start()
            return carry

        lax.fori_loop(first, group, one, 0)

    ask_group(0, 1)
    for g in range(1, AHEAD):
        ask_group(g, 0)
    ask_in[0] = ask_ref[me]
    left_scr[...] = store_ref[:, :LANES].astype(F32)
    right_scr[...] = store_ref[:, LANES:].astype(F32)
    offsets = sizes_ref[...].astype(F32)
    for t in range(sizes_ref.shape[0]):
        size_scr[t * LANES : (t + 1) * LANES, :] = column_of(offsets[t : t + 1, :])

    def settle(ref, first, count, sem):
        part = ref.at[pl.ds(first, count)]
        pltpu.make_async_copy(part, part, sem).wait()

    def down(g):
        part = pl.ds(g * group, group)
        return pltpu.make_async_copy(ask_in.at[part], ask_smem.at[part], down_sems.at[g])

    settle(ask_in, 0, group - 1, ask_sems.at[0])
    down(0).start()
    plane = lax.broadcasted_iota(jnp.int32, (per_pair, LANES), 1)
    place = lax.broadcasted_iota(jnp.int32, (per_pair, LANES), 0)
    place = place + lax.rem(me, LANES // per_pair) * per_pair

    def collect(i):
        for j in range(per_pair):
            row = ask_smem[i, 0, j] & (rows_dev - 1)
            left[pl.ds(j, 1), :] = left_scr[pl.ds(row, 1), :]
            right[pl.ds(j, 1), :] = right_scr[pl.ds(row, 1), :]
            size_stage[pl.ds(j, 1), :] = size_scr[pl.ds(row, 1), :]
        sizes = jnp.sum(jnp.where(plane == place, size_stage[...], 0.0), axis=0, keepdims=True)
        return left[...].astype(BF), right[...].astype(BF), sizes

    def answer(i, carry):
        store, scorer = peer_of(i, pairs, scorers)
        rows_send[i, :, :LANES], rows_send[i, :, LANES:], sizes_send[i] = collect(i)
        pltpu.make_async_remote_copy(
            src_ref=rows_send.at[i],
            dst_ref=rows_out.at[me],
            send_sem=send_sems.at[1],
            recv_sem=recv_sems.at[0],
            device_id=(store, scorer),
            device_id_type=MESH,
        ).start()
        pltpu.make_async_remote_copy(
            src_ref=sizes_send.at[i],
            dst_ref=sizes_out.at[me],
            send_sem=send_sems.at[2],
            recv_sem=recv_sems.at[1],
            device_id=(store, scorer),
            device_id_type=MESH,
        ).start()
        return carry

    def serve(g, carry):
        @pl.when(g + AHEAD < groups)
        def _():
            ask_group(g + AHEAD, 0)

        down(g).wait()

        @pl.when(g + 1 < groups)
        def _():
            settle(ask_in, 0, group, ask_sems.at[g + 1])
            down(g + 1).start()

        lax.fori_loop(jnp.where(g == 0, 1, g * group), (g + 1) * group, answer, 0)
        return carry

    lax.fori_loop(0, groups, serve, 0)
    rows_out[me, :, :LANES], rows_out[me, :, LANES:], sizes_out[me] = collect(0)
    settle(ask_in, 0, pairs - 1, send_sems.at[0])
    settle(rows_send, 0, pairs - 1, send_sems.at[1])
    settle(sizes_send, 0, pairs - 1, send_sems.at[2])
    settle(rows_out, 0, pairs - 1, recv_sems.at[0])
    settle(sizes_out, 0, pairs - 1, recv_sems.at[1])


def fetch(ids, valid, table, store_rows, logsize, stores, scorers, per_pair):
    pairs = stores * scorers
    groups = 8
    reqs, slots = ids.shape
    rows_dev, width = store_rows.shape
    vm = pl.BlockSpec(memory_space=pltpu.VMEM)
    hbm = pl.BlockSpec(memory_space=pltpu.HBM)
    column = pltpu.VMEM((rows_dev, LANES), F32)
    part = pltpu.VMEM((per_pair, LANES), F32)
    return pl.pallas_call(
        functools.partial(fetch_kernel, stores, scorers, per_pair),
        out_shape=(
            jax.ShapeDtypeStruct((pairs, per_pair, width), BF),
            jax.ShapeDtypeStruct((pairs, 1, LANES), F32),
            jax.ShapeDtypeStruct((4 * reqs, LANES), jnp.int32),
        ),
        in_specs=[hbm] * 5,
        out_specs=(vm, vm, vm),
        scratch_shapes=[
            pltpu.SMEM(ids.shape, jnp.int32),
            pltpu.SMEM(valid.shape, jnp.int32),
            pltpu.VMEM(ids.shape, jnp.int32),
            pltpu.VMEM(table.shape, jnp.int32),
            pltpu.VMEM(store_rows.shape, BF),
            pltpu.VMEM(logsize.shape, BF),
            pltpu.VMEM((reqs * slots, LANES), jnp.int32),
            pltpu.VMEM((pairs, 1, LANES), jnp.int32),
            pltpu.VMEM((pairs, 1, LANES), jnp.int32),
            pltpu.SMEM((pairs, 1, LANES), jnp.int32),
            column,
            column,
            column,
            part,
            part,
            part,
            pltpu.VMEM((pairs, per_pair, width), BF),
            pltpu.VMEM((pairs, 1, LANES), F32),
            pltpu.SemaphoreType.DMA((6,)),
            pltpu.SemaphoreType.DMA((groups,)),
            pltpu.SemaphoreType.DMA((groups,)),
            pltpu.SemaphoreType.DMA((3,)),
            pltpu.SemaphoreType.DMA((2,)),
        ],
        compiler_params=pltpu.CompilerParams(
            vmem_limit_bytes=VMEM_LIMIT, collective_id=0, has_side_effects=True
        ),
        cost_estimate=pl.CostEstimate(
            flops=FETCH_FLOPS, bytes_accessed=8 * 1024 * 1024, transcendentals=0
        ),
        name="fetch",
    )(ids, valid, table, store_rows, logsize)


def gather_kernel(scorers, table_ref, landed, send_sem, recv_sem):
    store = lax.axis_index("store")
    me = lax.axis_index("scorer")
    barrier = pltpu.get_barrier_semaphore()

    def greet(i, carry):
        pl.semaphore_signal(
            barrier, inc=1, device_id=(store, lax.rem(me + i, scorers)), device_id_type=MESH
        )
        return carry

    lax.fori_loop(1, scorers, greet, 0)
    pl.semaphore_wait(barrier, scorers - 1)

    def send(i, carry):
        to = lax.rem(me + i, scorers)
        pltpu.make_async_remote_copy(
            src_ref=table_ref.at[to],
            dst_ref=landed.at[i],
            send_sem=send_sem,
            recv_sem=recv_sem,
            device_id=(store, to),
            device_id_type=MESH,
        ).start()
        return carry

    lax.fori_loop(1, scorers, send, 0)
    landed[0] = table_ref[me]
    others = landed.at[pl.ds(1, scorers - 1)]
    pltpu.make_async_copy(others, others, send_sem).wait()
    pltpu.make_async_copy(others, others, recv_sem).wait()


def gather_spans(table, scorers):
    lines = table.shape[0] // scorers
    vm = pl.BlockSpec(memory_space=pltpu.VMEM)
    return pl.pallas_call(
        functools.partial(gather_kernel, scorers),
        out_shape=jax.ShapeDtypeStruct((scorers, lines, LANES), F32),
        in_specs=[vm],
        out_specs=vm,
        scratch_shapes=[pltpu.SemaphoreType.DMA, pltpu.SemaphoreType.DMA],
        compiler_params=pltpu.CompilerParams(
            vmem_limit_bytes=4 * 1024 * 1024, collective_id=1, has_side_effects=True
        ),
        name="gather_spans",
    )(table.reshape(scorers, lines, LANES))


def score_kernel(
    per_pair,
    plan_smem,
    sizes_ref,
    arrived_ref,
    cand_ref,
    *rest,
):
    held_in_hbm, out_ref, rest = rest[:12], rest[12], rest[13:]
    local_copies, rest = rest[:12], rest[12:]
    score_body(
        per_pair, plan_smem, sizes_ref, arrived_ref, cand_ref, out_ref, held_in_hbm, local_copies, *rest
    )


def score_body(
    per_pair,
    plan_smem,
    sizes_ref,
    arrived_ref,
    cand_ref,
    out_ref,
    held_in_hbm,
    local_copies,
    left_scr,
    right_scr,
    size_scr,
    x_left,
    x_right,
    x_size,
    k_scr,
    v_scr,
    ctx_scr,
    load_sems,
):
    (
        valid_smem,
        count_smem,
        row_ref,
        wq_ref,
        wk_ref,
        wv_ref,
        wo_ref,
        m1_ref,
        b1_ref,
        m2_ref,
        b2_ref,
        sp_ref,
    ) = local_copies
    r = pl.program_id(0)
    reqs = pl.num_programs(0)
    total_slots, width = arrived_ref.shape
    slots = ctx_scr.shape[0]
    cands = cand_ref.shape[1]
    pairs = sizes_ref.shape[0]
    head_size = width // HEADS
    copies = ((left_scr, x_left), (right_scr, x_right), (size_scr, x_size))

    @pl.when(r == 0)
    def _():
        loads = [
            pltpu.make_async_copy(src, dst, load_sems.at[n])
            for n, (src, dst) in enumerate(zip(held_in_hbm, local_copies))
        ]
        for load in loads:
            load.start()
        left_scr[:total_slots, :] = arrived_ref[:, :LANES].astype(F32)
        right_scr[:total_slots, :] = arrived_ref[:, LANES:].astype(F32)
        group = LANES // per_pair
        one = lax.broadcasted_iota(jnp.int32, (pairs // group, pairs), 1) // group
        one = one == lax.broadcasted_iota(jnp.int32, (pairs // group, pairs), 0)
        packed = jnp.dot(
            jnp.where(one, 1.0, 0.0).astype(BF),
            sizes_ref[...].astype(BF),
            preferred_element_type=F32,
        )
        for t in range(pairs // group):
            size_scr[t * LANES : (t + 1) * LANES, :] = column_of(packed[t : t + 1, :])
        for held, taken in copies:
            held[total_slots:, :] = jnp.zeros((CHUNK, LANES), F32)
            taken[...] = jnp.zeros_like(taken)
        out_ref[...] = jnp.zeros_like(out_ref)
        for load in loads:
            load.wait()

    valid = valid_smem[r]
    count = count_smem[r]

    for s in range(pairs):
        at = plan_smem[r, s]
        to = plan_smem[r + reqs, s]
        for held, taken in copies:
            taken[pl.ds(to, CHUNK), :] = held[pl.ds(at, CHUNK), :]

    @pl.when(plan_smem[r + 3 * reqs, 0] > CHUNK)
    def _():
        def rest(s, carry):
            at = plan_smem[r, s]
            to = plan_smem[r + reqs, s]
            left = plan_smem[r + 2 * reqs, s]
            sub = lax.broadcasted_iota(jnp.int32, (CHUNK, LANES), 0)

            @pl.when(left > CHUNK)
            def _():
                for held, taken in copies:
                    old = taken[pl.ds(to + CHUNK, CHUNK), :]
                    new = held[pl.ds(at + CHUNK, CHUNK), :]
                    taken[pl.ds(to + CHUNK, CHUNK), :] = jnp.where(sub < left - CHUNK, new, old)

            return carry

        lax.fori_loop(0, pairs, rest, 0)

    cand = cand_ref[0]
    query = jnp.dot(cand, wq_ref[...], preferred_element_type=F32)
    clane = lax.broadcasted_iota(jnp.int32, (cands, LANES), 1)
    queries = []
    for p in range(2):
        own = query[:, p * LANES : (p + 1) * LANES].astype(BF)
        other = query[:, (1 - p) * LANES : (2 - p) * LANES]
        other = jnp.where(clane == 0, 1.0, other).astype(BF)
        queries.append(jnp.concatenate([own, other] if p == 0 else [other, own], axis=1))

    def attend(live):
        x = jnp.concatenate([x_left[:live, :], x_right[:live, :]], axis=1).astype(BF)
        keys = jnp.dot(x, wk_ref[...], preferred_element_type=F32).astype(BF).astype(F32) * 0.125
        values = jnp.dot(x, wv_ref[...], preferred_element_type=F32).astype(BF).astype(F32)
        lane = lax.broadcasted_iota(jnp.int32, (live, LANES), 1)
        slot = lax.broadcasted_iota(jnp.int32, (live, LANES), 0)
        bias = jnp.where(slot < valid, x_size[:live, :], -1e30)
        bias = jnp.where(lane == 0, bias, 0.0).astype(BF)
        for h in range(HEADS):
            half = slice((h // 2) * LANES, (h // 2 + 1) * LANES)
            other = slice((1 - h // 2) * LANES, (2 - h // 2) * LANES)
            mine = (lane // head_size) == (h % 2)
            k_scr[h, :live, half] = jnp.where(mine, keys[:, half], 0.0).astype(BF)
            k_scr[h, :live, other] = bias
            v_scr[h, :live, :LANES] = jnp.where(mine, values[:, half], 0.0).astype(BF)
            v_scr[h, :live, LANES:] = jnp.where(mine, 1.0, 0.0).astype(BF)
        for p in range(2):
            total = None
            for h in (2 * p, 2 * p + 1):
                logits = lax.dot_general(
                    queries[p], k_scr[h, :live, :], NT, preferred_element_type=F32
                )
                top = jnp.max(logits, axis=1, keepdims=True)
                probs = jnp.exp(logits - top).astype(BF)
                part = jnp.dot(probs, v_scr[h, :live, :], preferred_element_type=F32)
                total = part if total is None else total + part
            ctx_scr[:, p * LANES : (p + 1) * LANES] = (
                total[:, :LANES] / total[:, LANES:]
            ).astype(BF)

    blocks = slots // LANES
    for n in range(1, blocks + 1):

        @pl.when(jnp.logical_and(valid <= n * LANES, valid > (n - 1) * LANES))
        def _(n=n):
            attend(n * LANES)

    attended = jnp.dot(ctx_scr[...], wo_ref[...], preferred_element_type=F32).astype(BF)
    hidden = jnp.dot(cand, m1_ref[:width, :], preferred_element_type=F32)
    hidden += jnp.dot(attended, m1_ref[width:, :], preferred_element_type=F32)
    hidden = jnp.maximum(hidden + b1_ref[...], 0.0).astype(BF)
    hidden = jnp.dot(hidden, m2_ref[...], preferred_element_type=F32)
    hidden = jnp.maximum(hidden + b2_ref[...], 0.0).astype(BF)
    weight = jnp.broadcast_to(sp_ref[...].astype(F32), (16, width)).astype(BF)
    score = lax.dot_general(weight, hidden, NT, preferred_element_type=F32)[0:1, :]
    slot = lax.broadcasted_iota(jnp.int32, (1, cands), 1)
    score = jnp.where(slot < count, score, 0.0)
    first = score.astype(BF).astype(F32)
    second = score - first
    row = row_ref[pl.ds(r, 1), :]
    lines = out_ref.shape[0]
    at_line = lax.broadcasted_iota(jnp.int32, (lines, cands), 0) == lax.shift_right_logical(row, 7)
    at_lane = lax.broadcasted_iota(jnp.int32, (LANES, cands), 0) == (row & (LANES - 1))
    at_lane = jnp.where(at_lane, 1.0, 0.0).astype(BF)
    out_ref[...] += lax.dot_general(
        jnp.where(at_line, first, 0.0).astype(BF), at_lane, NT, preferred_element_type=F32
    ) + lax.dot_general(
        jnp.where(at_line, second, 0.0).astype(BF), at_lane, NT, preferred_element_type=F32
    )


def score(plan, per_pair, valid, count, sizes, arrived, candidates, rows, weights, lines):
    reqs, cands, width = candidates.shape
    total_slots = arrived.shape[0]
    slots = total_slots // reqs
    sm = pl.BlockSpec(memory_space=pltpu.SMEM)
    hbm = pl.BlockSpec(memory_space=pltpu.HBM)
    loose = (valid, count, rows) + tuple(weights)

    def whole(a):
        return pl.BlockSpec(a.shape, lambda r, n=a.ndim: (0,) * n)

    held = pltpu.VMEM((total_slots + CHUNK, LANES), F32)
    taken = pltpu.VMEM((slots + 2 * CHUNK, LANES), F32)
    return pl.pallas_call(
        functools.partial(score_kernel, per_pair),
        grid=(reqs,),
        out_shape=jax.ShapeDtypeStruct((lines, LANES), F32),
        in_specs=[
            sm,
            whole(sizes),
            whole(arrived),
            pl.BlockSpec((1, cands, width), lambda r: (r, 0, 0)),
        ]
        + [hbm] * len(loose),
        out_specs=pl.BlockSpec((lines, LANES), lambda r: (0, 0)),
        scratch_shapes=[
            pltpu.SMEM(valid.shape, jnp.int32),
            pltpu.SMEM(count.shape, jnp.int32),
        ]
        + [pltpu.VMEM(a.shape, a.dtype) for a in loose[2:]]
        + [
            held,
            held,
            held,
            taken,
            taken,
            taken,
            pltpu.VMEM((HEADS, slots, width), BF),
            pltpu.VMEM((HEADS, slots, width), BF),
            pltpu.VMEM((cands, width), BF),
            pltpu.SemaphoreType.DMA((len(loose),)),
        ],
        compiler_params=pltpu.CompilerParams(vmem_limit_bytes=VMEM_LIMIT),
        cost_estimate=pl.CostEstimate(
            flops=SCORE_FLOPS, bytes_accessed=8 * 1024 * 1024, transcendentals=8 * 1024 * 1024
        ),
        name="score",
    )(plan, sizes, arrived, candidates, *loose)


def on_device(
    store_rows,
    cluster_logsize,
    cluster_home,
    cluster_ids,
    valid_count,
    candidates,
    cand_count,
    candidate_row,
    query_proj,
    key_proj,
    value_proj,
    out_proj,
    mlp_first,
    bias_first,
    mlp_second,
    bias_second,
    score_proj,
):
    device_count = lax.axis_size(AXES)
    scorer_count = lax.axis_size("scorer")
    rows_dev, width = store_rows.shape
    slot_total = cluster_ids.size
    per_pair = slot_total // device_count
    reqs, cands = candidate_row.shape
    arrived, sizes, plan = fetch(
        cluster_ids,
        valid_count,
        cluster_home.reshape(-1, LANES),
        store_rows,
        cluster_logsize.reshape(-1, LANES),
        device_count // scorer_count,
        scorer_count,
        per_pair,
    )
    arrived = arrived.reshape(slot_total, width)
    sizes = sizes.reshape(device_count, LANES)
    weights = (
        query_proj,
        key_proj,
        value_proj,
        out_proj,
        mlp_first,
        bias_first.reshape(1, -1),
        mlp_second,
        bias_second.reshape(1, -1),
        score_proj.reshape(1, -1),
    )
    lines = scorer_count * (reqs * cands // 2) // LANES
    table = score(
        plan, per_pair, valid_count, cand_count, sizes, arrived, candidates, candidate_row, weights, lines
    )
    return jnp.sum(gather_spans(table, scorer_count), axis=0).reshape(-1)


def solution(mesh):
    split = P(AXES)
    in_specs = (
        P(AXES, None),
        split,
        P(),
        P(AXES, None),
        split,
        P(AXES, None, None),
        split,
        P(AXES, None),
    ) + (P(),) * 9
    return jax.shard_map(
        on_device, mesh=mesh, in_specs=in_specs, out_specs=split, check_vma=False
    )
```

```python
import functools

import jax
import jax.numpy as jnp
from jax import lax
from jax.experimental import pallas as pl
from jax.experimental.pallas import tpu as pltpu
from jax.sharding import PartitionSpec as P

HEADS = 4
CHUNK = 16
AHEAD = 4
TURN = 59
FETCH_FLOPS = 40_000_000_000
SCORE_FLOPS = 30_000_000_000
AXES = ("store", "scorer")
LANES = 128
NT = (((1,), (1,)), ((), ()))
TN = (((0,), (0,)), ((), ()))
BF = jnp.bfloat16
F32 = jnp.float32
VMEM_LIMIT = 60 * 1024 * 1024
MESH = pl.DeviceIdType.MESH


def lane_pick(rows, lane_index):
    return jnp.take_along_axis(rows, lane_index, axis=1)


def column_of(row):
    return jnp.broadcast_to(row, (LANES, LANES)).T


def peer_of(step, pairs, scorers):
    turn = lax.rem(step * TURN, pairs)
    store = jnp.bitwise_xor(lax.axis_index("store"), turn // scorers)
    scorer = jnp.bitwise_xor(lax.axis_index("scorer"), lax.rem(turn, scorers))
    return store, scorer


def plan_asks(
    per_pair, rows_dev, ids_smem, valid_smem, ids_ref, table_ref, ask_ref, plan_ref, even, odd, starts
):
    reqs, slots = ids_ref.shape
    shift_rows = rows_dev.bit_length() - 1
    lane = lax.broadcasted_iota(jnp.int32, (LANES, LANES), 1)
    sub = lax.broadcasted_iota(jnp.int32, (LANES, LANES), 0)
    lower = jnp.where(sub >= lane, 1.0, 0.0).astype(BF)
    before = jnp.where(sub < lane, 1.0, 0.0).astype(BF)
    ones = jnp.ones((LANES, LANES), BF)
    wide = lax.broadcasted_iota(jnp.int32, (slots, LANES), 1)

    def look(r, into):
        for u in range(slots):
            c = ids_smem[r, u]
            into[u : u + 1, :] = table_ref[pl.ds(lax.shift_right_logical(c, 7), 1), :]

    def rank(r, held, base, acc):
        starts[pl.ds(r, 1), :] = base
        ids = ids_ref[pl.ds(r, 1), :]
        valid = valid_smem[r]
        homes, hots = [], []
        for t in range(0, slots, LANES):
            home = lane_pick(held[t : t + LANES, :], column_of(ids[:, t : t + LANES]) & (LANES - 1))
            hot = lax.shift_right_logical(home, shift_rows) == lane
            homes.append(home)
            hots.append(jnp.where(sub + t < valid, jnp.where(hot, 1.0, 0.0), 0.0))
        picked = []
        for t in range(0, len(hots), 2):
            two = jnp.concatenate(hots[t : t + 2], axis=1).astype(BF)
            incl = jnp.dot(lower, two, preferred_element_type=F32)
            for n in range(2):
                part = incl[:, n * LANES : (n + 1) * LANES]
                picked.append(hots[t + n] * (part + (base - 1.0)))
                base = base + part[LANES - 1 : LANES, :]
        picked = jnp.concatenate(picked, axis=0).astype(BF)
        place = jnp.dot(picked, ones, preferred_element_type=F32).astype(jnp.int32)
        home = jnp.concatenate(homes, axis=0)
        low = (home & 255).astype(F32)
        high = (lax.shift_right_logical(home, 8) & ((rows_dev >> 8) - 1)).astype(F32)
        at = place == wide
        parts = jnp.concatenate(
            [jnp.where(at, low, 0.0), jnp.where(at, high, 0.0)], axis=1
        ).astype(BF)
        hot = jnp.concatenate(hots, axis=0).astype(BF)
        acc = acc + lax.dot_general(hot, parts, TN, preferred_element_type=F32)
        return base, acc

    look(0, even)

    def both(n, carry):
        base, acc = rank(2 * n, even, *carry)
        look(2 * n + 1, odd)
        base, acc = rank(2 * n + 1, odd, base, acc)
        look(lax.rem(2 * n + 2, reqs), even)
        return base, acc

    base, acc = lax.fori_loop(
        0, reqs // 2, both, (jnp.zeros((1, LANES), F32), jnp.zeros((LANES, 2 * LANES), F32))
    )
    ask = (acc[:, :LANES] + 256.0 * acc[:, LANES:]).astype(jnp.int32)
    ask_ref[...] = ask.reshape(ask_ref.shape)
    first = starts[...]
    counts = jnp.concatenate([first[1:], base], axis=0) - first
    spots = jnp.dot(counts.astype(BF), before, preferred_element_type=F32)
    source = lax.broadcasted_iota(jnp.int32, (reqs, LANES), 1) * per_pair
    plan_ref[0:reqs, :] = source + first.astype(jnp.int32)
    plan_ref[reqs : 2 * reqs, :] = spots.astype(jnp.int32)
    plan_ref[2 * reqs : 3 * reqs, :] = counts.astype(jnp.int32)
    most = jnp.max(counts, axis=1, keepdims=True)
    plan_ref[3 * reqs :, :] = jnp.broadcast_to(most, (reqs, LANES)).astype(jnp.int32)


def fetch_kernel(
    stores,
    scorers,
    per_pair,
    ids_hbm,
    valid_hbm,
    table_hbm,
    store_hbm,
    sizes_hbm,
    rows_out,
    sizes_out,
    plan_hbm,
    plan_ref,
    ids_smem,
    valid_smem,
    ids_ref,
    table_ref,
    store_ref,
    sizes_ref,
    even,
    odd,
    starts,
    ask_ref,
    ask_in,
    ask_smem,
    left_scr,
    right_scr,
    size_scr,
    left,
    right,
    size_stage,
    rows_send,
    sizes_send,
    load_sems,
    ask_sems,
    down_sems,
    send_sems,
    recv_sems,
):
    pairs = stores * scorers
    groups = ask_sems.shape[0]
    group = pairs // groups
    rows_dev = store_ref.shape[0]
    me = lax.axis_index("store") * scorers + lax.axis_index("scorer")
    barrier = pltpu.get_barrier_semaphore()

    loads = [
        pltpu.make_async_copy(src, dst, load_sems.at[n])
        for n, (src, dst) in enumerate(
            (
                (ids_hbm, ids_smem),
                (table_hbm, table_ref),
                (ids_hbm, ids_ref),
                (valid_hbm, valid_smem),
                (store_hbm, store_ref),
                (sizes_hbm, sizes_ref),
            )
        )
    ]
    for load in loads:
        load.start()

    def greet(i, carry):
        pl.semaphore_signal(barrier, inc=1, device_id=peer_of(i, pairs, scorers), device_id_type=MESH)
        return carry

    lax.fori_loop(1, pairs, greet, 0)
    for load in loads:
        load.wait()

    plan_asks(
        per_pair, rows_dev, ids_smem, valid_smem, ids_ref, table_ref, ask_ref, plan_ref, even, odd, starts
    )
    plan_out = pltpu.make_async_copy(plan_ref, plan_hbm, load_sems.at[0])
    plan_out.start()
    pl.semaphore_wait(barrier, pairs - 1)

    def ask_group(g, first):
        def one(j, carry):
            i = g * group + j
            store, scorer = peer_of(i, pairs, scorers)
            pltpu.make_async_remote_copy(
                src_ref=ask_ref.at[store * scorers + scorer],
                dst_ref=ask_in.at[i],
                send_sem=send_sems.at[0],
                recv_sem=ask_sems.at[g],
                device_id=(store, scorer),
                device_id_type=MESH,
            ).start()
            return carry

        lax.fori_loop(first, group, one, 0)

    ask_group(0, 1)
    for g in range(1, AHEAD):
        ask_group(g, 0)
    ask_in[0] = ask_ref[me]
    left_scr[...] = store_ref[:, :LANES].astype(F32)
    right_scr[...] = store_ref[:, LANES:].astype(F32)
    offsets = sizes_ref[...].astype(F32)
    for t in range(sizes_ref.shape[0]):
        size_scr[t * LANES : (t + 1) * LANES, :] = column_of(offsets[t : t + 1, :])

    def settle(ref, first, count, sem):
        part = ref.at[pl.ds(first, count)]
        pltpu.make_async_copy(part, part, sem).wait()

    def down(g):
        part = pl.ds(g * group, group)
        return pltpu.make_async_copy(ask_in.at[part], ask_smem.at[part], down_sems.at[g])

    settle(ask_in, 0, group - 1, ask_sems.at[0])
    down(0).start()
    plane = lax.broadcasted_iota(jnp.int32, (per_pair, LANES), 1)
    place = lax.broadcasted_iota(jnp.int32, (per_pair, LANES), 0)
    place = place + lax.rem(me, LANES // per_pair) * per_pair

    def collect(i):
        for j in range(per_pair):
            row = ask_smem[i, 0, j] & (rows_dev - 1)
            left[pl.ds(j, 1), :] = left_scr[pl.ds(row, 1), :]
            right[pl.ds(j, 1), :] = right_scr[pl.ds(row, 1), :]
            size_stage[pl.ds(j, 1), :] = size_scr[pl.ds(row, 1), :]
        sizes = jnp.sum(jnp.where(plane == place, size_stage[...], 0.0), axis=0, keepdims=True)
        return left[...].astype(BF), right[...].astype(BF), sizes

    def answer(i, carry):
        store, scorer = peer_of(i, pairs, scorers)
        rows_send[i, :, :LANES], rows_send[i, :, LANES:], sizes_send[i] = collect(i)
        pltpu.make_async_remote_copy(
            src_ref=rows_send.at[i],
            dst_ref=rows_out.at[me],
            send_sem=send_sems.at[1],
            recv_sem=recv_sems.at[0],
            device_id=(store, scorer),
            device_id_type=MESH,
        ).start()
        pltpu.make_async_remote_copy(
            src_ref=sizes_send.at[i],
            dst_ref=sizes_out.at[me],
            send_sem=send_sems.at[2],
            recv_sem=recv_sems.at[1],
            device_id=(store, scorer),
            device_id_type=MESH,
        ).start()
        return carry

    def serve(g, carry):
        @pl.when(g + AHEAD < groups)
        def _():
            ask_group(g + AHEAD, 0)

        down(g).wait()

        @pl.when(g + 1 < groups)
        def _():
            settle(ask_in, 0, group, ask_sems.at[g + 1])
            down(g + 1).start()

        lax.fori_loop(jnp.where(g == 0, 1, g * group), (g + 1) * group, answer, 0)
        return carry

    lax.fori_loop(0, groups, serve, 0)
    rows_send[0, :, :LANES], rows_send[0, :, LANES:], sizes_send[0] = collect(0)
    own_rows = pltpu.make_async_copy(rows_send.at[0], rows_out.at[me], load_sems.at[1])
    own_sizes = pltpu.make_async_copy(sizes_send.at[0], sizes_out.at[me], load_sems.at[2])
    own_rows.start()
    own_sizes.start()
    own_rows.wait()
    own_sizes.wait()
    plan_out.wait()
    settle(ask_in, 0, pairs - 1, send_sems.at[0])
    settle(rows_send, 0, pairs - 1, send_sems.at[1])
    settle(sizes_send, 0, pairs - 1, send_sems.at[2])
    settle(rows_out, 0, pairs - 1, recv_sems.at[0])
    settle(sizes_out, 0, pairs - 1, recv_sems.at[1])


def fetch(ids, valid, table, store_rows, logsize, stores, scorers, per_pair):
    pairs = stores * scorers
    groups = 8
    reqs, slots = ids.shape
    rows_dev, width = store_rows.shape
    hbm = pl.BlockSpec(memory_space=pltpu.HBM)
    column = pltpu.VMEM((rows_dev, LANES), F32)
    part = pltpu.VMEM((per_pair, LANES), F32)
    return pl.pallas_call(
        functools.partial(fetch_kernel, stores, scorers, per_pair),
        out_shape=(
            jax.ShapeDtypeStruct((pairs, per_pair, width), BF),
            jax.ShapeDtypeStruct((pairs, 1, LANES), F32),
            jax.ShapeDtypeStruct((4 * reqs, LANES), jnp.int32),
        ),
        in_specs=[hbm] * 5,
        out_specs=(hbm, hbm, hbm),
        scratch_shapes=[
            pltpu.VMEM((4 * reqs, LANES), jnp.int32),
            pltpu.SMEM(ids.shape, jnp.int32),
            pltpu.SMEM(valid.shape, jnp.int32),
            pltpu.VMEM(ids.shape, jnp.int32),
            pltpu.VMEM(table.shape, jnp.int32),
            pltpu.VMEM(store_rows.shape, BF),
            pltpu.VMEM(logsize.shape, BF),
            pltpu.VMEM((slots, LANES), jnp.int32),
            pltpu.VMEM((slots, LANES), jnp.int32),
            pltpu.VMEM((reqs, LANES), F32),
            pltpu.VMEM((pairs, 1, LANES), jnp.int32),
            pltpu.VMEM((pairs, 1, LANES), jnp.int32),
            pltpu.SMEM((pairs, 1, LANES), jnp.int32),
            column,
            column,
            column,
            part,
            part,
            part,
            pltpu.VMEM((pairs, per_pair, width), BF),
            pltpu.VMEM((pairs, 1, LANES), F32),
            pltpu.SemaphoreType.DMA((6,)),
            pltpu.SemaphoreType.DMA((groups,)),
            pltpu.SemaphoreType.DMA((groups,)),
            pltpu.SemaphoreType.DMA((3,)),
            pltpu.SemaphoreType.DMA((2,)),
        ],
        compiler_params=pltpu.CompilerParams(
            vmem_limit_bytes=VMEM_LIMIT, collective_id=0, has_side_effects=True
        ),
        cost_estimate=pl.CostEstimate(
            flops=FETCH_FLOPS, bytes_accessed=8 * 1024 * 1024, transcendentals=0
        ),
        name="fetch",
    )(ids, valid, table, store_rows, logsize)


def gather_kernel(scorers, table_ref, landed, send_sem, recv_sem, own_sem):
    store = lax.axis_index("store")
    me = lax.axis_index("scorer")
    barrier = pltpu.get_barrier_semaphore()

    def greet(i, carry):
        pl.semaphore_signal(
            barrier, inc=1, device_id=(store, lax.rem(me + i, scorers)), device_id_type=MESH
        )
        return carry

    lax.fori_loop(1, scorers, greet, 0)
    pl.semaphore_wait(barrier, scorers - 1)

    def send(i, carry):
        to = lax.rem(me + i, scorers)
        pltpu.make_async_remote_copy(
            src_ref=table_ref.at[to],
            dst_ref=landed.at[i],
            send_sem=send_sem,
            recv_sem=recv_sem,
            device_id=(store, to),
            device_id_type=MESH,
        ).start()
        return carry

    lax.fori_loop(1, scorers, send, 0)
    own = pltpu.make_async_copy(table_ref.at[me], landed.at[0], own_sem)
    own.start()
    own.wait()
    others = landed.at[pl.ds(1, scorers - 1)]
    pltpu.make_async_copy(others, others, send_sem).wait()
    pltpu.make_async_copy(others, others, recv_sem).wait()


def gather_spans(table, scorers):
    lines = table.shape[0] // scorers
    vm = pl.BlockSpec(memory_space=pltpu.VMEM)
    return pl.pallas_call(
        functools.partial(gather_kernel, scorers),
        out_shape=jax.ShapeDtypeStruct((scorers, lines, LANES), F32),
        in_specs=[pl.BlockSpec(memory_space=pltpu.HBM)],
        out_specs=vm,
        scratch_shapes=[pltpu.SemaphoreType.DMA] * 3,
        compiler_params=pltpu.CompilerParams(
            vmem_limit_bytes=VMEM_LIMIT, collective_id=1, has_side_effects=True
        ),
        name="gather_spans",
    )(table.reshape(scorers, lines, LANES))


def score_kernel(
    per_pair,
    cand_ref,
    arrived_hbm,
    *rest,
):
    held_in_hbm, out_ref, rest = rest[:14], rest[14], rest[15:]
    local_copies, rest = rest[:14], rest[14:]
    score_body(per_pair, cand_ref, arrived_hbm, out_ref, held_in_hbm, local_copies, *rest)


def score_body(
    per_pair,
    cand_ref,
    arrived_hbm,
    out_ref,
    held_in_hbm,
    local_copies,
    arrived_ref,
    left_scr,
    right_scr,
    size_scr,
    x_left,
    x_right,
    x_size,
    k_scr,
    v_scr,
    ctx_scr,
    wkt_scr,
    load_sems,
):
    (
        plan_smem,
        sizes_ref,
        valid_smem,
        count_smem,
        row_ref,
        wq_ref,
        wk_ref,
        wv_ref,
        wo_ref,
        m1_ref,
        b1_ref,
        m2_ref,
        b2_ref,
        sp_ref,
    ) = local_copies
    r = pl.program_id(0)
    reqs = pl.num_programs(0)
    total_slots, width = arrived_ref.shape
    slots = ctx_scr.shape[0]
    cands = cand_ref.shape[1]
    pairs = sizes_ref.shape[0]
    head_size = width // HEADS
    copies = ((left_scr, x_left), (right_scr, x_right), (size_scr, x_size))

    @pl.when(r == 0)
    def _():
        loads = [
            pltpu.make_async_copy(src, dst, load_sems.at[n])
            for n, (src, dst) in enumerate(zip(held_in_hbm, local_copies))
        ]
        for load in loads:
            load.start()
        quarter = total_slots // 4
        blocks = [
            pltpu.make_async_copy(
                arrived_hbm.at[pl.ds(n * quarter, quarter)],
                arrived_ref.at[pl.ds(n * quarter, quarter)],
                load_sems.at[len(loads) + n],
            )
            for n in range(4)
        ]
        for block in blocks:
            block.start()
        k_scr[...] = jnp.zeros_like(k_scr)
        ones_lane = lax.broadcasted_iota(jnp.int32, (slots, LANES), 1) // head_size
        for h in range(HEADS):
            v_scr[h, :, LANES:] = jnp.where(ones_lane == h % 2, 1.0, 0.0).astype(BF)
        for held, taken in copies:
            held[total_slots:, :] = jnp.zeros((CHUNK, LANES), F32)
            taken[...] = jnp.zeros_like(taken)
        out_ref[...] = jnp.zeros_like(out_ref)
        for load in loads:
            load.wait()
        wkt_scr[...] = wk_ref[...].astype(F32).T.astype(BF)
        group = LANES // per_pair
        one = lax.broadcasted_iota(jnp.int32, (pairs // group, pairs), 1) // group
        one = one == lax.broadcasted_iota(jnp.int32, (pairs // group, pairs), 0)
        packed = jnp.dot(
            jnp.where(one, 1.0, 0.0).astype(BF),
            sizes_ref[...].astype(BF),
            preferred_element_type=F32,
        )
        for t in range(pairs // group):
            size_scr[t * LANES : (t + 1) * LANES, :] = column_of(packed[t : t + 1, :])
        for n, block in enumerate(blocks):
            block.wait()
            part = slice(n * quarter, (n + 1) * quarter)
            left_scr[part, :] = arrived_ref[part, :LANES].astype(F32)
            right_scr[part, :] = arrived_ref[part, LANES:].astype(F32)

    valid = valid_smem[r]
    count = count_smem[r]

    for s in range(pairs):
        at = plan_smem[r, s]
        to = plan_smem[r + reqs, s]
        for held, taken in copies:
            taken[pl.ds(to, CHUNK), :] = held[pl.ds(at, CHUNK), :]

    @pl.when(plan_smem[r + 3 * reqs, 0] > CHUNK)
    def _():
        def rest(s, carry):
            at = plan_smem[r, s]
            to = plan_smem[r + reqs, s]
            left = plan_smem[r + 2 * reqs, s]
            sub = lax.broadcasted_iota(jnp.int32, (CHUNK, LANES), 0)

            @pl.when(left > CHUNK)
            def _():
                for held, taken in copies:
                    old = taken[pl.ds(to + CHUNK, CHUNK), :]
                    new = held[pl.ds(at + CHUNK, CHUNK), :]
                    taken[pl.ds(to + CHUNK, CHUNK), :] = jnp.where(sub < left - CHUNK, new, old)

            return carry

        lax.fori_loop(0, pairs, rest, 0)

    cand = cand_ref[0]
    query = jnp.dot(cand, wq_ref[...], preferred_element_type=F32)
    clane = lax.broadcasted_iota(jnp.int32, (cands, LANES), 1)
    queries = []
    for p in range(2):
        own = query[:, p * LANES : (p + 1) * LANES].astype(BF)
        other = query[:, (1 - p) * LANES : (2 - p) * LANES]
        other = jnp.where(clane == 0, 1.0, other).astype(BF)
        queries.append(jnp.concatenate([own, other] if p == 0 else [other, own], axis=1))

    def attend(live):
        x = jnp.concatenate([x_left[:live, :], x_right[:live, :]], axis=1).astype(BF)
        keys = lax.dot_general(wkt_scr[...], x, NT, preferred_element_type=F32)
        keys = (keys.astype(BF).astype(F32) * 0.125).astype(BF)
        values = jnp.dot(x, wv_ref[...], preferred_element_type=F32)
        bias = jnp.concatenate(
            [x_size[t : t + LANES, :].T[0:16, :] for t in range(0, live, LANES)], axis=1
        )
        slot = lax.broadcasted_iota(jnp.int32, (16, live), 1)
        sub = lax.broadcasted_iota(jnp.int32, (16, live), 0)
        bias = jnp.where(slot < valid, bias, -1e30)
        bias = jnp.where(sub == 0, bias, 0.0).astype(BF)
        lane = lax.broadcasted_iota(jnp.int32, (live, LANES), 1)
        for h in range(HEADS):
            half = slice((h // 2) * LANES, (h // 2 + 1) * LANES)
            own = slice(h * head_size, (h + 1) * head_size)
            other = (1 - h // 2) * LANES
            mine = (lane // head_size) == (h % 2)
            k_scr[h, own, :live] = keys[own, :]
            k_scr[h, other : other + 16, :live] = bias
            v_scr[h, :live, :LANES] = jnp.where(mine, values[:, half], 0.0).astype(BF)
        for p in range(2):
            total = None
            for h in (2 * p, 2 * p + 1):
                logits = jnp.dot(queries[p], k_scr[h, :, :live], preferred_element_type=F32)
                top = jnp.max(logits, axis=1, keepdims=True)
                probs = jnp.exp(logits - top).astype(BF)
                part = jnp.dot(probs, v_scr[h, :live, :], preferred_element_type=F32)
                total = part if total is None else total + part
            ctx_scr[:, p * LANES : (p + 1) * LANES] = (
                total[:, :LANES] / total[:, LANES:]
            ).astype(BF)

    blocks = slots // LANES
    for n in range(1, blocks + 1):

        @pl.when(jnp.logical_and(valid <= n * LANES, valid > (n - 1) * LANES))
        def _(n=n):
            attend(n * LANES)

    attended = jnp.dot(ctx_scr[...], wo_ref[...], preferred_element_type=F32).astype(BF)
    hidden = jnp.dot(cand, m1_ref[:width, :], preferred_element_type=F32)
    hidden += jnp.dot(attended, m1_ref[width:, :], preferred_element_type=F32)
    hidden = jnp.maximum(hidden + b1_ref[...], 0.0).astype(BF)
    hidden = jnp.dot(hidden, m2_ref[...], preferred_element_type=F32)
    hidden = jnp.maximum(hidden + b2_ref[...], 0.0).astype(BF)
    weight = sp_ref[...].astype(F32)
    weight = jnp.concatenate([weight[n : n + 1, :] for n in range(width // LANES)], axis=1)
    weight = jnp.broadcast_to(weight, (16, width)).astype(BF)
    score = lax.dot_general(weight, hidden, NT, preferred_element_type=F32)[0:1, :]
    slot = lax.broadcasted_iota(jnp.int32, (1, cands), 1)
    score = jnp.where(slot < count, score, 0.0)
    first = score.astype(BF).astype(F32)
    second = score - first
    row = row_ref[pl.ds(r, 1), :]
    lines = out_ref.shape[0]
    at_line = lax.broadcasted_iota(jnp.int32, (lines, cands), 0) == lax.shift_right_logical(row, 7)
    at_lane = lax.broadcasted_iota(jnp.int32, (LANES, cands), 0) == (row & (LANES - 1))
    at_lane = jnp.where(at_lane, 1.0, 0.0).astype(BF)
    out_ref[...] += lax.dot_general(
        jnp.where(at_line, first, 0.0).astype(BF), at_lane, NT, preferred_element_type=F32
    ) + lax.dot_general(
        jnp.where(at_line, second, 0.0).astype(BF), at_lane, NT, preferred_element_type=F32
    )


def score(plan, per_pair, valid, count, sizes, arrived, candidates, rows, weights, lines):
    reqs, cands, width = candidates.shape
    total_slots = arrived.shape[0]
    slots = total_slots // reqs
    hbm = pl.BlockSpec(memory_space=pltpu.HBM)
    loose = (plan, sizes, valid, count, rows) + tuple(weights)
    held = pltpu.VMEM((total_slots + CHUNK, LANES), F32)
    taken = pltpu.VMEM((slots + 2 * CHUNK, LANES), F32)
    return pl.pallas_call(
        functools.partial(score_kernel, per_pair),
        grid=(reqs,),
        out_shape=jax.ShapeDtypeStruct((lines, LANES), F32),
        in_specs=[pl.BlockSpec((1, cands, width), lambda r: (r, 0, 0)), hbm] + [hbm] * len(loose),
        out_specs=pl.BlockSpec((lines, LANES), lambda r: (0, 0)),
        scratch_shapes=[
            pltpu.SMEM(plan.shape, jnp.int32),
            pltpu.VMEM(sizes.shape, F32),
            pltpu.SMEM(valid.shape, jnp.int32),
            pltpu.SMEM(count.shape, jnp.int32),
        ]
        + [pltpu.VMEM(a.shape, a.dtype) for a in loose[4:]]
        + [
            pltpu.VMEM(arrived.shape, BF),
            held,
            held,
            held,
            taken,
            taken,
            taken,
            pltpu.VMEM((HEADS, width, slots), BF),
            pltpu.VMEM((HEADS, slots, width), BF),
            pltpu.VMEM((cands, width), BF),
            pltpu.VMEM((width, width), BF),
            pltpu.SemaphoreType.DMA((len(loose) + 4,)),
        ],
        compiler_params=pltpu.CompilerParams(vmem_limit_bytes=VMEM_LIMIT),
        cost_estimate=pl.CostEstimate(
            flops=SCORE_FLOPS, bytes_accessed=8 * 1024 * 1024, transcendentals=8 * 1024 * 1024
        ),
        name="score",
    )(candidates, arrived, *loose)


def on_device(
    store_rows,
    cluster_logsize,
    cluster_home,
    cluster_ids,
    valid_count,
    candidates,
    cand_count,
    candidate_row,
    query_proj,
    key_proj,
    value_proj,
    out_proj,
    mlp_first,
    bias_first,
    mlp_second,
    bias_second,
    score_proj,
):
    device_count = lax.axis_size(AXES)
    scorer_count = lax.axis_size("scorer")
    rows_dev, width = store_rows.shape
    slot_total = cluster_ids.size
    per_pair = slot_total // device_count
    reqs, cands = candidate_row.shape
    arrived, sizes, plan = fetch(
        cluster_ids,
        valid_count,
        cluster_home.reshape(-1, LANES),
        store_rows,
        cluster_logsize.reshape(-1, LANES),
        device_count // scorer_count,
        scorer_count,
        per_pair,
    )
    arrived = arrived.reshape(slot_total, width)
    sizes = sizes.reshape(device_count, LANES)
    weights = (
        query_proj,
        key_proj,
        value_proj,
        out_proj,
        mlp_first,
        bias_first.reshape(1, -1),
        mlp_second,
        bias_second.reshape(1, -1),
        score_proj.reshape(-1, LANES),
    )
    lines = scorer_count * (reqs * cands // 2) // LANES
    table = score(
        plan, per_pair, valid_count, cand_count, sizes, arrived, candidates, candidate_row, weights, lines
    )
    return jnp.sum(gather_spans(table, scorer_count), axis=0).reshape(-1)


def solution(mesh):
    split = P(AXES)
    in_specs = (
        P(AXES, None),
        split,
        P(),
        P(AXES, None),
        split,
        P(AXES, None, None),
        split,
        P(AXES, None),
    ) + (P(),) * 9
    return jax.shard_map(
        on_device, mesh=mesh, in_specs=in_specs, out_specs=split, check_vma=False
    )
```

```python
import functools

import jax
import jax.numpy as jnp
from jax import lax
from jax.experimental import pallas as pl
from jax.experimental.pallas import tpu as pltpu
from jax.sharding import PartitionSpec as P

HEADS = 4
CHUNK = 16
AHEAD = 4
TURN = 59
FETCH_FLOPS = 40_000_000_000
SCORE_FLOPS = 30_000_000_000
AXES = ("store", "scorer")
LANES = 128
NT = (((1,), (1,)), ((), ()))
TN = (((0,), (0,)), ((), ()))
BF = jnp.bfloat16
F32 = jnp.float32
VMEM_LIMIT = 60 * 1024 * 1024
MESH = pl.DeviceIdType.MESH


def lane_pick(rows, lane_index):
    return jnp.take_along_axis(rows, lane_index, axis=1)


def column_of(row):
    return jnp.broadcast_to(row, (LANES, LANES)).T


def peer_of(step, pairs, scorers):
    turn = lax.rem(step * TURN, pairs)
    store = jnp.bitwise_xor(lax.axis_index("store"), turn // scorers)
    scorer = jnp.bitwise_xor(lax.axis_index("scorer"), lax.rem(turn, scorers))
    return store, scorer


def plan_asks(
    per_pair, rows_dev, lines_smem, valid_smem, ids_ref, table_ref, ask_ref, plan_ref, even, odd, starts
):
    reqs, slots = ids_ref.shape
    shift_rows = rows_dev.bit_length() - 1
    lane = lax.broadcasted_iota(jnp.int32, (LANES, LANES), 1)
    sub = lax.broadcasted_iota(jnp.int32, (LANES, LANES), 0)
    lower = jnp.where(sub >= lane, 1.0, 0.0).astype(BF)
    before = jnp.where(sub < lane, 1.0, 0.0).astype(BF)
    ones = jnp.ones((LANES, LANES), BF)
    wide = lax.broadcasted_iota(jnp.int32, (slots, LANES), 1)

    def look(r, into):
        for u in range(slots):
            c = lines_smem[r, u]
            into[u : u + 1, :] = table_ref[pl.ds(c, 1), :]

    def rank(r, held, base, acc):
        starts[pl.ds(r, 1), :] = base
        ids = ids_ref[pl.ds(r, 1), :]
        valid = valid_smem[r]
        homes, hots = [], []
        for t in range(0, slots, LANES):
            home = lane_pick(held[t : t + LANES, :], column_of(ids[:, t : t + LANES]) & (LANES - 1))
            hot = lax.shift_right_logical(home, shift_rows) == lane
            homes.append(home)
            hots.append(jnp.where(sub + t < valid, jnp.where(hot, 1.0, 0.0), 0.0))
        picked = []
        for t in range(0, len(hots), 2):
            two = jnp.concatenate(hots[t : t + 2], axis=1).astype(BF)
            incl = jnp.dot(lower, two, preferred_element_type=F32)
            for n in range(2):
                part = incl[:, n * LANES : (n + 1) * LANES]
                picked.append(hots[t + n] * (part + (base - 1.0)))
                base = base + part[LANES - 1 : LANES, :]
        picked = jnp.concatenate(picked, axis=0).astype(BF)
        place = jnp.dot(picked, ones, preferred_element_type=F32).astype(jnp.int32)
        home = jnp.concatenate(homes, axis=0)
        low = (home & 255).astype(F32)
        high = (lax.shift_right_logical(home, 8) & ((rows_dev >> 8) - 1)).astype(F32)
        at = place == wide
        parts = jnp.concatenate(
            [jnp.where(at, low, 0.0), jnp.where(at, high, 0.0)], axis=1
        ).astype(BF)
        hot = jnp.concatenate(hots, axis=0).astype(BF)
        acc = acc + lax.dot_general(hot, parts, TN, preferred_element_type=F32)
        return base, acc

    look(0, even)

    def both(n, carry):
        base, acc = rank(2 * n, even, *carry)
        look(2 * n + 1, odd)
        base, acc = rank(2 * n + 1, odd, base, acc)
        look(lax.rem(2 * n + 2, reqs), even)
        return base, acc

    base, acc = lax.fori_loop(
        0, reqs // 2, both, (jnp.zeros((1, LANES), F32), jnp.zeros((LANES, 2 * LANES), F32))
    )
    ask = (acc[:, :LANES] + 256.0 * acc[:, LANES:]).astype(jnp.int32)
    ask_ref[...] = ask.reshape(ask_ref.shape)
    first = starts[...]
    counts = jnp.concatenate([first[1:], base], axis=0) - first
    spots = jnp.dot(counts.astype(BF), before, preferred_element_type=F32)
    source = lax.broadcasted_iota(jnp.int32, (reqs, LANES), 1) * per_pair
    plan_ref[0:reqs, :] = source + first.astype(jnp.int32)
    plan_ref[reqs : 2 * reqs, :] = spots.astype(jnp.int32)
    plan_ref[2 * reqs : 3 * reqs, :] = counts.astype(jnp.int32)
    most = jnp.max(counts, axis=1, keepdims=True)
    plan_ref[3 * reqs :, :] = jnp.broadcast_to(most, (reqs, LANES)).astype(jnp.int32)


def fetch_kernel(
    stores,
    scorers,
    per_pair,
    ids_hbm,
    valid_hbm,
    table_hbm,
    store_hbm,
    sizes_hbm,
    cand_hbm,
    wq_hbm,
    m1_hbm,
    b1_hbm,
    rows_out,
    sizes_out,
    plan_hbm,
    query_hbm,
    hidden_hbm,
    plan_ref,
    lines_smem,
    valid_smem,
    ids_ref,
    lines_ref,
    cand_ref,
    wq_ref,
    m1_ref,
    b1_ref,
    query_scr,
    hidden_scr,
    table_ref,
    store_ref,
    sizes_ref,
    even,
    odd,
    starts,
    ask_ref,
    ask_in,
    ask_smem,
    left_scr,
    right_scr,
    size_scr,
    left,
    right,
    size_stage,
    rows_send,
    sizes_send,
    load_sems,
    ask_sems,
    down_sems,
    send_sems,
    recv_sems,
):
    pairs = stores * scorers
    groups = ask_sems.shape[0]
    group = pairs // groups
    rows_dev = store_ref.shape[0]
    me = lax.axis_index("store") * scorers + lax.axis_index("scorer")
    barrier = pltpu.get_barrier_semaphore()

    loads = [
        pltpu.make_async_copy(src, dst, load_sems.at[n])
        for n, (src, dst) in enumerate(
            (
                (ids_hbm, ids_ref),
                (store_hbm, store_ref),
                (sizes_hbm, sizes_ref),
                (table_hbm, table_ref),
                (valid_hbm, valid_smem),
                (cand_hbm, cand_ref),
                (wq_hbm, wq_ref),
                (m1_hbm.at[pl.ds(0, m1_ref.shape[0])], m1_ref),
                (b1_hbm, b1_ref),
            )
        )
    ]
    for load in loads:
        load.start()

    def greet(i):
        pl.semaphore_signal(barrier, inc=1, device_id=peer_of(i, pairs, scorers), device_id_type=MESH)

    def greet_one(i, carry):
        greet(i)
        return carry

    loads[0].wait()
    lines_ref[...] = lax.shift_right_logical(ids_ref[...], 7)
    lines_load = pltpu.make_async_copy(lines_ref, lines_smem, load_sems.at[0])
    lines_load.start()
    half = pairs // 2
    lax.fori_loop(1, half, greet_one, 0)
    for load in loads[1:5]:
        load.wait()
    portion = rows_dev // half

    def greet_and_widen(i, carry):
        greet(half + i)
        part = pl.ds(pl.multiple_of(i * portion, portion), portion)
        left_scr[part, :] = store_ref[part, :LANES].astype(F32)
        right_scr[part, :] = store_ref[part, LANES:].astype(F32)
        return carry

    lax.fori_loop(0, half, greet_and_widen, 0)
    offsets = sizes_ref[...].astype(F32)
    for t in range(sizes_ref.shape[0]):
        size_scr[t * LANES : (t + 1) * LANES, :] = column_of(offsets[t : t + 1, :])
    lines_load.wait()
    plan_asks(
        per_pair, rows_dev, lines_smem, valid_smem, ids_ref, table_ref, ask_ref, plan_ref, even, odd, starts
    )
    plan_out = pltpu.make_async_copy(plan_ref, plan_hbm, load_sems.at[0])
    plan_out.start()
    pl.semaphore_wait(barrier, pairs - 1)

    def ask_group(g, first):
        def one(j, carry):
            i = g * group + j
            store, scorer = peer_of(i, pairs, scorers)
            pltpu.make_async_remote_copy(
                src_ref=ask_ref.at[store * scorers + scorer],
                dst_ref=ask_in.at[i],
                send_sem=send_sems.at[0],
                recv_sem=ask_sems.at[g],
                device_id=(store, scorer),
                device_id_type=MESH,
            ).start()
            return carry

        lax.fori_loop(first, group, one, 0)

    ask_group(0, 1)
    for g in range(1, AHEAD):
        ask_group(g, 0)
    ask_in[0] = ask_ref[me]

    def settle(ref, first, count, sem):
        part = ref.at[pl.ds(first, count)]
        pltpu.make_async_copy(part, part, sem).wait()

    def down(g):
        part = pl.ds(g * group, group)
        return pltpu.make_async_copy(ask_in.at[part], ask_smem.at[part], down_sems.at[g])

    settle(ask_in, 0, group - 1, ask_sems.at[0])
    down(0).start()
    plane = lax.broadcasted_iota(jnp.int32, (per_pair, LANES), 1)
    place = lax.broadcasted_iota(jnp.int32, (per_pair, LANES), 0)
    place = place + lax.rem(me, LANES // per_pair) * per_pair

    def collect(i):
        for j in range(per_pair):
            row = ask_smem[i, 0, j] & (rows_dev - 1)
            left[pl.ds(j, 1), :] = left_scr[pl.ds(row, 1), :]
            right[pl.ds(j, 1), :] = right_scr[pl.ds(row, 1), :]
            size_stage[pl.ds(j, 1), :] = size_scr[pl.ds(row, 1), :]
        sizes = jnp.sum(jnp.where(plane == place, size_stage[...], 0.0), axis=0, keepdims=True)
        return left[...].astype(BF), right[...].astype(BF), sizes

    def answer(i, carry):
        store, scorer = peer_of(i, pairs, scorers)
        rows_send[i, :, :LANES], rows_send[i, :, LANES:], sizes_send[i] = collect(i)
        pltpu.make_async_remote_copy(
            src_ref=rows_send.at[i],
            dst_ref=rows_out.at[me],
            send_sem=send_sems.at[1],
            recv_sem=recv_sems.at[0],
            device_id=(store, scorer),
            device_id_type=MESH,
        ).start()
        pltpu.make_async_remote_copy(
            src_ref=sizes_send.at[i],
            dst_ref=sizes_out.at[me],
            send_sem=send_sems.at[2],
            recv_sem=recv_sems.at[1],
            device_id=(store, scorer),
            device_id_type=MESH,
        ).start()
        return carry

    def serve(g, carry):
        @pl.when(g + AHEAD < groups)
        def _():
            ask_group(g + AHEAD, 0)

        down(g).wait()

        @pl.when(g + 1 < groups)
        def _():
            settle(ask_in, 0, group, ask_sems.at[g + 1])
            down(g + 1).start()

        lax.fori_loop(jnp.where(g == 0, 1, g * group), (g + 1) * group, answer, 0)
        return carry

    lax.fori_loop(0, groups, serve, 0)
    rows_send[0, :, :LANES], rows_send[0, :, LANES:], sizes_send[0] = collect(0)
    own_rows = pltpu.make_async_copy(rows_send.at[0], rows_out.at[me], load_sems.at[1])
    own_sizes = pltpu.make_async_copy(sizes_send.at[0], sizes_out.at[me], load_sems.at[2])
    own_rows.start()
    own_sizes.start()
    for load in loads[5:]:
        load.wait()

    def project(r, carry):
        cand = cand_ref[r]
        query_scr[r] = jnp.dot(cand, wq_ref[...], preferred_element_type=F32).astype(BF)
        hidden_scr[r] = jnp.dot(cand, m1_ref[...], preferred_element_type=F32) + b1_ref[...]
        pltpu.make_async_copy(query_scr.at[r], query_hbm.at[r], load_sems.at[3]).start()
        pltpu.make_async_copy(hidden_scr.at[r], hidden_hbm.at[r], load_sems.at[4]).start()
        return carry

    lax.fori_loop(0, cand_ref.shape[0], project, 0)
    pltpu.make_async_copy(query_scr, query_hbm, load_sems.at[3]).wait()
    pltpu.make_async_copy(hidden_scr, hidden_hbm, load_sems.at[4]).wait()
    own_rows.wait()
    own_sizes.wait()
    plan_out.wait()
    settle(ask_in, 0, pairs - 1, send_sems.at[0])
    settle(rows_send, 0, pairs - 1, send_sems.at[1])
    settle(sizes_send, 0, pairs - 1, send_sems.at[2])
    settle(rows_out, 0, pairs - 1, recv_sems.at[0])
    settle(sizes_out, 0, pairs - 1, recv_sems.at[1])


def fetch(
    ids, valid, table, store_rows, logsize, candidates, wq, m1, b1, stores, scorers, per_pair
):
    pairs = stores * scorers
    groups = 4
    reqs, slots = ids.shape
    rows_dev, width = store_rows.shape
    hbm = pl.BlockSpec(memory_space=pltpu.HBM)
    column = pltpu.VMEM((rows_dev, LANES), F32)
    part = pltpu.VMEM((per_pair, LANES), F32)
    return pl.pallas_call(
        functools.partial(fetch_kernel, stores, scorers, per_pair),
        out_shape=(
            jax.ShapeDtypeStruct((pairs, per_pair, width), BF),
            jax.ShapeDtypeStruct((pairs, 1, LANES), F32),
            jax.ShapeDtypeStruct((4 * reqs, LANES), jnp.int32),
            jax.ShapeDtypeStruct(candidates.shape, BF),
            jax.ShapeDtypeStruct(candidates.shape[:2] + m1.shape[1:], F32),
        ),
        in_specs=[hbm] * 9,
        out_specs=(hbm,) * 5,
        scratch_shapes=[
            pltpu.VMEM((4 * reqs, LANES), jnp.int32),
            pltpu.SMEM(ids.shape, jnp.int32),
            pltpu.SMEM(valid.shape, jnp.int32),
            pltpu.VMEM(ids.shape, jnp.int32),
            pltpu.VMEM(ids.shape, jnp.int32),
            pltpu.VMEM(candidates.shape, BF),
            pltpu.VMEM(wq.shape, BF),
            pltpu.VMEM((width, m1.shape[1]), BF),
            pltpu.VMEM(b1.shape, F32),
            pltpu.VMEM(candidates.shape, BF),
            pltpu.VMEM(candidates.shape[:2] + m1.shape[1:], F32),
            pltpu.VMEM(table.shape, jnp.int32),
            pltpu.VMEM(store_rows.shape, BF),
            pltpu.VMEM(logsize.shape, BF),
            pltpu.VMEM((slots, LANES), jnp.int32),
            pltpu.VMEM((slots, LANES), jnp.int32),
            pltpu.VMEM((reqs, LANES), F32),
            pltpu.VMEM((pairs, 1, LANES), jnp.int32),
            pltpu.VMEM((pairs, 1, LANES), jnp.int32),
            pltpu.SMEM((pairs, 1, LANES), jnp.int32),
            column,
            column,
            column,
            part,
            part,
            part,
            pltpu.VMEM((pairs, per_pair, width), BF),
            pltpu.VMEM((pairs, 1, LANES), F32),
            pltpu.SemaphoreType.DMA((9,)),
            pltpu.SemaphoreType.DMA((groups,)),
            pltpu.SemaphoreType.DMA((groups,)),
            pltpu.SemaphoreType.DMA((3,)),
            pltpu.SemaphoreType.DMA((2,)),
        ],
        compiler_params=pltpu.CompilerParams(
            vmem_limit_bytes=VMEM_LIMIT, collective_id=0, has_side_effects=True
        ),
        cost_estimate=pl.CostEstimate(
            flops=FETCH_FLOPS, bytes_accessed=8 * 1024 * 1024, transcendentals=0
        ),
        name="fetch",
    )(ids, valid, table, store_rows, logsize, candidates, wq, m1, b1)


def gather_kernel(scorers, table_ref, landed, send_sem, recv_sem, own_sem):
    store = lax.axis_index("store")
    me = lax.axis_index("scorer")
    barrier = pltpu.get_barrier_semaphore()

    def greet(i, carry):
        pl.semaphore_signal(
            barrier, inc=1, device_id=(store, lax.rem(me + i, scorers)), device_id_type=MESH
        )
        return carry

    lax.fori_loop(1, scorers, greet, 0)
    pl.semaphore_wait(barrier, scorers - 1)

    def send(i, carry):
        to = lax.rem(me + i, scorers)
        pltpu.make_async_remote_copy(
            src_ref=table_ref.at[to],
            dst_ref=landed.at[i],
            send_sem=send_sem,
            recv_sem=recv_sem,
            device_id=(store, to),
            device_id_type=MESH,
        ).start()
        return carry

    lax.fori_loop(1, scorers, send, 0)
    own = pltpu.make_async_copy(table_ref.at[me], landed.at[0], own_sem)
    own.start()
    own.wait()
    others = landed.at[pl.ds(1, scorers - 1)]
    pltpu.make_async_copy(others, others, send_sem).wait()
    pltpu.make_async_copy(others, others, recv_sem).wait()


def gather_spans(table, scorers):
    lines = table.shape[0] // scorers
    vm = pl.BlockSpec(memory_space=pltpu.VMEM)
    return pl.pallas_call(
        functools.partial(gather_kernel, scorers),
        out_shape=jax.ShapeDtypeStruct((scorers, lines, LANES), F32),
        in_specs=[pl.BlockSpec(memory_space=pltpu.HBM)],
        out_specs=vm,
        scratch_shapes=[pltpu.SemaphoreType.DMA] * 3,
        compiler_params=pltpu.CompilerParams(
            vmem_limit_bytes=4 * 1024 * 1024, collective_id=1, has_side_effects=True
        ),
        name="gather_spans",
    )(table.reshape(scorers, lines, LANES))


def score_kernel(
    per_pair,
    query_ref,
    hidden_ref,
    arrived_hbm,
    *rest,
):
    held_in_hbm, out_ref, rest = rest[:12], rest[12], rest[13:]
    local_copies, rest = rest[:12], rest[12:]
    score_body(per_pair, query_ref, hidden_ref, arrived_hbm, out_ref, held_in_hbm, local_copies, *rest)


def score_body(
    per_pair,
    query_ref,
    hidden_ref,
    arrived_hbm,
    out_ref,
    held_in_hbm,
    local_copies,
    arrived_ref,
    left_scr,
    right_scr,
    size_scr,
    x_left,
    x_right,
    x_size,
    k_scr,
    v_scr,
    ctx_scr,
    wkt_scr,
    load_sems,
):
    (
        plan_smem,
        sizes_ref,
        valid_smem,
        count_smem,
        row_ref,
        wk_ref,
        wv_ref,
        wo_ref,
        m1_ref,
        m2_ref,
        b2_ref,
        sp_ref,
    ) = local_copies
    r = pl.program_id(0)
    reqs = pl.num_programs(0)
    total_slots, width = arrived_ref.shape
    slots = ctx_scr.shape[0]
    cands = query_ref.shape[1]
    pairs = sizes_ref.shape[0]
    head_size = width // HEADS
    copies = ((left_scr, x_left), (right_scr, x_right), (size_scr, x_size))

    def group_rows(req):
        for s in range(pairs):
            at = plan_smem[req, s]
            to = plan_smem[req + reqs, s]
            for held, taken in copies:
                taken[pl.ds(to, CHUNK), :] = held[pl.ds(at, CHUNK), :]

    @pl.when(r == 0)
    def _():
        loads = [
            pltpu.make_async_copy(src, dst, load_sems.at[n])
            for n, (src, dst) in enumerate(zip(held_in_hbm, local_copies))
        ]
        for load in loads:
            load.start()
        quarter = total_slots // 4
        blocks = [
            pltpu.make_async_copy(
                arrived_hbm.at[pl.ds(n * quarter, quarter)],
                arrived_ref.at[pl.ds(n * quarter, quarter)],
                load_sems.at[len(loads) + n],
            )
            for n in range(4)
        ]
        for block in blocks:
            block.start()
        k_scr[...] = jnp.zeros_like(k_scr)
        ones_lane = lax.broadcasted_iota(jnp.int32, (slots, LANES), 1) // head_size
        for h in range(HEADS):
            v_scr[h, :, LANES:] = jnp.where(ones_lane == h % 2, 1.0, 0.0).astype(BF)
        for held, taken in copies:
            held[total_slots:, :] = jnp.zeros((CHUNK, LANES), F32)
            taken[...] = jnp.zeros_like(taken)
        out_ref[...] = jnp.zeros_like(out_ref)
        for load in loads:
            load.wait()
        wkt_scr[...] = wk_ref[...].astype(F32).T.astype(BF)
        group = LANES // per_pair
        one = lax.broadcasted_iota(jnp.int32, (pairs // group, pairs), 1) // group
        one = one == lax.broadcasted_iota(jnp.int32, (pairs // group, pairs), 0)
        packed = jnp.dot(
            jnp.where(one, 1.0, 0.0).astype(BF),
            sizes_ref[...].astype(BF),
            preferred_element_type=F32,
        )
        for t in range(pairs // group):
            size_scr[t * LANES : (t + 1) * LANES, :] = column_of(packed[t : t + 1, :])
        for n, block in enumerate(blocks):
            block.wait()
            part = slice(n * quarter, (n + 1) * quarter)
            left_scr[part, :] = arrived_ref[part, :LANES].astype(F32)
            right_scr[part, :] = arrived_ref[part, LANES:].astype(F32)
        group_rows(0)

    valid = valid_smem[r]
    count = count_smem[r]

    @pl.when(plan_smem[r + 3 * reqs, 0] > CHUNK)
    def _():
        def rest(s, carry):
            at = plan_smem[r, s]
            to = plan_smem[r + reqs, s]
            left = plan_smem[r + 2 * reqs, s]
            sub = lax.broadcasted_iota(jnp.int32, (CHUNK, LANES), 0)

            @pl.when(left > CHUNK)
            def _():
                for held, taken in copies:
                    old = taken[pl.ds(to + CHUNK, CHUNK), :]
                    new = held[pl.ds(at + CHUNK, CHUNK), :]
                    taken[pl.ds(to + CHUNK, CHUNK), :] = jnp.where(sub < left - CHUNK, new, old)

            return carry

        lax.fori_loop(0, pairs, rest, 0)

    query = query_ref[0]
    clane = lax.broadcasted_iota(jnp.int32, (cands, LANES), 1)
    queries = []
    for p in range(2):
        own = query[:, p * LANES : (p + 1) * LANES]
        other = query[:, (1 - p) * LANES : (2 - p) * LANES].astype(F32)
        other = jnp.where(clane == 0, 1.0, other).astype(BF)
        queries.append(jnp.concatenate([own, other] if p == 0 else [other, own], axis=1))

    def attend(live):
        x = jnp.concatenate([x_left[:live, :], x_right[:live, :]], axis=1).astype(BF)
        keys = lax.dot_general(wkt_scr[...], x, NT, preferred_element_type=F32)
        keys = (keys.astype(BF).astype(F32) * 0.125).astype(BF)
        values = jnp.dot(x, wv_ref[...], preferred_element_type=F32)
        bias = jnp.concatenate(
            [x_size[t : t + LANES, :].T[0:16, :] for t in range(0, live, LANES)], axis=1
        )
        slot = lax.broadcasted_iota(jnp.int32, (16, live), 1)
        sub = lax.broadcasted_iota(jnp.int32, (16, live), 0)
        bias = jnp.where(slot < valid, bias, -1e30)
        bias = jnp.where(sub == 0, bias, 0.0).astype(BF)
        lane = lax.broadcasted_iota(jnp.int32, (live, LANES), 1)
        for h in range(HEADS):
            half = slice((h // 2) * LANES, (h // 2 + 1) * LANES)
            own = slice(h * head_size, (h + 1) * head_size)
            other = (1 - h // 2) * LANES
            mine = (lane // head_size) == (h % 2)
            k_scr[h, own, :live] = keys[own, :]
            k_scr[h, other : other + 16, :live] = bias
            v_scr[h, :live, :LANES] = jnp.where(mine, values[:, half], 0.0).astype(BF)
        for p in range(2):
            total = None
            for h in (2 * p, 2 * p + 1):
                logits = jnp.dot(queries[p], k_scr[h, :, :live], preferred_element_type=F32)
                top = jnp.max(logits, axis=1, keepdims=True)
                probs = jnp.exp(logits - top).astype(BF)
                part = jnp.dot(probs, v_scr[h, :live, :], preferred_element_type=F32)
                total = part if total is None else total + part
            ctx_scr[:, p * LANES : (p + 1) * LANES] = (
                total[:, :LANES] / total[:, LANES:]
            ).astype(BF)

    blocks = slots // LANES
    for n in range(1, blocks + 1):

        @pl.when(jnp.logical_and(valid <= n * LANES, valid > (n - 1) * LANES))
        def _(n=n):
            attend(n * LANES)

    group_rows(jnp.minimum(r + 1, reqs - 1))
    attended = jnp.dot(ctx_scr[...], wo_ref[...], preferred_element_type=F32).astype(BF)
    hidden = hidden_ref[0] + jnp.dot(attended, m1_ref[width:, :], preferred_element_type=F32)
    hidden = jnp.maximum(hidden, 0.0).astype(BF)
    hidden = jnp.dot(hidden, m2_ref[...], preferred_element_type=F32)
    hidden = jnp.maximum(hidden + b2_ref[...], 0.0).astype(BF)
    weight = sp_ref[...].astype(F32)
    weight = jnp.concatenate([weight[n : n + 1, :] for n in range(width // LANES)], axis=1)
    weight = jnp.broadcast_to(weight, (16, width)).astype(BF)
    score = lax.dot_general(weight, hidden, NT, preferred_element_type=F32)[0:1, :]
    slot = lax.broadcasted_iota(jnp.int32, (1, cands), 1)
    score = jnp.where(slot < count, score, 0.0)
    first = score.astype(BF).astype(F32)
    second = score - first
    row = row_ref[pl.ds(r, 1), :]
    lines = out_ref.shape[0]
    at_line = lax.broadcasted_iota(jnp.int32, (lines, cands), 0) == lax.shift_right_logical(row, 7)
    at_lane = lax.broadcasted_iota(jnp.int32, (LANES, cands), 0) == (row & (LANES - 1))
    at_lane = jnp.where(at_lane, 1.0, 0.0).astype(BF)
    out_ref[...] += lax.dot_general(
        jnp.where(at_line, first, 0.0).astype(BF), at_lane, NT, preferred_element_type=F32
    ) + lax.dot_general(
        jnp.where(at_line, second, 0.0).astype(BF), at_lane, NT, preferred_element_type=F32
    )


def score(plan, per_pair, valid, count, sizes, arrived, queries, hidden, rows, weights, lines):
    reqs, cands, width = queries.shape
    total_slots = arrived.shape[0]
    slots = total_slots // reqs
    hbm = pl.BlockSpec(memory_space=pltpu.HBM)
    loose = (plan, sizes, valid, count, rows) + tuple(weights)
    held = pltpu.VMEM((total_slots + CHUNK, LANES), F32)
    taken = pltpu.VMEM((slots + 2 * CHUNK, LANES), F32)
    return pl.pallas_call(
        functools.partial(score_kernel, per_pair),
        grid=(reqs,),
        out_shape=jax.ShapeDtypeStruct((lines, LANES), F32),
        in_specs=[
            pl.BlockSpec((1, cands, width), lambda r: (r, 0, 0)),
            pl.BlockSpec((1,) + hidden.shape[1:], lambda r: (r, 0, 0)),
            hbm,
        ]
        + [hbm] * len(loose),
        out_specs=pl.BlockSpec((lines, LANES), lambda r: (0, 0)),
        scratch_shapes=[
            pltpu.SMEM(plan.shape, jnp.int32),
            pltpu.VMEM(sizes.shape, F32),
            pltpu.SMEM(valid.shape, jnp.int32),
            pltpu.SMEM(count.shape, jnp.int32),
        ]
        + [pltpu.VMEM(a.shape, a.dtype) for a in loose[4:]]
        + [
            pltpu.VMEM(arrived.shape, BF),
            held,
            held,
            held,
            taken,
            taken,
            taken,
            pltpu.VMEM((HEADS, width, slots), BF),
            pltpu.VMEM((HEADS, slots, width), BF),
            pltpu.VMEM((cands, width), BF),
            pltpu.VMEM((width, width), BF),
            pltpu.SemaphoreType.DMA((len(loose) + 4,)),
        ],
        compiler_params=pltpu.CompilerParams(vmem_limit_bytes=VMEM_LIMIT),
        cost_estimate=pl.CostEstimate(
            flops=SCORE_FLOPS, bytes_accessed=8 * 1024 * 1024, transcendentals=8 * 1024 * 1024
        ),
        name="score",
    )(queries, hidden, arrived, *loose)


def on_device(
    store_rows,
    cluster_logsize,
    cluster_home,
    cluster_ids,
    valid_count,
    candidates,
    cand_count,
    candidate_row,
    query_proj,
    key_proj,
    value_proj,
    out_proj,
    mlp_first,
    bias_first,
    mlp_second,
    bias_second,
    score_proj,
):
    device_count = lax.axis_size(AXES)
    scorer_count = lax.axis_size("scorer")
    rows_dev, width = store_rows.shape
    slot_total = cluster_ids.size
    per_pair = slot_total // device_count
    reqs, cands = candidate_row.shape
    arrived, sizes, plan, queries, hidden = fetch(
        cluster_ids,
        valid_count,
        cluster_home.reshape(-1, LANES),
        store_rows,
        cluster_logsize.reshape(-1, LANES),
        candidates,
        query_proj,
        mlp_first,
        bias_first.reshape(1, -1),
        device_count // scorer_count,
        scorer_count,
        per_pair,
    )
    arrived = arrived.reshape(slot_total, width)
    sizes = sizes.reshape(device_count, LANES)
    weights = (
        key_proj,
        value_proj,
        out_proj,
        mlp_first,
        mlp_second,
        bias_second.reshape(1, -1),
        score_proj.reshape(-1, LANES),
    )
    lines = scorer_count * (reqs * cands // 2) // LANES
    table = score(
        plan, per_pair, valid_count, cand_count, sizes, arrived, queries, hidden, candidate_row, weights, lines
    )
    return jnp.sum(gather_spans(table, scorer_count), axis=0).reshape(-1)


def solution(mesh):
    split = P(AXES)
    in_specs = (
        P(AXES, None),
        split,
        P(),
        P(AXES, None),
        split,
        P(AXES, None, None),
        split,
        P(AXES, None),
    ) + (P(),) * 9
    return jax.shard_map(
        on_device, mesh=mesh, in_specs=in_specs, out_specs=split, check_vma=False
    )
```

```python
import functools

import jax
import jax.numpy as jnp
from jax import lax
from jax.experimental import pallas as pl
from jax.experimental.pallas import tpu as pltpu
from jax.sharding import PartitionSpec as P

HEADS = 4
CHUNK = 16
AHEAD = 4
TURN = 59
FETCH_FLOPS = 40_000_000_000
SCORE_FLOPS = 30_000_000_000
AXES = ("store", "scorer")
LANES = 128
NT = (((1,), (1,)), ((), ()))
TN = (((0,), (0,)), ((), ()))
BF = jnp.bfloat16
F32 = jnp.float32
VMEM_LIMIT = 60 * 1024 * 1024
MESH = pl.DeviceIdType.MESH


def lane_pick(rows, lane_index):
    return jnp.take_along_axis(rows, lane_index, axis=1)


def column_of(row):
    return jnp.broadcast_to(row, (LANES, LANES)).T


def peer_of(step, pairs, scorers):
    turn = lax.rem(step * TURN, pairs)
    store = jnp.bitwise_xor(lax.axis_index("store"), turn // scorers)
    scorer = jnp.bitwise_xor(lax.axis_index("scorer"), lax.rem(turn, scorers))
    return store, scorer


def plan_asks(
    per_pair, rows_dev, lines_smem, valid_smem, ids_ref, table_ref, ask_ref, plan_ref, even, odd, starts
):
    reqs, slots = ids_ref.shape
    shift_rows = rows_dev.bit_length() - 1
    lane = lax.broadcasted_iota(jnp.int32, (LANES, LANES), 1)
    sub = lax.broadcasted_iota(jnp.int32, (LANES, LANES), 0)
    lower = jnp.where(sub >= lane, 1.0, 0.0).astype(BF)
    before = jnp.where(sub < lane, 1.0, 0.0).astype(BF)
    ones = jnp.ones((LANES, LANES), BF)
    wide = lax.broadcasted_iota(jnp.int32, (slots, LANES), 1)

    def look(r, into):
        for u in range(slots):
            c = lines_smem[r, u]
            into[u : u + 1, :] = table_ref[pl.ds(c, 1), :]

    def rank(r, held, base, acc):
        starts[pl.ds(r, 1), :] = base
        ids = ids_ref[pl.ds(r, 1), :]
        valid = valid_smem[r]
        homes, hots = [], []
        for t in range(0, slots, LANES):
            home = lane_pick(held[t : t + LANES, :], column_of(ids[:, t : t + LANES]) & (LANES - 1))
            hot = lax.shift_right_logical(home, shift_rows) == lane
            homes.append(home)
            hots.append(jnp.where(sub + t < valid, jnp.where(hot, 1.0, 0.0), 0.0))
        picked = []
        for t in range(0, len(hots), 2):
            two = jnp.concatenate(hots[t : t + 2], axis=1).astype(BF)
            incl = jnp.dot(lower, two, preferred_element_type=F32)
            for n in range(2):
                part = incl[:, n * LANES : (n + 1) * LANES]
                picked.append(hots[t + n] * (part + (base - 1.0)))
                base = base + part[LANES - 1 : LANES, :]
        picked = jnp.concatenate(picked, axis=0).astype(BF)
        place = jnp.dot(picked, ones, preferred_element_type=F32).astype(jnp.int32)
        home = jnp.concatenate(homes, axis=0)
        low = (home & 255).astype(F32)
        high = (lax.shift_right_logical(home, 8) & ((rows_dev >> 8) - 1)).astype(F32)
        at = place == wide
        parts = jnp.concatenate(
            [jnp.where(at, low, 0.0), jnp.where(at, high, 0.0)], axis=1
        ).astype(BF)
        hot = jnp.concatenate(hots, axis=0).astype(BF)
        acc = acc + lax.dot_general(hot, parts, TN, preferred_element_type=F32)
        return base, acc

    look(0, even)

    def both(n, carry):
        base, acc = rank(2 * n, even, *carry)
        look(2 * n + 1, odd)
        base, acc = rank(2 * n + 1, odd, base, acc)
        look(lax.rem(2 * n + 2, reqs), even)
        return base, acc

    base, acc = lax.fori_loop(
        0, reqs // 2, both, (jnp.zeros((1, LANES), F32), jnp.zeros((LANES, 2 * LANES), F32))
    )
    ask = (acc[:, :LANES] + 256.0 * acc[:, LANES:]).astype(jnp.int32)
    ask_ref[...] = ask.reshape(ask_ref.shape)
    first = starts[...]
    counts = jnp.concatenate([first[1:], base], axis=0) - first
    spots = jnp.dot(counts.astype(BF), before, preferred_element_type=F32)
    source = lax.broadcasted_iota(jnp.int32, (reqs, LANES), 1) * per_pair
    plan_ref[0:reqs, :] = source + first.astype(jnp.int32)
    plan_ref[reqs : 2 * reqs, :] = spots.astype(jnp.int32)
    plan_ref[2 * reqs : 3 * reqs, :] = counts.astype(jnp.int32)
    most = jnp.max(counts, axis=1, keepdims=True)
    plan_ref[3 * reqs :, :] = jnp.broadcast_to(most, (reqs, LANES)).astype(jnp.int32)


def fetch_kernel(
    stores,
    scorers,
    per_pair,
    ids_hbm,
    valid_hbm,
    table_hbm,
    store_hbm,
    sizes_hbm,
    cand_hbm,
    wq_hbm,
    m1_hbm,
    b1_hbm,
    rows_out,
    sizes_out,
    plan_hbm,
    query_hbm,
    hidden_hbm,
    plan_ref,
    lines_smem,
    valid_smem,
    ids_ref,
    lines_ref,
    cand_ref,
    wq_ref,
    m1_ref,
    b1_ref,
    query_scr,
    hidden_scr,
    table_ref,
    store_ref,
    sizes_ref,
    even,
    odd,
    starts,
    ask_ref,
    ask_in,
    ask_smem,
    left_scr,
    right_scr,
    size_scr,
    left,
    right,
    size_stage,
    rows_send,
    sizes_send,
    load_sems,
    ask_sems,
    down_sems,
    send_sems,
    recv_sems,
):
    pairs = stores * scorers
    groups = ask_sems.shape[0]
    group = pairs // groups
    rows_dev = store_ref.shape[0]
    me = lax.axis_index("store") * scorers + lax.axis_index("scorer")
    barrier = pltpu.get_barrier_semaphore()

    loads = [
        pltpu.make_async_copy(src, dst, load_sems.at[n])
        for n, (src, dst) in enumerate(
            (
                (ids_hbm, ids_ref),
                (store_hbm, store_ref),
                (sizes_hbm, sizes_ref),
                (table_hbm, table_ref),
                (valid_hbm, valid_smem),
                (cand_hbm, cand_ref),
                (wq_hbm, wq_ref),
                (m1_hbm.at[pl.ds(0, m1_ref.shape[0])], m1_ref),
                (b1_hbm, b1_ref),
            )
        )
    ]
    for load in loads:
        load.start()

    def greet(i):
        pl.semaphore_signal(barrier, inc=1, device_id=peer_of(i, pairs, scorers), device_id_type=MESH)

    def greet_one(i, carry):
        greet(i)
        return carry

    loads[0].wait()
    lines_ref[...] = lax.shift_right_logical(ids_ref[...], 7)
    lines_load = pltpu.make_async_copy(lines_ref, lines_smem, load_sems.at[0])
    lines_load.start()
    half = pairs // 2
    lax.fori_loop(1, half, greet_one, 0)
    for load in loads[1:5]:
        load.wait()
    portion = rows_dev // half

    def greet_and_widen(i, carry):
        greet(half + i)
        part = pl.ds(pl.multiple_of(i * portion, portion), portion)
        left_scr[part, :] = store_ref[part, :LANES].astype(F32)
        right_scr[part, :] = store_ref[part, LANES:].astype(F32)
        return carry

    lax.fori_loop(0, half, greet_and_widen, 0)
    offsets = sizes_ref[...].astype(F32)
    for t in range(sizes_ref.shape[0]):
        size_scr[t * LANES : (t + 1) * LANES, :] = column_of(offsets[t : t + 1, :])
    lines_load.wait()
    plan_asks(
        per_pair, rows_dev, lines_smem, valid_smem, ids_ref, table_ref, ask_ref, plan_ref, even, odd, starts
    )
    plan_out = pltpu.make_async_copy(plan_ref, plan_hbm, load_sems.at[0])
    plan_out.start()
    pl.semaphore_wait(barrier, pairs - 1)

    def ask_group(g, first):
        def one(j, carry):
            i = g * group + j
            store, scorer = peer_of(i, pairs, scorers)
            pltpu.make_async_remote_copy(
                src_ref=ask_ref.at[store * scorers + scorer],
                dst_ref=ask_in.at[i],
                send_sem=send_sems.at[0],
                recv_sem=ask_sems.at[g],
                device_id=(store, scorer),
                device_id_type=MESH,
            ).start()
            return carry

        lax.fori_loop(first, group, one, 0)

    ask_group(0, 1)
    for g in range(1, AHEAD):
        ask_group(g, 0)
    ask_in[0] = ask_ref[me]

    def settle(ref, first, count, sem):
        part = ref.at[pl.ds(first, count)]
        pltpu.make_async_copy(part, part, sem).wait()

    def down(g):
        part = pl.ds(g * group, group)
        return pltpu.make_async_copy(ask_in.at[part], ask_smem.at[part], down_sems.at[g])

    settle(ask_in, 0, group - 1, ask_sems.at[0])
    down(0).start()
    plane = lax.broadcasted_iota(jnp.int32, (per_pair, LANES), 1)
    place = lax.broadcasted_iota(jnp.int32, (per_pair, LANES), 0)
    place = place + lax.rem(me, LANES // per_pair) * per_pair

    def collect(i):
        for j in range(per_pair):
            row = ask_smem[i, 0, j] & (rows_dev - 1)
            left[pl.ds(j, 1), :] = left_scr[pl.ds(row, 1), :]
            right[pl.ds(j, 1), :] = right_scr[pl.ds(row, 1), :]
            size_stage[pl.ds(j, 1), :] = size_scr[pl.ds(row, 1), :]
        sizes = jnp.sum(jnp.where(plane == place, size_stage[...], 0.0), axis=0, keepdims=True)
        return left[...].astype(BF), right[...].astype(BF), sizes

    def answer(i, carry):
        store, scorer = peer_of(i, pairs, scorers)
        rows_send[i, :, :LANES], rows_send[i, :, LANES:], sizes_send[i] = collect(i)
        pltpu.make_async_remote_copy(
            src_ref=rows_send.at[i],
            dst_ref=rows_out.at[me],
            send_sem=send_sems.at[1],
            recv_sem=recv_sems.at[0],
            device_id=(store, scorer),
            device_id_type=MESH,
        ).start()
        pltpu.make_async_remote_copy(
            src_ref=sizes_send.at[i],
            dst_ref=sizes_out.at[me],
            send_sem=send_sems.at[2],
            recv_sem=recv_sems.at[1],
            device_id=(store, scorer),
            device_id_type=MESH,
        ).start()
        return carry

    def serve(g, carry):
        @pl.when(g + AHEAD < groups)
        def _():
            ask_group(g + AHEAD, 0)

        down(g).wait()

        @pl.when(g + 1 < groups)
        def _():
            settle(ask_in, 0, group, ask_sems.at[g + 1])
            down(g + 1).start()

        lax.fori_loop(jnp.where(g == 0, 1, g * group), (g + 1) * group, answer, 0)
        return carry

    lax.fori_loop(0, groups, serve, 0)
    rows_send[0, :, :LANES], rows_send[0, :, LANES:], sizes_send[0] = collect(0)
    own_rows = pltpu.make_async_copy(rows_send.at[0], rows_out.at[me], load_sems.at[1])
    own_sizes = pltpu.make_async_copy(sizes_send.at[0], sizes_out.at[me], load_sems.at[2])
    own_rows.start()
    own_sizes.start()
    for load in loads[5:]:
        load.wait()

    def project(r, carry):
        cand = cand_ref[r]
        query_scr[r] = jnp.dot(cand, wq_ref[...], preferred_element_type=F32).astype(BF)
        hidden_scr[r] = jnp.dot(cand, m1_ref[...], preferred_element_type=F32) + b1_ref[...]
        pltpu.make_async_copy(query_scr.at[r], query_hbm.at[r], load_sems.at[3]).start()
        pltpu.make_async_copy(hidden_scr.at[r], hidden_hbm.at[r], load_sems.at[4]).start()
        return carry

    lax.fori_loop(0, cand_ref.shape[0], project, 0)
    pltpu.make_async_copy(query_scr, query_hbm, load_sems.at[3]).wait()
    pltpu.make_async_copy(hidden_scr, hidden_hbm, load_sems.at[4]).wait()
    own_rows.wait()
    own_sizes.wait()
    plan_out.wait()
    settle(ask_in, 0, pairs - 1, send_sems.at[0])
    settle(rows_send, 0, pairs - 1, send_sems.at[1])
    settle(sizes_send, 0, pairs - 1, send_sems.at[2])
    settle(rows_out, 0, pairs - 1, recv_sems.at[0])
    settle(sizes_out, 0, pairs - 1, recv_sems.at[1])


def fetch(
    ids, valid, table, store_rows, logsize, candidates, wq, m1, b1, stores, scorers, per_pair
):
    pairs = stores * scorers
    groups = 4
    reqs, slots = ids.shape
    rows_dev, width = store_rows.shape
    hbm = pl.BlockSpec(memory_space=pltpu.HBM)
    column = pltpu.VMEM((rows_dev, LANES), F32)
    part = pltpu.VMEM((per_pair, LANES), F32)
    return pl.pallas_call(
        functools.partial(fetch_kernel, stores, scorers, per_pair),
        out_shape=(
            jax.ShapeDtypeStruct((pairs, per_pair, width), BF),
            jax.ShapeDtypeStruct((pairs, 1, LANES), F32),
            jax.ShapeDtypeStruct((4 * reqs, LANES), jnp.int32),
            jax.ShapeDtypeStruct(candidates.shape, BF),
            jax.ShapeDtypeStruct(candidates.shape[:2] + m1.shape[1:], F32),
        ),
        in_specs=[hbm] * 9,
        out_specs=(hbm,) * 5,
        scratch_shapes=[
            pltpu.VMEM((4 * reqs, LANES), jnp.int32),
            pltpu.SMEM(ids.shape, jnp.int32),
            pltpu.SMEM(valid.shape, jnp.int32),
            pltpu.VMEM(ids.shape, jnp.int32),
            pltpu.VMEM(ids.shape, jnp.int32),
            pltpu.VMEM(candidates.shape, BF),
            pltpu.VMEM(wq.shape, BF),
            pltpu.VMEM((width, m1.shape[1]), BF),
            pltpu.VMEM(b1.shape, F32),
            pltpu.VMEM(candidates.shape, BF),
            pltpu.VMEM(candidates.shape[:2] + m1.shape[1:], F32),
            pltpu.VMEM(table.shape, jnp.int32),
            pltpu.VMEM(store_rows.shape, BF),
            pltpu.VMEM(logsize.shape, BF),
            pltpu.VMEM((slots, LANES), jnp.int32),
            pltpu.VMEM((slots, LANES), jnp.int32),
            pltpu.VMEM((reqs, LANES), F32),
            pltpu.VMEM((pairs, 1, LANES), jnp.int32),
            pltpu.VMEM((pairs, 1, LANES), jnp.int32),
            pltpu.SMEM((pairs, 1, LANES), jnp.int32),
            column,
            column,
            column,
            part,
            part,
            part,
            pltpu.VMEM((pairs, per_pair, width), BF),
            pltpu.VMEM((pairs, 1, LANES), F32),
            pltpu.SemaphoreType.DMA((9,)),
            pltpu.SemaphoreType.DMA((groups,)),
            pltpu.SemaphoreType.DMA((groups,)),
            pltpu.SemaphoreType.DMA((3,)),
            pltpu.SemaphoreType.DMA((2,)),
        ],
        compiler_params=pltpu.CompilerParams(
            vmem_limit_bytes=VMEM_LIMIT, collective_id=0, has_side_effects=True
        ),
        cost_estimate=pl.CostEstimate(
            flops=FETCH_FLOPS, bytes_accessed=8 * 1024 * 1024, transcendentals=0
        ),
        name="fetch",
    )(ids, valid, table, store_rows, logsize, candidates, wq, m1, b1)


def gather_kernel(scorers, table_ref, landed, send_sem, recv_sem, own_sem):
    store = lax.axis_index("store")
    me = lax.axis_index("scorer")
    barrier = pltpu.get_barrier_semaphore()

    def greet(i, carry):
        pl.semaphore_signal(
            barrier, inc=1, device_id=(store, lax.rem(me + i, scorers)), device_id_type=MESH
        )
        return carry

    lax.fori_loop(1, scorers, greet, 0)
    pl.semaphore_wait(barrier, scorers - 1)

    def send(i, carry):
        to = lax.rem(me + i, scorers)
        pltpu.make_async_remote_copy(
            src_ref=table_ref.at[to],
            dst_ref=landed.at[i],
            send_sem=send_sem,
            recv_sem=recv_sem,
            device_id=(store, to),
            device_id_type=MESH,
        ).start()
        return carry

    lax.fori_loop(1, scorers, send, 0)
    own = pltpu.make_async_copy(table_ref.at[me], landed.at[0], own_sem)
    own.start()
    own.wait()
    others = landed.at[pl.ds(1, scorers - 1)]
    pltpu.make_async_copy(others, others, send_sem).wait()
    pltpu.make_async_copy(others, others, recv_sem).wait()


def gather_spans(table, scorers):
    lines = table.shape[0] // scorers
    vm = pl.BlockSpec(memory_space=pltpu.VMEM)
    return pl.pallas_call(
        functools.partial(gather_kernel, scorers),
        out_shape=jax.ShapeDtypeStruct((scorers, lines, LANES), F32),
        in_specs=[pl.BlockSpec(memory_space=pltpu.HBM)],
        out_specs=vm,
        scratch_shapes=[pltpu.SemaphoreType.DMA] * 3,
        compiler_params=pltpu.CompilerParams(
            vmem_limit_bytes=4 * 1024 * 1024, collective_id=1, has_side_effects=True
        ),
        name="gather_spans",
    )(table.reshape(scorers, lines, LANES))


def score_kernel(
    per_pair,
    query_ref,
    hidden_ref,
    arrived_hbm,
    *rest,
):
    held_in_hbm, out_ref, rest = rest[:12], rest[12], rest[13:]
    local_copies, rest = rest[:12], rest[12:]
    score_body(per_pair, query_ref, hidden_ref, arrived_hbm, out_ref, held_in_hbm, local_copies, *rest)


def score_body(
    per_pair,
    query_ref,
    hidden_ref,
    arrived_hbm,
    out_ref,
    held_in_hbm,
    local_copies,
    arrived_ref,
    left_scr,
    right_scr,
    size_scr,
    x_left,
    x_right,
    x_size,
    k_scr,
    v_scr,
    ctx_scr,
    wkt_scr,
    load_sems,
):
    (
        plan_smem,
        sizes_ref,
        valid_smem,
        count_smem,
        row_ref,
        wk_ref,
        wv_ref,
        wo_ref,
        m1_ref,
        m2_ref,
        b2_ref,
        sp_ref,
    ) = local_copies
    r = pl.program_id(0)
    reqs = pl.num_programs(0)
    total_slots, width = arrived_ref.shape
    slots = ctx_scr.shape[0]
    cands = query_ref.shape[1]
    pairs = sizes_ref.shape[0]
    head_size = width // HEADS
    copies = ((left_scr, x_left), (right_scr, x_right), (size_scr, x_size))

    def group_rows(req):
        for s in range(pairs):
            at = plan_smem[req, s]
            to = plan_smem[req + reqs, s]
            for held, taken in copies:
                taken[pl.ds(to, CHUNK), :] = held[pl.ds(at, CHUNK), :]

    @pl.when(r == 0)
    def _():
        loads = [
            pltpu.make_async_copy(src, dst, load_sems.at[n])
            for n, (src, dst) in enumerate(zip(held_in_hbm, local_copies))
        ]
        for load in loads:
            load.start()
        quarter = total_slots // 4
        blocks = [
            pltpu.make_async_copy(
                arrived_hbm.at[pl.ds(n * quarter, quarter)],
                arrived_ref.at[pl.ds(n * quarter, quarter)],
                load_sems.at[len(loads) + n],
            )
            for n in range(4)
        ]
        for block in blocks:
            block.start()
        k_scr[...] = jnp.zeros_like(k_scr)
        for held, taken in copies:
            held[total_slots:, :] = jnp.zeros((CHUNK, LANES), F32)
            taken[...] = jnp.zeros_like(taken)
        out_ref[...] = jnp.zeros_like(out_ref)
        for load in loads:
            load.wait()
        wkt_scr[...] = wk_ref[...].astype(F32).T.astype(BF)
        group = LANES // per_pair
        one = lax.broadcasted_iota(jnp.int32, (pairs // group, pairs), 1) // group
        one = one == lax.broadcasted_iota(jnp.int32, (pairs // group, pairs), 0)
        packed = jnp.dot(
            jnp.where(one, 1.0, 0.0).astype(BF),
            sizes_ref[...].astype(BF),
            preferred_element_type=F32,
        )
        for t in range(pairs // group):
            size_scr[t * LANES : (t + 1) * LANES, :] = column_of(packed[t : t + 1, :])
        for n, block in enumerate(blocks):
            block.wait()
            part = slice(n * quarter, (n + 1) * quarter)
            left_scr[part, :] = arrived_ref[part, :LANES].astype(F32)
            right_scr[part, :] = arrived_ref[part, LANES:].astype(F32)
        group_rows(0)

    valid = valid_smem[r]
    count = count_smem[r]

    @pl.when(plan_smem[r + 3 * reqs, 0] > CHUNK)
    def _():
        def rest(s, carry):
            at = plan_smem[r, s]
            to = plan_smem[r + reqs, s]
            left = plan_smem[r + 2 * reqs, s]
            sub = lax.broadcasted_iota(jnp.int32, (CHUNK, LANES), 0)

            @pl.when(left > CHUNK)
            def _():
                for held, taken in copies:
                    old = taken[pl.ds(to + CHUNK, CHUNK), :]
                    new = held[pl.ds(at + CHUNK, CHUNK), :]
                    taken[pl.ds(to + CHUNK, CHUNK), :] = jnp.where(sub < left - CHUNK, new, old)

            return carry

        lax.fori_loop(0, pairs, rest, 0)

    query = query_ref[0]
    clane = lax.broadcasted_iota(jnp.int32, (cands, LANES), 1)
    queries = []
    for p in range(2):
        own = query[:, p * LANES : (p + 1) * LANES]
        other = query[:, (1 - p) * LANES : (2 - p) * LANES].astype(F32)
        other = jnp.where(clane == 0, 1.0, other).astype(BF)
        queries.append(jnp.concatenate([own, other] if p == 0 else [other, own], axis=1))

    def attend(live):
        x = jnp.concatenate([x_left[:live, :], x_right[:live, :]], axis=1).astype(BF)
        keys = lax.dot_general(wkt_scr[...], x, NT, preferred_element_type=F32)
        keys = (keys.astype(BF).astype(F32) * 0.125).astype(BF)
        values = jnp.dot(x, wv_ref[...], preferred_element_type=F32)
        bias = jnp.concatenate(
            [x_size[t : t + LANES, :].T[0:16, :] for t in range(0, live, LANES)], axis=1
        )
        slot = lax.broadcasted_iota(jnp.int32, (16, live), 1)
        sub = lax.broadcasted_iota(jnp.int32, (16, live), 0)
        bias = jnp.where(slot < valid, bias, -1e30)
        bias = jnp.where(sub == 0, bias, 0.0).astype(BF)
        lane = lax.broadcasted_iota(jnp.int32, (live, LANES), 1)
        blank = jnp.zeros((head_size, live), BF)
        for h in range(HEADS):
            p, side = h // 2, h % 2
            half = slice(p * LANES, (p + 1) * LANES)
            own = keys[h * head_size : (h + 1) * head_size, :]
            other = (1 - p) * LANES
            span = slice(side * live, (side + 1) * live)
            mine = (lane // head_size) == side
            k_scr[p, half, span] = jnp.concatenate(
                [own, blank] if side == 0 else [blank, own], axis=0
            )
            k_scr[p, other : other + 16, span] = bias
            v_scr[p, span, :LANES] = jnp.where(mine, values[:, half], 0.0).astype(BF)
            v_scr[p, span, LANES:] = jnp.where(mine, 1.0, 0.0).astype(BF)
        for p in range(2):
            logits = jnp.dot(queries[p], k_scr[p, :, : 2 * live], preferred_element_type=F32)
            probs = []
            for side in range(2):
                part = logits[:, side * live : (side + 1) * live]
                top = jnp.max(part, axis=1, keepdims=True)
                probs.append(jnp.exp(part - top).astype(BF))
            probs = jnp.concatenate(probs, axis=1)
            total = jnp.dot(probs, v_scr[p, : 2 * live, :], preferred_element_type=F32)
            ctx_scr[:, p * LANES : (p + 1) * LANES] = (
                total[:, :LANES] / total[:, LANES:]
            ).astype(BF)

    blocks = slots // LANES
    for n in range(1, blocks + 1):

        @pl.when(jnp.logical_and(count > 0, (valid + LANES - 1) // LANES == n))
        def _(n=n):
            attend(n * LANES)

    following = jnp.minimum(r + 1, reqs - 1)

    @pl.when(count <= 0)
    def _():
        group_rows(following)

    @pl.when(count > 0)
    def _():
        group_rows(following)
        attended = jnp.dot(ctx_scr[...], wo_ref[...], preferred_element_type=F32).astype(BF)
        hidden = hidden_ref[0] + jnp.dot(attended, m1_ref[width:, :], preferred_element_type=F32)
        hidden = jnp.maximum(hidden, 0.0).astype(BF)
        hidden = jnp.dot(hidden, m2_ref[...], preferred_element_type=F32)
        hidden = jnp.maximum(hidden + b2_ref[...], 0.0).astype(BF)
        weight = sp_ref[...].astype(F32)
        weight = jnp.concatenate([weight[n : n + 1, :] for n in range(width // LANES)], axis=1)
        weight = jnp.broadcast_to(weight, (16, width)).astype(BF)
        score = lax.dot_general(weight, hidden, NT, preferred_element_type=F32)[0:1, :]
        slot = lax.broadcasted_iota(jnp.int32, (1, cands), 1)
        score = jnp.where(slot < count, score, 0.0)
        first = score.astype(BF).astype(F32)
        second = score - first
        row = row_ref[pl.ds(r, 1), :]
        lines = out_ref.shape[0]
        at_line = lax.broadcasted_iota(jnp.int32, (lines, cands), 0) == lax.shift_right_logical(row, 7)
        at_lane = lax.broadcasted_iota(jnp.int32, (LANES, cands), 0) == (row & (LANES - 1))
        at_lane = jnp.where(at_lane, 1.0, 0.0).astype(BF)
        out_ref[...] += lax.dot_general(
            jnp.where(at_line, first, 0.0).astype(BF), at_lane, NT, preferred_element_type=F32
        ) + lax.dot_general(
            jnp.where(at_line, second, 0.0).astype(BF), at_lane, NT, preferred_element_type=F32
        )


def score(plan, per_pair, valid, count, sizes, arrived, queries, hidden, rows, weights, lines):
    reqs, cands, width = queries.shape
    total_slots = arrived.shape[0]
    slots = total_slots // reqs
    hbm = pl.BlockSpec(memory_space=pltpu.HBM)
    loose = (plan, sizes, valid, count, rows) + tuple(weights)
    held = pltpu.VMEM((total_slots + CHUNK, LANES), F32)
    taken = pltpu.VMEM((slots + 2 * CHUNK, LANES), F32)
    return pl.pallas_call(
        functools.partial(score_kernel, per_pair),
        grid=(reqs,),
        out_shape=jax.ShapeDtypeStruct((lines, LANES), F32),
        in_specs=[
            pl.BlockSpec((1, cands, width), lambda r: (r, 0, 0)),
            pl.BlockSpec((1,) + hidden.shape[1:], lambda r: (r, 0, 0)),
            hbm,
        ]
        + [hbm] * len(loose),
        out_specs=pl.BlockSpec((lines, LANES), lambda r: (0, 0)),
        scratch_shapes=[
            pltpu.SMEM(plan.shape, jnp.int32),
            pltpu.VMEM(sizes.shape, F32),
            pltpu.SMEM(valid.shape, jnp.int32),
            pltpu.SMEM(count.shape, jnp.int32),
        ]
        + [pltpu.VMEM(a.shape, a.dtype) for a in loose[4:]]
        + [
            pltpu.VMEM(arrived.shape, BF),
            held,
            held,
            held,
            taken,
            taken,
            taken,
            pltpu.VMEM((2, width, 2 * slots), BF),
            pltpu.VMEM((2, 2 * slots, width), BF),
            pltpu.VMEM((cands, width), BF),
            pltpu.VMEM((width, width), BF),
            pltpu.SemaphoreType.DMA((len(loose) + 4,)),
        ],
        compiler_params=pltpu.CompilerParams(vmem_limit_bytes=VMEM_LIMIT),
        cost_estimate=pl.CostEstimate(
            flops=SCORE_FLOPS, bytes_accessed=8 * 1024 * 1024, transcendentals=8 * 1024 * 1024
        ),
        name="score",
    )(queries, hidden, arrived, *loose)


def on_device(
    store_rows,
    cluster_logsize,
    cluster_home,
    cluster_ids,
    valid_count,
    candidates,
    cand_count,
    candidate_row,
    query_proj,
    key_proj,
    value_proj,
    out_proj,
    mlp_first,
    bias_first,
    mlp_second,
    bias_second,
    score_proj,
):
    device_count = lax.axis_size(AXES)
    scorer_count = lax.axis_size("scorer")
    rows_dev, width = store_rows.shape
    slot_total = cluster_ids.size
    per_pair = slot_total // device_count
    reqs, cands = candidate_row.shape
    arrived, sizes, plan, queries, hidden = fetch(
        cluster_ids,
        valid_count,
        cluster_home.reshape(-1, LANES),
        store_rows,
        cluster_logsize.reshape(-1, LANES),
        candidates,
        query_proj,
        mlp_first,
        bias_first.reshape(1, -1),
        device_count // scorer_count,
        scorer_count,
        per_pair,
    )
    arrived = arrived.reshape(slot_total, width)
    sizes = sizes.reshape(device_count, LANES)
    weights = (
        key_proj,
        value_proj,
        out_proj,
        mlp_first,
        mlp_second,
        bias_second.reshape(1, -1),
        score_proj.reshape(-1, LANES),
    )
    lines = scorer_count * (reqs * cands // 2) // LANES
    table = score(
        plan, per_pair, valid_count, cand_count, sizes, arrived, queries, hidden, candidate_row, weights, lines
    )
    return jnp.sum(gather_spans(table, scorer_count), axis=0).reshape(-1)


def solution(mesh):
    split = P(AXES)
    in_specs = (
        P(AXES, None),
        split,
        P(),
        P(AXES, None),
        split,
        P(AXES, None, None),
        split,
        P(AXES, None),
    ) + (P(),) * 9
    return jax.shard_map(
        on_device, mesh=mesh, in_specs=in_specs, out_specs=split, check_vma=False
    )
```

```python
import functools

import jax
import jax.numpy as jnp
from jax import lax
from jax.experimental import pallas as pl
from jax.experimental.pallas import tpu as pltpu
from jax.sharding import PartitionSpec as P

HEADS = 4
CHUNK = 16
AHEAD = 4
TURN = 59
FETCH_FLOPS = 40_000_000_000
SCORE_FLOPS = 30_000_000_000
AXES = ("store", "scorer")
LANES = 128
NT = (((1,), (1,)), ((), ()))
TN = (((0,), (0,)), ((), ()))
BF = jnp.bfloat16
F32 = jnp.float32
VMEM_LIMIT = 60 * 1024 * 1024
MESH = pl.DeviceIdType.MESH


def lane_pick(rows, lane_index):
    return jnp.take_along_axis(rows, lane_index, axis=1)


def column_of(row):
    return jnp.broadcast_to(row, (LANES, LANES)).T


def peer_of(step, pairs, scorers):
    turn = lax.rem(step * TURN, pairs)
    store = jnp.bitwise_xor(lax.axis_index("store"), turn // scorers)
    scorer = jnp.bitwise_xor(lax.axis_index("scorer"), lax.rem(turn, scorers))
    return store, scorer


def plan_asks(
    per_pair, rows_dev, lines_smem, valid_smem, ids_ref, table_ref, ask_ref, plan_ref, even, odd, starts
):
    reqs, slots = ids_ref.shape
    shift_rows = rows_dev.bit_length() - 1
    lane = lax.broadcasted_iota(jnp.int32, (LANES, LANES), 1)
    sub = lax.broadcasted_iota(jnp.int32, (LANES, LANES), 0)
    lower = jnp.where(sub >= lane, 1.0, 0.0).astype(BF)
    before = jnp.where(sub < lane, 1.0, 0.0).astype(BF)
    ones = jnp.ones((LANES, LANES), BF)
    wide = lax.broadcasted_iota(jnp.int32, (slots, LANES), 1)

    def look(r, into):
        for u in range(slots):
            c = lines_smem[r, u]
            into[u : u + 1, :] = table_ref[pl.ds(c, 1), :]

    def rank(r, held, base, acc):
        starts[pl.ds(r, 1), :] = base
        ids = ids_ref[pl.ds(r, 1), :]
        valid = valid_smem[r]
        homes, hots = [], []
        for t in range(0, slots, LANES):
            home = lane_pick(held[t : t + LANES, :], column_of(ids[:, t : t + LANES]) & (LANES - 1))
            hot = lax.shift_right_logical(home, shift_rows) == lane
            homes.append(home)
            hots.append(jnp.where(sub + t < valid, jnp.where(hot, 1.0, 0.0), 0.0))
        picked = []
        for t in range(0, len(hots), 2):
            two = jnp.concatenate(hots[t : t + 2], axis=1).astype(BF)
            incl = jnp.dot(lower, two, preferred_element_type=F32)
            for n in range(2):
                part = incl[:, n * LANES : (n + 1) * LANES]
                picked.append(hots[t + n] * (part + (base - 1.0)))
                base = base + part[LANES - 1 : LANES, :]
        picked = jnp.concatenate(picked, axis=0).astype(BF)
        place = jnp.dot(picked, ones, preferred_element_type=F32).astype(jnp.int32)
        home = jnp.concatenate(homes, axis=0)
        low = (home & 255).astype(F32)
        high = (lax.shift_right_logical(home, 8) & ((rows_dev >> 8) - 1)).astype(F32)
        at = place == wide
        parts = jnp.concatenate(
            [jnp.where(at, low, 0.0), jnp.where(at, high, 0.0)], axis=1
        ).astype(BF)
        hot = jnp.concatenate(hots, axis=0).astype(BF)
        acc = acc + lax.dot_general(hot, parts, TN, preferred_element_type=F32)
        return base, acc

    look(0, even)

    def both(n, carry):
        base, acc = rank(2 * n, even, *carry)
        look(2 * n + 1, odd)
        base, acc = rank(2 * n + 1, odd, base, acc)
        look(lax.rem(2 * n + 2, reqs), even)
        return base, acc

    base, acc = lax.fori_loop(
        0, reqs // 2, both, (jnp.zeros((1, LANES), F32), jnp.zeros((LANES, 2 * LANES), F32))
    )
    ask = (acc[:, :LANES] + 256.0 * acc[:, LANES:]).astype(jnp.int32)
    ask_ref[...] = ask.reshape(ask_ref.shape)
    first = starts[...]
    counts = jnp.concatenate([first[1:], base], axis=0) - first
    spots = jnp.dot(counts.astype(BF), before, preferred_element_type=F32)
    source = lax.broadcasted_iota(jnp.int32, (reqs, LANES), 1) * per_pair
    plan_ref[0:reqs, :] = source + first.astype(jnp.int32)
    plan_ref[reqs : 2 * reqs, :] = spots.astype(jnp.int32)
    plan_ref[2 * reqs : 3 * reqs, :] = counts.astype(jnp.int32)
    most = jnp.max(counts, axis=1, keepdims=True)
    plan_ref[3 * reqs :, :] = jnp.broadcast_to(most, (reqs, LANES)).astype(jnp.int32)


def fetch_kernel(
    stores,
    scorers,
    per_pair,
    ids_hbm,
    valid_hbm,
    table_hbm,
    store_hbm,
    sizes_hbm,
    cand_hbm,
    wq_hbm,
    m1_hbm,
    b1_hbm,
    rows_out,
    sizes_out,
    plan_hbm,
    query_hbm,
    hidden_hbm,
    plan_ref,
    lines_smem,
    valid_smem,
    ids_ref,
    lines_ref,
    cand_ref,
    wq_ref,
    m1_ref,
    b1_ref,
    query_scr,
    hidden_scr,
    table_ref,
    store_ref,
    sizes_ref,
    even,
    odd,
    starts,
    ask_ref,
    ask_in,
    ask_smem,
    left_scr,
    right_scr,
    size_scr,
    left,
    right,
    size_stage,
    rows_send,
    sizes_send,
    load_sems,
    ask_sems,
    down_sems,
    send_sems,
    recv_sems,
):
    pairs = stores * scorers
    groups = ask_sems.shape[0]
    group = pairs // groups
    rows_dev = store_ref.shape[0]
    me = lax.axis_index("store") * scorers + lax.axis_index("scorer")
    barrier = pltpu.get_barrier_semaphore()

    loads = [
        pltpu.make_async_copy(src, dst, load_sems.at[n])
        for n, (src, dst) in enumerate(
            (
                (ids_hbm, ids_ref),
                (store_hbm, store_ref),
                (sizes_hbm, sizes_ref),
                (table_hbm, table_ref),
                (valid_hbm, valid_smem),
                (cand_hbm, cand_ref),
                (wq_hbm, wq_ref),
                (m1_hbm.at[pl.ds(0, m1_ref.shape[0])], m1_ref),
                (b1_hbm, b1_ref),
            )
        )
    ]
    for load in loads:
        load.start()

    def greet(i):
        pl.semaphore_signal(barrier, inc=1, device_id=peer_of(i, pairs, scorers), device_id_type=MESH)

    def greet_one(i, carry):
        greet(i)
        return carry

    loads[0].wait()
    lines_ref[...] = lax.shift_right_logical(ids_ref[...], 7)
    lines_load = pltpu.make_async_copy(lines_ref, lines_smem, load_sems.at[0])
    lines_load.start()
    half = pairs // 2
    lax.fori_loop(1, half, greet_one, 0)
    for load in loads[1:5]:
        load.wait()
    portion = rows_dev // half

    def greet_and_widen(i, carry):
        greet(half + i)
        part = pl.ds(pl.multiple_of(i * portion, portion), portion)
        left_scr[part, :] = store_ref[part, :LANES].astype(F32)
        right_scr[part, :] = store_ref[part, LANES:].astype(F32)
        return carry

    lax.fori_loop(0, half, greet_and_widen, 0)
    offsets = sizes_ref[...].astype(F32)
    for t in range(sizes_ref.shape[0]):
        size_scr[t * LANES : (t + 1) * LANES, :] = column_of(offsets[t : t + 1, :])
    lines_load.wait()
    plan_asks(
        per_pair, rows_dev, lines_smem, valid_smem, ids_ref, table_ref, ask_ref, plan_ref, even, odd, starts
    )
    plan_out = pltpu.make_async_copy(plan_ref, plan_hbm, load_sems.at[0])
    plan_out.start()
    pl.semaphore_wait(barrier, pairs - 1)

    def ask_group(g, first):
        def one(j, carry):
            i = g * group + j
            store, scorer = peer_of(i, pairs, scorers)
            pltpu.make_async_remote_copy(
                src_ref=ask_ref.at[store * scorers + scorer],
                dst_ref=ask_in.at[i],
                send_sem=send_sems.at[0],
                recv_sem=ask_sems.at[g],
                device_id=(store, scorer),
                device_id_type=MESH,
            ).start()
            return carry

        lax.fori_loop(first, group, one, 0)

    ask_group(0, 1)
    for g in range(1, AHEAD):
        ask_group(g, 0)
    ask_in[0] = ask_ref[me]

    def settle(ref, first, count, sem):
        part = ref.at[pl.ds(first, count)]
        pltpu.make_async_copy(part, part, sem).wait()

    def down(g):
        part = pl.ds(g * group, group)
        return pltpu.make_async_copy(ask_in.at[part], ask_smem.at[part], down_sems.at[g])

    settle(ask_in, 0, group - 1, ask_sems.at[0])
    down(0).start()
    plane = lax.broadcasted_iota(jnp.int32, (per_pair, LANES), 1)
    place = lax.broadcasted_iota(jnp.int32, (per_pair, LANES), 0)
    place = place + lax.rem(me, LANES // per_pair) * per_pair

    def collect(i):
        for j in range(per_pair):
            row = ask_smem[i, 0, j] & (rows_dev - 1)
            left[pl.ds(j, 1), :] = left_scr[pl.ds(row, 1), :]
            right[pl.ds(j, 1), :] = right_scr[pl.ds(row, 1), :]
            size_stage[pl.ds(j, 1), :] = size_scr[pl.ds(row, 1), :]
        sizes = jnp.sum(jnp.where(plane == place, size_stage[...], 0.0), axis=0, keepdims=True)
        return left[...].astype(BF), right[...].astype(BF), sizes

    def answer(i, carry):
        store, scorer = peer_of(i, pairs, scorers)
        rows_send[i, :, :LANES], rows_send[i, :, LANES:], sizes_send[i] = collect(i)
        pltpu.make_async_remote_copy(
            src_ref=rows_send.at[i],
            dst_ref=rows_out.at[me],
            send_sem=send_sems.at[1],
            recv_sem=recv_sems.at[0],
            device_id=(store, scorer),
            device_id_type=MESH,
        ).start()
        pltpu.make_async_remote_copy(
            src_ref=sizes_send.at[i],
            dst_ref=sizes_out.at[me],
            send_sem=send_sems.at[2],
            recv_sem=recv_sems.at[1],
            device_id=(store, scorer),
            device_id_type=MESH,
        ).start()
        return carry

    def serve(g, carry):
        @pl.when(g + AHEAD < groups)
        def _():
            ask_group(g + AHEAD, 0)

        down(g).wait()

        @pl.when(g + 1 < groups)
        def _():
            settle(ask_in, 0, group, ask_sems.at[g + 1])
            down(g + 1).start()

        lax.fori_loop(jnp.where(g == 0, 1, g * group), (g + 1) * group, answer, 0)
        return carry

    lax.fori_loop(0, groups, serve, 0)
    rows_send[0, :, :LANES], rows_send[0, :, LANES:], sizes_send[0] = collect(0)
    own_rows = pltpu.make_async_copy(rows_send.at[0], rows_out.at[me], load_sems.at[1])
    own_sizes = pltpu.make_async_copy(sizes_send.at[0], sizes_out.at[me], load_sems.at[2])
    own_rows.start()
    own_sizes.start()
    for load in loads[5:]:
        load.wait()

    def project(r, carry):
        cand = cand_ref[r]
        query_scr[r] = jnp.dot(cand, wq_ref[...], preferred_element_type=F32).astype(BF)
        hidden_scr[r] = jnp.dot(cand, m1_ref[...], preferred_element_type=F32) + b1_ref[...]
        pltpu.make_async_copy(query_scr.at[r], query_hbm.at[r], load_sems.at[3]).start()
        pltpu.make_async_copy(hidden_scr.at[r], hidden_hbm.at[r], load_sems.at[4]).start()
        return carry

    lax.fori_loop(0, cand_ref.shape[0], project, 0)
    pltpu.make_async_copy(query_scr, query_hbm, load_sems.at[3]).wait()
    pltpu.make_async_copy(hidden_scr, hidden_hbm, load_sems.at[4]).wait()
    own_rows.wait()
    own_sizes.wait()
    plan_out.wait()
    settle(ask_in, 0, pairs - 1, send_sems.at[0])
    settle(rows_send, 0, pairs - 1, send_sems.at[1])
    settle(sizes_send, 0, pairs - 1, send_sems.at[2])
    settle(rows_out, 0, pairs - 1, recv_sems.at[0])
    settle(sizes_out, 0, pairs - 1, recv_sems.at[1])


def fetch(
    ids, valid, table, store_rows, logsize, candidates, wq, m1, b1, stores, scorers, per_pair
):
    pairs = stores * scorers
    groups = 4
    reqs, slots = ids.shape
    rows_dev, width = store_rows.shape
    hbm = pl.BlockSpec(memory_space=pltpu.HBM)
    column = pltpu.VMEM((rows_dev, LANES), F32)
    part = pltpu.VMEM((per_pair, LANES), F32)
    return pl.pallas_call(
        functools.partial(fetch_kernel, stores, scorers, per_pair),
        out_shape=(
            jax.ShapeDtypeStruct((pairs, per_pair, width), BF),
            jax.ShapeDtypeStruct((pairs, 1, LANES), F32),
            jax.ShapeDtypeStruct((4 * reqs, LANES), jnp.int32),
            jax.ShapeDtypeStruct(candidates.shape, BF),
            jax.ShapeDtypeStruct(candidates.shape[:2] + m1.shape[1:], F32),
        ),
        in_specs=[hbm] * 9,
        out_specs=(hbm,) * 5,
        scratch_shapes=[
            pltpu.VMEM((4 * reqs, LANES), jnp.int32),
            pltpu.SMEM(ids.shape, jnp.int32),
            pltpu.SMEM(valid.shape, jnp.int32),
            pltpu.VMEM(ids.shape, jnp.int32),
            pltpu.VMEM(ids.shape, jnp.int32),
            pltpu.VMEM(candidates.shape, BF),
            pltpu.VMEM(wq.shape, BF),
            pltpu.VMEM((width, m1.shape[1]), BF),
            pltpu.VMEM(b1.shape, F32),
            pltpu.VMEM(candidates.shape, BF),
            pltpu.VMEM(candidates.shape[:2] + m1.shape[1:], F32),
            pltpu.VMEM(table.shape, jnp.int32),
            pltpu.VMEM(store_rows.shape, BF),
            pltpu.VMEM(logsize.shape, BF),
            pltpu.VMEM((slots, LANES), jnp.int32),
            pltpu.VMEM((slots, LANES), jnp.int32),
            pltpu.VMEM((reqs, LANES), F32),
            pltpu.VMEM((pairs, 1, LANES), jnp.int32),
            pltpu.VMEM((pairs, 1, LANES), jnp.int32),
            pltpu.SMEM((pairs, 1, LANES), jnp.int32),
            column,
            column,
            column,
            part,
            part,
            part,
            pltpu.VMEM((pairs, per_pair, width), BF),
            pltpu.VMEM((pairs, 1, LANES), F32),
            pltpu.SemaphoreType.DMA((9,)),
            pltpu.SemaphoreType.DMA((groups,)),
            pltpu.SemaphoreType.DMA((groups,)),
            pltpu.SemaphoreType.DMA((3,)),
            pltpu.SemaphoreType.DMA((2,)),
        ],
        compiler_params=pltpu.CompilerParams(
            vmem_limit_bytes=VMEM_LIMIT, collective_id=0, has_side_effects=True
        ),
        cost_estimate=pl.CostEstimate(
            flops=FETCH_FLOPS, bytes_accessed=8 * 1024 * 1024, transcendentals=0
        ),
        name="fetch",
    )(ids, valid, table, store_rows, logsize, candidates, wq, m1, b1)


def gather_kernel(scorers, table_ref, landed, send_sem, recv_sem, own_sem):
    store = lax.axis_index("store")
    me = lax.axis_index("scorer")
    barrier = pltpu.get_barrier_semaphore()

    def greet(i, carry):
        pl.semaphore_signal(
            barrier, inc=1, device_id=(store, lax.rem(me + i, scorers)), device_id_type=MESH
        )
        return carry

    lax.fori_loop(1, scorers, greet, 0)
    pl.semaphore_wait(barrier, scorers - 1)

    def send(i, carry):
        to = lax.rem(me + i, scorers)
        pltpu.make_async_remote_copy(
            src_ref=table_ref.at[to],
            dst_ref=landed.at[i],
            send_sem=send_sem,
            recv_sem=recv_sem,
            device_id=(store, to),
            device_id_type=MESH,
        ).start()
        return carry

    lax.fori_loop(1, scorers, send, 0)
    own = pltpu.make_async_copy(table_ref.at[me], landed.at[0], own_sem)
    own.start()
    own.wait()
    others = landed.at[pl.ds(1, scorers - 1)]
    pltpu.make_async_copy(others, others, send_sem).wait()
    pltpu.make_async_copy(others, others, recv_sem).wait()


def gather_spans(table, scorers):
    lines = table.shape[0] // scorers
    vm = pl.BlockSpec(memory_space=pltpu.VMEM)
    return pl.pallas_call(
        functools.partial(gather_kernel, scorers),
        out_shape=jax.ShapeDtypeStruct((scorers, lines, LANES), F32),
        in_specs=[pl.BlockSpec(memory_space=pltpu.HBM)],
        out_specs=vm,
        scratch_shapes=[pltpu.SemaphoreType.DMA] * 3,
        compiler_params=pltpu.CompilerParams(
            vmem_limit_bytes=4 * 1024 * 1024, collective_id=1, has_side_effects=True
        ),
        name="gather_spans",
    )(table.reshape(scorers, lines, LANES))


def score_kernel(
    per_pair,
    query_hbm,
    hidden_hbm,
    arrived_hbm,
    *rest,
):
    held_in_hbm, out_ref, rest = rest[:12], rest[12], rest[13:]
    local_copies, rest = rest[:12], rest[12:]
    score_body(per_pair, query_hbm, hidden_hbm, arrived_hbm, out_ref, held_in_hbm, local_copies, *rest)


def score_body(
    per_pair,
    query_hbm,
    hidden_hbm,
    arrived_hbm,
    out_ref,
    held_in_hbm,
    local_copies,
    arrived_ref,
    left_scr,
    right_scr,
    size_scr,
    x_left,
    x_right,
    x_size,
    k_scr,
    v_scr,
    ctx_scr,
    wkt_scr,
    query_ref,
    hidden_ref,
    load_sems,
    step_sems,
):
    (
        plan_smem,
        sizes_ref,
        valid_smem,
        count_smem,
        row_ref,
        wk_ref,
        wv_ref,
        wo_ref,
        m1_ref,
        m2_ref,
        b2_ref,
        sp_ref,
    ) = local_copies
    reqs = query_ref.shape[0]
    total_slots, width = arrived_ref.shape
    slots = ctx_scr.shape[0]
    cands = query_ref.shape[1]
    pairs = sizes_ref.shape[0]
    head_size = width // HEADS
    copies = ((left_scr, x_left), (right_scr, x_right), (size_scr, x_size))

    def group_rows(req):
        for s in range(pairs):
            at = plan_smem[req, s]
            to = plan_smem[req + reqs, s]
            for held, taken in copies:
                taken[pl.ds(to, CHUNK), :] = held[pl.ds(at, CHUNK), :]

    loads = [
        pltpu.make_async_copy(src, dst, load_sems.at[n])
        for n, (src, dst) in enumerate(zip(held_in_hbm, local_copies))
    ]
    for load in loads:
        load.start()
    quarter = total_slots // 4
    blocks = [
        pltpu.make_async_copy(
            arrived_hbm.at[pl.ds(n * quarter, quarter)],
            arrived_ref.at[pl.ds(n * quarter, quarter)],
            load_sems.at[len(loads) + n],
        )
        for n in range(4)
    ]
    for block in blocks:
        block.start()

    def step_loads(r):
        return (
            pltpu.make_async_copy(query_hbm.at[r], query_ref.at[r], step_sems.at[0, r]),
            pltpu.make_async_copy(hidden_hbm.at[r], hidden_ref.at[r], step_sems.at[1, r]),
        )

    for load in step_loads(0):
        load.start()
    k_scr[...] = jnp.zeros_like(k_scr)
    for held, taken in copies:
        held[total_slots:, :] = jnp.zeros((CHUNK, LANES), F32)
        taken[...] = jnp.zeros_like(taken)
    out_ref[...] = jnp.zeros_like(out_ref)
    for load in loads:
        load.wait()
    wkt_scr[...] = wk_ref[...].astype(F32).T.astype(BF)
    group = LANES // per_pair
    one = lax.broadcasted_iota(jnp.int32, (pairs // group, pairs), 1) // group
    one = one == lax.broadcasted_iota(jnp.int32, (pairs // group, pairs), 0)
    packed = jnp.dot(
        jnp.where(one, 1.0, 0.0).astype(BF),
        sizes_ref[...].astype(BF),
        preferred_element_type=F32,
    )
    for t in range(pairs // group):
        size_scr[t * LANES : (t + 1) * LANES, :] = column_of(packed[t : t + 1, :])
    for n, block in enumerate(blocks):
        block.wait()
        part = slice(n * quarter, (n + 1) * quarter)
        left_scr[part, :] = arrived_ref[part, :LANES].astype(F32)
        right_scr[part, :] = arrived_ref[part, LANES:].astype(F32)
    group_rows(0)

    def one_request(r, carry):
        for load in step_loads(r):
            load.wait()

        @pl.when(r + 1 < reqs)
        def _():
            for load in step_loads(r + 1):
                load.start()

        valid = valid_smem[r]
        count = count_smem[r]

        @pl.when(plan_smem[r + 3 * reqs, 0] > CHUNK)
        def _():
            def rest(s, carry):
                at = plan_smem[r, s]
                to = plan_smem[r + reqs, s]
                left = plan_smem[r + 2 * reqs, s]
                sub = lax.broadcasted_iota(jnp.int32, (CHUNK, LANES), 0)

                @pl.when(left > CHUNK)
                def _():
                    for held, taken in copies:
                        old = taken[pl.ds(to + CHUNK, CHUNK), :]
                        new = held[pl.ds(at + CHUNK, CHUNK), :]
                        taken[pl.ds(to + CHUNK, CHUNK), :] = jnp.where(sub < left - CHUNK, new, old)

                return carry

            lax.fori_loop(0, pairs, rest, 0)

        query = query_ref[r]
        clane = lax.broadcasted_iota(jnp.int32, (cands, LANES), 1)
        queries = []
        for p in range(2):
            own = query[:, p * LANES : (p + 1) * LANES]
            other = query[:, (1 - p) * LANES : (2 - p) * LANES].astype(F32)
            other = jnp.where(clane == 0, 1.0, other).astype(BF)
            queries.append(jnp.concatenate([own, other] if p == 0 else [other, own], axis=1))

        def attend(live):
            x = jnp.concatenate([x_left[:live, :], x_right[:live, :]], axis=1).astype(BF)
            keys = lax.dot_general(wkt_scr[...], x, NT, preferred_element_type=F32)
            keys = (keys.astype(BF).astype(F32) * 0.125).astype(BF)
            values = jnp.dot(x, wv_ref[...], preferred_element_type=F32)
            bias = jnp.concatenate(
                [x_size[t : t + LANES, :].T[0:16, :] for t in range(0, live, LANES)], axis=1
            )
            slot = lax.broadcasted_iota(jnp.int32, (16, live), 1)
            sub = lax.broadcasted_iota(jnp.int32, (16, live), 0)
            bias = jnp.where(slot < valid, bias, -1e30)
            bias = jnp.where(sub == 0, bias, 0.0).astype(BF)
            lane = lax.broadcasted_iota(jnp.int32, (live, LANES), 1)
            blank = jnp.zeros((head_size, live), BF)
            for h in range(HEADS):
                p, side = h // 2, h % 2
                half = slice(p * LANES, (p + 1) * LANES)
                own = keys[h * head_size : (h + 1) * head_size, :]
                other = (1 - p) * LANES
                span = slice(side * live, (side + 1) * live)
                mine = (lane // head_size) == side
                k_scr[p, half, span] = jnp.concatenate(
                    [own, blank] if side == 0 else [blank, own], axis=0
                )
                k_scr[p, other : other + 16, span] = bias
                v_scr[p, span, :LANES] = jnp.where(mine, values[:, half], 0.0).astype(BF)
                v_scr[p, span, LANES:] = jnp.where(mine, 1.0, 0.0).astype(BF)
            for p in range(2):
                logits = jnp.dot(queries[p], k_scr[p, :, : 2 * live], preferred_element_type=F32)
                probs = []
                for side in range(2):
                    part = logits[:, side * live : (side + 1) * live]
                    top = jnp.max(part, axis=1, keepdims=True)
                    probs.append(jnp.exp(part - top).astype(BF))
                probs = jnp.concatenate(probs, axis=1)
                total = jnp.dot(probs, v_scr[p, : 2 * live, :], preferred_element_type=F32)
                ctx_scr[:, p * LANES : (p + 1) * LANES] = (
                    total[:, :LANES] / total[:, LANES:]
                ).astype(BF)

        blocks = slots // LANES
        for n in range(1, blocks + 1):

            @pl.when(jnp.logical_and(count > 0, (valid + LANES - 1) // LANES == n))
            def _(n=n):
                attend(n * LANES)

        following = jnp.minimum(r + 1, reqs - 1)

        @pl.when(count <= 0)
        def _():
            group_rows(following)

        @pl.when(count > 0)
        def _():
            group_rows(following)
            attended = jnp.dot(ctx_scr[...], wo_ref[...], preferred_element_type=F32).astype(BF)
            hidden = hidden_ref[r] + jnp.dot(attended, m1_ref[width:, :], preferred_element_type=F32)
            hidden = jnp.maximum(hidden, 0.0).astype(BF)
            hidden = jnp.dot(hidden, m2_ref[...], preferred_element_type=F32)
            hidden = jnp.maximum(hidden + b2_ref[...], 0.0).astype(BF)
            weight = sp_ref[...].astype(F32)
            weight = jnp.concatenate([weight[n : n + 1, :] for n in range(width // LANES)], axis=1)
            weight = jnp.broadcast_to(weight, (16, width)).astype(BF)
            score = lax.dot_general(weight, hidden, NT, preferred_element_type=F32)[0:1, :]
            slot = lax.broadcasted_iota(jnp.int32, (1, cands), 1)
            score = jnp.where(slot < count, score, 0.0)
            first = score.astype(BF).astype(F32)
            second = score - first
            row = row_ref[pl.ds(r, 1), :]
            lines = out_ref.shape[0]
            at_line = lax.broadcasted_iota(jnp.int32, (lines, cands), 0) == lax.shift_right_logical(row, 7)
            at_lane = lax.broadcasted_iota(jnp.int32, (LANES, cands), 0) == (row & (LANES - 1))
            at_lane = jnp.where(at_lane, 1.0, 0.0).astype(BF)
            out_ref[...] += lax.dot_general(
                jnp.where(at_line, first, 0.0).astype(BF), at_lane, NT, preferred_element_type=F32
            ) + lax.dot_general(
                jnp.where(at_line, second, 0.0).astype(BF), at_lane, NT, preferred_element_type=F32
            )
        return carry

    lax.fori_loop(0, reqs, one_request, 0)


def score(plan, per_pair, valid, count, sizes, arrived, queries, hidden, rows, weights, lines):
    reqs, cands, width = queries.shape
    total_slots = arrived.shape[0]
    slots = total_slots // reqs
    hbm = pl.BlockSpec(memory_space=pltpu.HBM)
    loose = (plan, sizes, valid, count, rows) + tuple(weights)
    held = pltpu.VMEM((total_slots + CHUNK, LANES), F32)
    taken = pltpu.VMEM((slots + 2 * CHUNK, LANES), F32)
    return pl.pallas_call(
        functools.partial(score_kernel, per_pair),
        out_shape=jax.ShapeDtypeStruct((lines, LANES), F32),
        in_specs=[hbm] * (3 + len(loose)),
        out_specs=pl.BlockSpec(memory_space=pltpu.VMEM),
        scratch_shapes=[
            pltpu.SMEM(plan.shape, jnp.int32),
            pltpu.VMEM(sizes.shape, F32),
            pltpu.SMEM(valid.shape, jnp.int32),
            pltpu.SMEM(count.shape, jnp.int32),
        ]
        + [pltpu.VMEM(a.shape, a.dtype) for a in loose[4:]]
        + [
            pltpu.VMEM(arrived.shape, BF),
            held,
            held,
            held,
            taken,
            taken,
            taken,
            pltpu.VMEM((2, width, 2 * slots), BF),
            pltpu.VMEM((2, 2 * slots, width), BF),
            pltpu.VMEM((cands, width), BF),
            pltpu.VMEM((width, width), BF),
            pltpu.VMEM(queries.shape, BF),
            pltpu.VMEM(hidden.shape, F32),
            pltpu.SemaphoreType.DMA((len(loose) + 4,)),
            pltpu.SemaphoreType.DMA((2, reqs)),
        ],
        compiler_params=pltpu.CompilerParams(vmem_limit_bytes=VMEM_LIMIT),
        cost_estimate=pl.CostEstimate(
            flops=SCORE_FLOPS, bytes_accessed=8 * 1024 * 1024, transcendentals=8 * 1024 * 1024
        ),
        name="score",
    )(queries, hidden, arrived, *loose)


def on_device(
    store_rows,
    cluster_logsize,
    cluster_home,
    cluster_ids,
    valid_count,
    candidates,
    cand_count,
    candidate_row,
    query_proj,
    key_proj,
    value_proj,
    out_proj,
    mlp_first,
    bias_first,
    mlp_second,
    bias_second,
    score_proj,
):
    device_count = lax.axis_size(AXES)
    scorer_count = lax.axis_size("scorer")
    rows_dev, width = store_rows.shape
    slot_total = cluster_ids.size
    per_pair = slot_total // device_count
    reqs, cands = candidate_row.shape
    arrived, sizes, plan, queries, hidden = fetch(
        cluster_ids,
        valid_count,
        cluster_home.reshape(-1, LANES),
        store_rows,
        cluster_logsize.reshape(-1, LANES),
        candidates,
        query_proj,
        mlp_first,
        bias_first.reshape(1, -1),
        device_count // scorer_count,
        scorer_count,
        per_pair,
    )
    arrived = arrived.reshape(slot_total, width)
    sizes = sizes.reshape(device_count, LANES)
    weights = (
        key_proj,
        value_proj,
        out_proj,
        mlp_first,
        mlp_second,
        bias_second.reshape(1, -1),
        score_proj.reshape(-1, LANES),
    )
    lines = scorer_count * (reqs * cands // 2) // LANES
    table = score(
        plan, per_pair, valid_count, cand_count, sizes, arrived, queries, hidden, candidate_row, weights, lines
    )
    return jnp.sum(gather_spans(table, scorer_count), axis=0).reshape(-1)


def solution(mesh):
    split = P(AXES)
    in_specs = (
        P(AXES, None),
        split,
        P(),
        P(AXES, None),
        split,
        P(AXES, None, None),
        split,
        P(AXES, None),
    ) + (P(),) * 9
    return jax.shard_map(
        on_device, mesh=mesh, in_specs=in_specs, out_specs=split, check_vma=False
    )
```
